256 devices in a mesh: member: 8 (over y, core), space: 32 (over z, x).
Axes of the slice: x: 4, y: 4, z: 8, core: 2. Of those that a mesh axis runs over, the one named last changes fastest.
Arguments:
- state: float32 [256, 512, 1024], P('member', 'space'), may hold values from -8 to 8
- obs_index: int32 [32768], P('space'), may hold values from 0 to 16383
- obs_value: float32 [32768], P('space'), may hold values from -6 to 6
- obs_scale: float32 [32768], P('space'), may hold values from 0.3 to 3
- ksat: float32 [512, 1024], P('space'), may hold values from 0.05 to 0.2
- storage: float32 [512, 1024], P('space'), may hold values from 0.5 to 4
- recharge: float32 [512, 1024], P('space'), may hold values from -1.8 to 1.8
- newton_counts: int32 [256], replicated, may hold values from 1 to 8, as said below
Outputs:
- forecast: float32 [256, 512, 1024], P('member', 'space')
The draws below stay inside these ranges and needn't reach their ends.
Inputs may be any that keep to these rules, and one draw needn't show every extreme that they name: `newton_counts`: A count of 8 occurs in every draw.
All inputs are finite; a program needn't handle non-finite values.
Results may differ from the reference program's by a relative error of at most 0.0003.
Values sent between devices are 32-bit elements; how exact they have to be, the bound alone decides.
No kernel may reach another device: no remote copies, remote signals or barrier semaphores. Data moves between devices by JAX's collectives and lax.ppermute only.
A program may use at most 64 MiB of HBM per device.

```python
import math
import jax
import jax.numpy as jnp
from jax import lax

M = 256
CX = 16
NY = 1024
NOBS_DEV = 1024
KMAX = 8
NS_ITERS = 12
NX = 512
NOBS = 32768


def draw_state(key, part):
    key_one, key_two, key_three = jax.random.split(jax.random.fold_in(key, 11), 3)
    member_scale = jnp.exp(jax.random.uniform(key_one, (M, 1, 1), jnp.float32, math.log(0.1), 0.0))
    noise = jnp.clip(jax.random.normal(key_two, (M, NX, NY), jnp.float32), -4.0, 4.0)
    centre = jnp.clip(jax.random.normal(key_three, (1, NX, NY), jnp.float32), -4.0, 4.0)
    return (centre + member_scale * noise).astype(jnp.float32)


def draw_recharge(key, part):
    key_one, key_two = jax.random.split(jax.random.fold_in(key, 37))
    phases = jax.random.uniform(key_one, (4,), jnp.float32, 0.0, 2.0 * math.pi)
    row_place = (jnp.arange(NX, dtype=jnp.float32) / NX)[:, None]
    col_place = (jnp.arange(NY, dtype=jnp.float32) / NY)[None, :]
    waves = jnp.sin(2.0 * math.pi * 3.0 * row_place + phases[0]) * jnp.cos(2.0 * math.pi * 2.0 * col_place + phases[1])
    bent = waves + 0.3 * jnp.sin(2.0 * math.pi * 5.0 * col_place + phases[2]) * jnp.cos(2.0 * math.pi * 4.0 * row_place + phases[3])
    smooth = jnp.tanh(3.0 * bent)
    rough = 0.5 * jnp.clip(jax.random.normal(key_two, (NX, NY), jnp.float32), -2.0, 2.0)
    value = 0.7 * smooth + 0.3 * rough
    return (1.8 * jnp.clip(value, -1.0, 1.0)).astype(jnp.float32)


def draw_newton_counts(key, part):
    key_one, key_two = jax.random.split(jax.random.fold_in(key, 23))
    low_counts = jax.random.randint(key_one, (M,), 1, 4, dtype=jnp.int32)
    run_start = jax.random.randint(key_two, (), 0, M, dtype=jnp.int32)
    distance = (jnp.arange(M, dtype=jnp.int32) - run_start) % M
    return jnp.where(distance < M // 8, KMAX, low_counts).astype(jnp.int32)


def place_ends(drawn, key, low, top_value):
    dims = drawn.shape
    index_at = [jax.random.randint(jax.random.fold_in(key, axis), (), 0, dims[axis]) for axis in range(len(dims))]
    drawn = drawn.at[tuple(index_at)].set(low)
    longest = dims.index(max(dims))
    index_at[longest] = (index_at[longest] + 1) % dims[longest]
    return drawn.at[tuple(index_at)].set(top_value)


def block_scale(key, dims, shards, least, high):
    loudness, own = 1.0, jax.random.fold_in(key, 6)
    for position, parts in shards:
        heights = jnp.exp(jax.random.uniform(jax.random.fold_in(own, position), (parts,), jnp.float32, least / len(shards), high / len(shards)))
        loudness = loudness * jnp.repeat(heights, dims[position] // parts).reshape([-1 if axis == position else 1 for axis in range(len(dims))])
    return loudness


def centred(stream_key, dims, scale, bound, cuts=(), kind=jnp.bfloat16):
    values = jax.random.normal(stream_key, dims, jnp.float32) * scale
    if len(cuts) > 0:
        values = block_scale(stream_key, dims, cuts, -0.22, 0.18) * values
    return jnp.clip(values, min=-bound, max=bound).astype(kind)


def setup_inputs(seed: int = 0) -> dict:
    keys = jax.random.split(jax.random.key(seed), 9)
    state = draw_state(jax.random.fold_in(keys[8], 71), 0)
    obs_index = place_ends(jax.random.randint(keys[1], (NOBS,), 0, CX * NY), jax.random.fold_in(keys[1], 1), 0, (CX * NY) - 1).astype(jnp.int32)
    obs_value = centred(keys[2], (NOBS,), 1.0, 6.0, ((0, 32),), jnp.float32)
    obs_scale = jnp.clip(jnp.exp(math.log(3.0) - 2.3025851 * jax.random.uniform(keys[3], (NOBS,), jnp.float32) ** block_scale(keys[3], (NOBS,), ((0, 32),), -0.2, 0.2)), 0.3, 3.0)
    ksat = jnp.clip(jnp.exp(math.log(0.2) - 1.3862944 * jax.random.uniform(keys[4], (NX, NY), jnp.float32) ** block_scale(keys[4], (NX, NY), ((0, 32),), -0.2, 0.2)), 0.05, 0.2)
    storage = jnp.clip(jnp.exp(math.log(4.0) - 2.0794415 * jax.random.uniform(keys[5], (NX, NY), jnp.float32) ** block_scale(keys[5], (NX, NY), ((0, 32),), -0.2, 0.2)), 0.5, 4.0)
    recharge = draw_recharge(jax.random.fold_in(keys[8], 71), 0)
    newton_counts = draw_newton_counts(jax.random.fold_in(keys[8], 71), 0)
    return dict(state=state, obs_index=obs_index, obs_value=obs_value, obs_scale=obs_scale, ksat=ksat, storage=storage, recharge=recharge, newton_counts=newton_counts)


HIGHEST_PRECISION = lax.Precision.HIGHEST
DAMPING = 0.3

def inverse_root(gram_matrix):
    order_size = gram_matrix.shape[0]
    identity = jnp.eye(order_size, dtype=jnp.float32)
    whole = identity + gram_matrix
    norm_value = jnp.sqrt(jnp.sum(whole * whole))
    upper_iter = whole / norm_value
    lower_iter = identity
    for sweep_index in range(NS_ITERS):
        middle = 1.5 * identity - 0.5 * jnp.dot(lower_iter, upper_iter, precision=HIGHEST_PRECISION)
        upper_iter = jnp.dot(upper_iter, middle, precision=HIGHEST_PRECISION)
        lower_iter = jnp.dot(middle, lower_iter, precision=HIGHEST_PRECISION)
    return lower_iter / jnp.sqrt(norm_value)

def face_flux(padded, conduct):
    wide_level = jnp.pad(padded, ((0, 0), (0, 0), (1, 1)))
    wide_cond = jnp.pad(conduct, ((0, 0), (0, 0), (1, 1)))
    centre_level = wide_level[:, 1:-1, 1:-1]
    centre_cond = wide_cond[:, 1:-1, 1:-1]
    height = centre_level.shape[1]
    breadth = centre_level.shape[2]
    divergence = jnp.zeros_like(centre_level)
    for offset_row, offset_col in ((0, 1), (2, 1), (1, 0), (1, 2)):
        other_level = wide_level[:, offset_row:offset_row + height, offset_col:offset_col + breadth]
        other_cond = wide_cond[:, offset_row:offset_row + height, offset_col:offset_col + breadth]
        divergence = divergence + 0.5 * (centre_cond + other_cond) * (other_level - centre_level)
    return divergence

def relax(pressure, drive_term, storage, counts):
    target = pressure + storage * jnp.tanh(pressure) + drive_term
    iterate = pressure
    for sweep_index in range(KMAX):
        bend_value = jnp.tanh(iterate)
        derivative = 1.0 + storage * (1.0 - bend_value * bend_value)
        stepped = iterate - DAMPING * (iterate + storage * bend_value - target) / derivative
        iterate = jnp.where((counts > sweep_index)[:, None, None], stepped, iterate)
    return iterate

def advance(pressure, ksat, storage, recharge, counts):
    padded = jnp.pad(pressure, ((0, 0), (1, 1), (0, 0)))
    padded_ksat = jnp.pad(ksat, ((1, 1), (0, 0)))
    conduct = padded_ksat * jax.nn.sigmoid(padded)
    drive_term = face_flux(padded, conduct) + recharge
    return relax(pressure, drive_term, storage, counts)

def reference(state, obs_index, obs_value, obs_scale, ksat, storage, recharge, newton_counts):
    members = state.shape[0]
    flattened = state.reshape(members, NX * NY)
    mean_state = lax.optimization_barrier(jnp.mean(flattened, axis=0))
    anomaly = flattened - mean_state
    tile_of = jnp.arange(obs_index.shape[0], dtype=jnp.int32) // NOBS_DEV
    observed = (tile_of * (CX * NY) + obs_index).astype(jnp.int32)
    root_count = jnp.sqrt(jnp.float32(members - 1))
    spread = jnp.take(anomaly, observed, axis=1) * obs_scale / root_count
    innovation = obs_scale * (obs_value - jnp.take(mean_state, observed))
    gram_matrix = jnp.dot(spread, spread.T, precision=HIGHEST_PRECISION)
    drive_vector = jnp.dot(spread, innovation, precision=HIGHEST_PRECISION)
    root_inverse = inverse_root(gram_matrix)
    mean_weights = jnp.dot(root_inverse, jnp.dot(root_inverse, drive_vector, precision=HIGHEST_PRECISION), precision=HIGHEST_PRECISION)
    transform = mean_weights[:, None] / root_count + root_inverse

    def one_group(inputs):
        columns, counts = inputs
        analysis = mean_state + jnp.dot(columns.T, anomaly, precision=HIGHEST_PRECISION)
        pressure = analysis.reshape(columns.shape[1], NX, NY)
        for step_index in range(2):
            pressure = advance(pressure, ksat, storage, recharge, counts)
        return pressure
    grouped = transform.reshape(members, members // 8, 8).transpose(1, 0, 2)
    counts_grouped = newton_counts.reshape(members // 8, 8)
    result = lax.map(one_group, (grouped, counts_grouped))
    return result.reshape(members, NX, NY)
```

```python
import functools

import jax
import jax.numpy as jnp
from jax import lax
from jax.experimental import pallas as pl
from jax.experimental.pallas import tpu as pltpu
from jax.sharding import Mesh
from jax.sharding import PartitionSpec as P

NS_ITERS = 12
DAMPING = 0.3
MEMBER = ("member_0", "member_1")
SPACE = ("space_0", "space_1")
HIGHEST = lax.Precision.HIGHEST
F32 = jnp.float32

OWNERS = 8
HELD = 32
ROWS = 16
LANES = 128
MEMBERS = OWNERS * HELD
EDGE = ROWS
SENT_ROWS = ROWS + 1
OUTER = 36
OWN = 72


def shape(*dims, dtype=F32):
    return jax.ShapeDtypeStruct(dims, dtype)


def whole(count):
    return [pl.BlockSpec(memory_space=pltpu.VMEM)] * count


def params(mib):
    return pltpu.CompilerParams(vmem_limit_bytes=mib * 2**20)


SCALARS = pl.BlockSpec(memory_space=pltpu.SMEM)


def lane_ids(rows=8):
    return lax.broadcasted_iota(jnp.int32, (rows, LANES), 1)


def turned(array, amount):
    return pltpu.roll(array, amount % LANES, 1)


def dot(a, b, dims=((1,), (0,))):
    return lax.dot_general(a, b, (dims, ((), ())), precision=HIGHEST, preferred_element_type=F32)


def observe_kernel(index_ref, state_ref, seen_ref):
    values = state_ref[...]
    high = values.astype(jnp.bfloat16)
    rest = values - high.astype(F32)
    middle = rest.astype(jnp.bfloat16)
    low = (rest - middle.astype(F32)).astype(jnp.bfloat16)
    width = values.shape[1]
    step = 256
    for first in range(0, index_ref.shape[1], step):
        cell = index_ref[:, first : first + step]
        row = cell // width
        column = cell - row * width
        places = lax.broadcasted_iota(jnp.int32, (width, step), 0)
        chosen = (places == column).astype(F32).astype(jnp.bfloat16)
        picked = jnp.dot(low, chosen, preferred_element_type=F32)
        picked += jnp.dot(middle, chosen, preferred_element_type=F32)
        picked += jnp.dot(high, chosen, preferred_element_type=F32)
        picked = picked.reshape(HELD, ROWS, step)
        rows = lax.broadcasted_iota(jnp.int32, (ROWS, step), 0)
        seen_ref[:, first : first + step] = jnp.sum(
            jnp.where((rows == row)[None], picked, 0.0), axis=1
        )


def observed(state, obs_index):
    return pl.pallas_call(
        observe_kernel,
        out_shape=shape(HELD, obs_index.shape[1]),
        in_specs=whole(2),
        out_specs=whole(1)[0],
        compiler_params=params(32),
        name="observe",
    )(obs_index, state)


def pack_kernel(place_ref, state_ref, sent_ref, column_ref):
    own = place_ref[0]
    lane = lane_ids()
    even = lane % 2 == 0
    near_left = (lane < OUTER) & even
    near_right = (lane < OUTER) & ~even
    far_left = (lane >= OUTER) & (lane < OUTER + 2 * ROWS) & even
    far_right = (lane >= OUTER + 3) & (lane < OUTER + 3 + 2 * ROWS) & ~even

    def one_group(group, carry):
        near, far = [], []
        for block in range(OWNERS):
            slot = lax.rem(own - block + OWNERS, OWNERS)
            packed_near = jnp.zeros((8, LANES), F32)
            packed_far = jnp.zeros((8, LANES), F32)
            start = pl.multiple_of(group * 8 * ROWS, 8 * ROWS)
            column_ref[block] = state_ref[
                pl.ds(start, 8 * ROWS), block * LANES : (block + 1) * LANES
            ]
            for r in range(ROWS):
                value = column_ref[block, pl.ds(r, 8, stride=ROWS), :]
                sent_ref[slot, r, pl.ds(group * 8, 8)] = value
                at = 2 * (r + 1)
                packed_near = jnp.where(
                    (lane == at) | (lane == at + 1), turned(value, at + 1), packed_near
                )
                at = OUTER + 2 * r
                packed_far = jnp.where(
                    (lane == at) | (lane == at + 3), turned(value, at + 2), packed_far
                )
            near.append(packed_near)
            far.append(packed_far)
        nothing = jnp.zeros((8, LANES), F32)
        for block in range(OWNERS):
            slot = lax.rem(own - block + OWNERS, OWNERS)
            edge = turned(near[block], OWN)
            edge = jnp.where((lane >= OWN) & (lane < OWN + 2 * ROWS + 4), edge, nothing)
            if block > 0:
                edge = jnp.where(near_left, near[block - 1], edge)
                edge = jnp.where(far_left, far[block - 1], edge)
            if block < OWNERS - 1:
                edge = jnp.where(near_right, near[block + 1], edge)
                edge = jnp.where(far_right, far[block + 1], edge)
            sent_ref[slot, EDGE, pl.ds(group * 8, 8)] = edge
        return carry

    lax.fori_loop(0, HELD // 8, one_group, 0)


def packed_blocks(place, state):
    return pl.pallas_call(
        pack_kernel,
        out_shape=shape(OWNERS, SENT_ROWS, HELD, LANES),
        in_specs=[SCALARS] + whole(1),
        out_specs=whole(1)[0],
        scratch_shapes=[pltpu.VMEM((OWNERS, 8 * ROWS, LANES), F32)],
        compiler_params=params(16),
        name="pack",
    )(place, state)


def gram_kernel(place_ref, same_ref, other_ref, value_ref, scale_ref, out_ref):
    own = place_ref[0]
    total = jnp.sum(same_ref[...], axis=(0, 1)) + jnp.sum(other_ref[...], axis=(0, 1))
    mean = (total / MEMBERS)[None]
    scale = scale_ref[...]
    weight = scale / jnp.sqrt(F32(MEMBERS - 1))
    blocks = []
    for k in range(5):
        at = lax.rem(own + k, OWNERS) // 2
        block = same_ref[at] if k % 2 == 0 else other_ref[at]
        blocks.append((block - mean) * weight)
    innovation = scale * (value_ref[...] - mean)
    left = jnp.concatenate([blocks[0], jnp.broadcast_to(innovation, (8, mean.shape[1]))], axis=0)
    out_ref[0:40] = dot(left, jnp.concatenate(blocks[:4], axis=0), ((1,), (1,)))
    last = jnp.concatenate([blocks[4], jnp.zeros((96, mean.shape[1]), F32)], axis=0)
    opposite = dot(blocks[0], last, ((1,), (1,)))
    packed = opposite[0:8]
    for g in range(1, 4):
        packed += turned(opposite[8 * g : 8 * g + 8], HELD * g)
    out_ref[40:48] = packed


def gram_blocks(place, same, other, value, scale):
    return pl.pallas_call(
        gram_kernel,
        out_shape=shape(48, LANES),
        in_specs=[SCALARS] + whole(4),
        out_specs=whole(1)[0],
        compiler_params=params(16),
        name="gram",
    )(place, same, other, value, scale)


def root_kernel(place_ref, parts_ref, out_ref, half_ref):
    own = place_ref[0]
    lane = lane_ids()
    drive_row = jnp.zeros((8, MEMBERS), F32)
    nothing = jnp.zeros((8, LANES), F32)
    for i in range(OWNERS):
        at = lax.rem(own + i, OWNERS)
        for g in range(4):
            rows = parts_ref[at, 8 * g : 8 * g + 8]
            rows = jnp.where(lane < HELD, 0.5 * rows, rows)
            fifth = turned(parts_ref[at, 40:48], -HELD * g)
            fifth = jnp.where(lane < HELD, 0.5 * fifth, 0.0)
            line = jnp.concatenate([rows, fifth], axis=1)
            half_ref[i * HELD + 8 * g : i * HELD + 8 * g + 8] = pltpu.roll(line, HELD * i, 1)
        drive = jnp.where(lane < HELD, parts_ref[at, 32:40], 0.0)
        line = jnp.concatenate([drive, nothing], axis=1)
        drive_row += pltpu.roll(line, HELD * i, 1)
    half = half_ref[...]
    rows = lax.broadcasted_iota(jnp.int32, (MEMBERS, MEMBERS), 0)
    columns = lax.broadcasted_iota(jnp.int32, (MEMBERS, MEMBERS), 1)
    identity = (rows == columns).astype(F32)
    big = identity + (half + half.T)
    norm = jnp.sqrt(jnp.sum(big * big))
    upper = big / norm
    middle = 1.5 * identity - 0.5 * upper
    upper = dot(upper, middle)
    lower = middle
    for _ in range(NS_ITERS - 2):
        middle = 1.5 * identity - 0.5 * dot(lower, upper)
        upper = dot(upper, middle)
        lower = dot(middle, lower)
    middle = 1.5 * identity - 0.5 * dot(lower, upper)
    root = dot(middle, lower) / jnp.sqrt(norm)
    weights = dot(dot(drive_row, root, ((1,), (1,))), root, ((1,), (1,)))
    out_ref[...] = root + weights[0:1] / jnp.sqrt(F32(MEMBERS - 1))


def transform_of(place, parts):
    return pl.pallas_call(
        root_kernel,
        out_shape=shape(MEMBERS, MEMBERS),
        in_specs=[SCALARS] + whole(1),
        out_specs=whole(1)[0],
        scratch_shapes=[pltpu.VMEM((MEMBERS, MEMBERS), F32)],
        compiler_params=params(16),
        name="root",
    )(place, parts)


UNITS = ROWS + 5


def analyse_kernel(*refs):
    transform_ref = refs[0]
    piece_refs = refs[1 : 1 + OWNERS]
    above_ref, below_ref = refs[1 + OWNERS : 3 + OWNERS]
    out_refs = refs[3 + OWNERS :]
    transform = transform_ref[...]
    lane = lax.broadcasted_iota(jnp.int32, (MEMBERS, LANES), 1)

    def stacked(unit):
        if unit < SENT_ROWS:
            return jnp.concatenate([ref[unit] for ref in piece_refs], axis=0)
        if unit < SENT_ROWS + 2:
            return jnp.concatenate([above_ref[i, unit - SENT_ROWS] for i in range(OWNERS)], axis=0)
        return jnp.concatenate([below_ref[i, unit - SENT_ROWS - 2] for i in range(OWNERS)], axis=0)

    def cells(unit):
        found = stacked(unit)
        if unit == EDGE:
            top = jnp.concatenate([above_ref[i, 2] for i in range(OWNERS)], axis=0)
            low = jnp.concatenate([below_ref[i, 2] for i in range(OWNERS)], axis=0)
            first = (lane < 2) | ((lane >= OWN) & (lane < OWN + 2))
            last = 2 * ROWS + 2
            final = ((lane >= last) & (lane < last + 2)) | (
                (lane >= OWN + last) & (lane < OWN + last + 2)
            )
            found = jnp.where(first, turned(top, -2 * ROWS), found)
            found = jnp.where(final, turned(low, 2 * ROWS), found)
        return found

    for first in range(0, UNITS, 2):
        units = range(first, min(first + 2, UNITS))
        found = [cells(u) for u in units]
        joined = found[0] if len(found) == 1 else jnp.concatenate(found, axis=1)
        mean = jnp.sum(joined, axis=0, keepdims=True) / MEMBERS
        result = dot(transform, joined - mean) + mean
        for at, unit in enumerate(units):
            for i in range(OWNERS):
                out_refs[i][unit] = result[
                    i * HELD : (i + 1) * HELD, at * LANES : (at + 1) * LANES
                ]


def analysed(transform, pieces, above, below):
    return pl.pallas_call(
        analyse_kernel,
        out_shape=[shape(UNITS, HELD, LANES)] * OWNERS,
        in_specs=whole(3 + OWNERS),
        out_specs=whole(OWNERS),
        compiler_params=params(24),
        name="analyse",
    )(transform, *pieces, above, below)


FIELD_ROWS = 20
NEAR_K, INNER_K, OUTER_K, NEAR_S, NEAR_R, NEAR_MASK = range(6)


def field_kernel(place_ref, ksat_ref, storage_ref, recharge_ref, above_ref, below_ref, out_ref, edge_ref):
    own = place_ref[0]
    lane = lane_ids(1)
    even = lane % 2 == 0
    start = pl.multiple_of(own * LANES, LANES)
    left_start = pl.multiple_of(jnp.maximum(own - 1, 0) * LANES, LANES)
    right_start = pl.multiple_of(jnp.minimum(own + 1, OWNERS - 1) * LANES, LANES)
    has_left = own > 0
    has_right = own < OWNERS - 1
    packed = [jnp.zeros((1, LANES), F32) for _ in range(5)]
    for which, ref in enumerate((ksat_ref, storage_ref, recharge_ref)):
        for place in range(FIELD_ROWS):
            r = place - 2

            def row_of(first):
                if r < 0:
                    return above_ref[which, r + 2 : r + 3, pl.ds(first, LANES)]
                if r >= ROWS:
                    return below_ref[which, r - ROWS : r - ROWS + 1, pl.ds(first, LANES)]
                return ref[r : r + 1, pl.ds(first, LANES)]

            mine = row_of(start)
            out_ref[which, place] = jnp.broadcast_to(mine, (8, LANES))
            if r < -1 or r > ROWS:
                continue
            at = 2 * (r + 1)
            here = (lane == at) | (lane == at + 1)
            left = jnp.where(has_left, row_of(left_start), 0.0)
            right = jnp.where(has_right, row_of(right_start), 0.0)
            near = jnp.where(lane < LANES // 2, right, left)
            near = turned(near, at + 1)
            if which == 0:
                inner = jnp.where(even, turned(mine, at), turned(mine, at + 2))
                outer = jnp.where(even, turned(left, at + 2), turned(right, at))
                packed[NEAR_K] = jnp.where(here, near, packed[NEAR_K])
                packed[INNER_K] = jnp.where(here, inner, packed[INNER_K])
                packed[OUTER_K] = jnp.where(here, outer, packed[OUTER_K])
            elif which == 1:
                packed[NEAR_S] = jnp.where(here, near, packed[NEAR_S])
            else:
                packed[NEAR_R] = jnp.where(here, near, packed[NEAR_R])
    for n in range(5):
        edge_ref[n] = jnp.broadcast_to(packed[n], (8, LANES))
    lane = lane_ids()
    keep = jnp.where(lane % 2 == 0, has_left.astype(F32), has_right.astype(F32))
    edge_ref[NEAR_MASK] = jnp.where((lane >= 2) & (lane < 2 * ROWS + 2), keep, 0.0)


def block_fields(place, ksat, storage, recharge, above, below):
    return pl.pallas_call(
        field_kernel,
        out_shape=[shape(3, FIELD_ROWS, 8, LANES), shape(6, 8, LANES)],
        in_specs=[SCALARS] + whole(5),
        out_specs=whole(2),
        compiler_params=params(8),
        name="fields",
    )(place, ksat, storage, recharge, above, below)


def logistic(x):
    return 0.5 * jnp.tanh(0.5 * x) + 0.5


def forecast_kernel(shift, place_ref, counts_ref, wide_ref, field_ref, edge_field_ref, cells_ref, out_ref, iterate, goal, edge_row):
    own = place_ref[0]
    has_above = place_ref[1].astype(F32)
    has_below = place_ref[2].astype(F32)
    owner = lax.rem(own + shift, OWNERS)
    lane = lane_ids()
    even = lane % 2 == 0
    first_lane = lane == 0
    ends = first_lane | (lane == LANES - 1)
    sat, store, rain = 0, 1, 2

    def face(level, other, cond, other_cond):
        return 0.5 * (cond + other_cond) * (other - level)

    def swapped(packed):
        return jnp.where(even, turned(packed, -1), turned(packed, 1))

    def one_group(group, carry):
        first_member = owner * HELD + group * 8
        most = counts_ref[first_member]
        for n in range(1, 8):
            most = jnp.maximum(most, counts_ref[first_member + n])
        counts = wide_ref[pl.ds(pl.multiple_of(first_member, 8), 8)]

        def begun(level, flux, storage):
            bend = jnp.tanh(level)
            held = storage * bend
            return level + DAMPING * flux / (1.0 + storage * (1.0 - bend * bend)), level + held + flux

        def swept(value, target, storage, sweep):
            bend = jnp.tanh(value)
            derivative = 1.0 + storage * (1.0 - bend * bend)
            moved = value - DAMPING * (value + storage * bend - target) / derivative
            return jnp.where(counts > sweep, moved, value)

        def cell_at(r):
            if r < 0:
                at = SENT_ROWS + r + 2
            elif r >= ROWS:
                at = SENT_ROWS + 2 + r - ROWS
            else:
                at = r
            return cells_ref[at, pl.ds(pl.multiple_of(group * 8, 8), 8)]

        packed = cells_ref[EDGE, pl.ds(pl.multiple_of(group * 8, 8), 8)]
        near = jnp.where(lane < OUTER, packed, 0.0)
        inner = jnp.where(even, turned(packed, -OWN - 1), turned(packed, -OWN + 1))
        outer = jnp.where(even, turned(packed, 2 - OUTER), turned(packed, -OUTER))
        near_k = edge_field_ref[NEAR_K] * logistic(near)
        inner_k = edge_field_ref[INNER_K] * logistic(inner)
        outer_k = edge_field_ref[OUTER_K] * logistic(outer)
        inward = face(near, inner, near_k, inner_k)
        side = swapped(inward)
        flux = inward + face(near, outer, near_k, outer_k)
        flux += face(near, turned(near, 2), near_k, turned(near_k, 2))
        flux += face(near, turned(near, -2), near_k, turned(near_k, -2))
        flux += edge_field_ref[NEAR_R]
        value, target = begun(near, flux, edge_field_ref[NEAR_S])
        edge_row[0] = value
        edge_row[1] = target

        def conduct(level, r):
            return field_ref[sat, r + 2] * logistic(level)

        level, cond = cell_at(-1), conduct(cell_at(-1), -1)
        above = face(cell_at(-2), level, conduct(cell_at(-2), -2), cond)
        for r in range(-1, ROWS + 1):
            lower_level = cell_at(r + 1)
            lower_cond = conduct(lower_level, r + 1)
            under = face(level, lower_level, cond, lower_cond)
            across = face(turned(level, 1), level, turned(cond, 1), cond)
            across = jnp.where(first_lane, 0.0, across)
            flux = under - above + (turned(across, -1) - across)
            flux -= jnp.where(ends, turned(side, -2 * (r + 1) - 1), 0.0)
            flux += field_ref[rain, r + 2]
            iterate[r + 1], goal[r + 1] = begun(level, flux, field_ref[store, r + 2])
            level, cond, above = lower_level, lower_cond, under

        def first_sweep(sweep, carry):
            for n in range(ROWS + 2):
                iterate[n] = swept(iterate[n], goal[n], field_ref[store, n + 1], sweep)
            edge_row[0] = swept(edge_row[0], edge_row[1], edge_field_ref[NEAR_S], sweep)
            return carry

        lax.fori_loop(1, most, first_sweep, 0)

        near = edge_row[0] * edge_field_ref[NEAR_MASK]
        near_k = edge_field_ref[NEAR_K] * logistic(near)
        side = swapped(near)
        side_k = swapped(near_k)
        level = iterate[1]
        cond = conduct(level, 0)
        before = iterate[0] * has_above
        above = face(before, level, conduct(before, -1), cond)
        for r in range(ROWS):
            lower_level = iterate[r + 2]
            if r == ROWS - 1:
                lower_level = lower_level * has_below
            lower_cond = conduct(lower_level, r + 1)
            under = face(level, lower_level, cond, lower_cond)
            across = face(turned(level, 1), level, turned(cond, 1), cond)
            across = jnp.where(first_lane, 0.0, across)
            flux = under - above + (turned(across, -1) - across)
            turn = -2 * (r + 1) - 1
            entering = face(level, turned(side, turn), cond, turned(side_k, turn))
            flux += jnp.where(ends, entering, 0.0)
            flux += field_ref[rain, r + 2]
            iterate[r + 1], goal[r + 1] = begun(level, flux, field_ref[store, r + 2])
            level, cond, above = lower_level, lower_cond, under

        def second_sweep(sweep, carry):
            for n in range(1, ROWS + 1):
                iterate[n] = swept(iterate[n], goal[n], field_ref[store, n + 1], sweep)
            return carry

        lax.fori_loop(1, most, second_sweep, 0)
        for r in range(ROWS):
            out_ref[pl.ds(group * 8 * ROWS + r, 8, stride=ROWS), :] = iterate[r + 1]
        return carry

    lax.fori_loop(0, HELD // 8, one_group, 0)


def forecast_of(shift, place, counts, wide_counts, fields, edge_fields, cells):
    return pl.pallas_call(
        functools.partial(forecast_kernel, shift),
        out_shape=shape(HELD * ROWS, LANES),
        in_specs=[SCALARS, SCALARS] + whole(4),
        out_specs=whole(1)[0],
        scratch_shapes=[
            pltpu.VMEM((ROWS + 2, 8, LANES), F32),
            pltpu.VMEM((ROWS + 2, 8, LANES), F32),
            pltpu.VMEM((2, 8, LANES), F32),
        ],
        compiler_params=params(8),
        name="forecast",
    )(place, counts, wide_counts, fields, edge_fields, cells)


def unpack_kernel(place_ref, *refs):
    own = place_ref[0]
    pieces, out_ref, sems = refs[:OWNERS], refs[OWNERS], refs[OWNERS + 1]
    copies = []
    for i, piece in enumerate(pieces):
        block = lax.rem(own - i + OWNERS, OWNERS)
        start = pl.multiple_of(block * LANES, LANES)
        copies.append(
            pltpu.make_async_copy(piece, out_ref.at[:, pl.ds(start, LANES)], sems.at[i])
        )
    for copy in copies:
        copy.start()
    for copy in copies:
        copy.wait()


def unpacked(place, pieces):
    anywhere = pl.BlockSpec(memory_space=pl.ANY)
    return pl.pallas_call(
        unpack_kernel,
        out_shape=shape(HELD * ROWS, OWNERS * LANES),
        in_specs=[SCALARS] + [anywhere] * OWNERS,
        out_specs=anywhere,
        scratch_shapes=[pltpu.SemaphoreType.DMA((OWNERS,))],
        name="unpack",
    )(place, *pieces)


def shared(array, axis):
    peers = lax.axis_size(axis)
    copies = jnp.broadcast_to(array, (peers, *array.shape))
    return lax.all_to_all(copies, axis, split_axis=0, concat_axis=0, tiled=True)


def along(array, axis, step):
    peers = lax.axis_size(axis)
    return lax.ppermute(array, axis, [(i, (i + step) % peers) for i in range(peers)])


def to_strips_beside(array, step):
    peers = lax.axis_size(SPACE)
    pairs = [(i, i + step) for i in range(peers) if 0 <= i + step < peers]
    return lax.ppermute(array, SPACE, pairs)


def on_device(state, obs_index, obs_value, obs_scale, ksat, storage, recharge, newton_counts):
    members, rows, columns = state.shape
    flat = state.reshape(members * rows, columns)
    own = lax.axis_index(MEMBER)
    strip = lax.axis_index(SPACE)
    place = jnp.stack(
        [own, (strip > 0).astype(jnp.int32), (strip < lax.axis_size(SPACE) - 1).astype(jnp.int32)]
    ).astype(jnp.int32)

    seen = observed(flat, obs_index[None])
    same = shared(seen, MEMBER[0])
    other = along(same, MEMBER[1], 1)

    blocks = packed_blocks(place, flat)
    pieces = [blocks[0]]
    for i in range(1, OWNERS):
        pieces.append(along(blocks[i], MEMBER, -i))

    part = gram_blocks(place, same, other, obs_value[None], obs_scale[None])
    part = jnp.sum(shared(part, SPACE[0]), axis=0)
    part = jnp.sum(shared(part, SPACE[1]), axis=0)
    transform = transform_of(place, shared(part, MEMBER))

    cell_fields = jnp.stack([ksat, storage, recharge])
    fields_above = to_strips_beside(cell_fields[:, -2:], 1)
    fields_below = to_strips_beside(cell_fields[:, :2], -1)
    fields, edge_fields = block_fields(place, ksat, storage, recharge, fields_above, fields_below)
    wide_counts = jnp.broadcast_to(newton_counts[:, None], (MEMBERS, LANES))

    above = to_strips_beside(jnp.stack([p[ROWS - 2 :] for p in pieces]), 1)
    below = to_strips_beside(
        jnp.stack([jnp.concatenate([p[:2], p[EDGE:]], axis=0) for p in pieces]), -1
    )
    cells = analysed(transform, pieces, above, below)

    arrived = [None] * OWNERS
    for i in (2, 6, 3, 5, 4, 1, 7, 0):
        moved = forecast_of(i, place, newton_counts, wide_counts, fields, edge_fields, cells[i])
        arrived[i] = along(moved, MEMBER, i) if i else moved
    return unpacked(place, arrived).reshape(members, rows, columns)


def solution(mesh):
    x = 4
    finer = Mesh(
        mesh.devices.reshape(4, 2, -1, x), ("member_0", "member_1", "space_0", "space_1")
    )
    placed = (
        P(MEMBER, SPACE, None),
        P(SPACE),
        P(SPACE),
        P(SPACE),
        P(SPACE, None),
        P(SPACE, None),
        P(SPACE, None),
        P(),
    )
    return jax.shard_map(
        on_device, mesh=finer, in_specs=placed, out_specs=P(MEMBER, SPACE, None), check_vma=False
    )
```

```python
import functools

import jax
import jax.numpy as jnp
from jax import lax
from jax.experimental import pallas as pl
from jax.experimental.pallas import tpu as pltpu
from jax.sharding import Mesh
from jax.sharding import PartitionSpec as P

NS_ITERS = 12
DAMPING = 0.3
MEMBER = ("member_0", "member_1")
SPACE = ("space_0", "space_1")
HIGHEST = lax.Precision.HIGHEST
F32 = jnp.float32

OWNERS = 8
HELD = 32
ROWS = 16
LANES = 128
MEMBERS = OWNERS * HELD
EDGE = ROWS
SENT_ROWS = ROWS + 1
OUTER = 36
OWN = 72


def shape(*dims, dtype=F32):
    return jax.ShapeDtypeStruct(dims, dtype)


def whole(count):
    return [pl.BlockSpec(memory_space=pltpu.VMEM)] * count


def params(mib):
    return pltpu.CompilerParams(vmem_limit_bytes=mib * 2**20)


SCALARS = pl.BlockSpec(memory_space=pltpu.SMEM)


def lane_ids(rows=8):
    return lax.broadcasted_iota(jnp.int32, (rows, LANES), 1)


def turned(array, amount):
    return pltpu.roll(array, amount % LANES, 1)


def dot(a, b, dims=((1,), (0,))):
    return lax.dot_general(a, b, (dims, ((), ())), precision=HIGHEST, preferred_element_type=F32)


def observe_kernel(index_ref, state_ref, seen_ref):
    values = state_ref[...]
    high = values.astype(jnp.bfloat16)
    rest = values - high.astype(F32)
    middle = rest.astype(jnp.bfloat16)
    low = (rest - middle.astype(F32)).astype(jnp.bfloat16)
    width = values.shape[1]
    step = 256
    for first in range(0, index_ref.shape[1], step):
        cell = index_ref[:, first : first + step]
        row = cell // width
        column = cell - row * width
        places = lax.broadcasted_iota(jnp.int32, (width, step), 0)
        chosen = (places == column).astype(F32).astype(jnp.bfloat16)
        picked = jnp.dot(low, chosen, preferred_element_type=F32)
        picked += jnp.dot(middle, chosen, preferred_element_type=F32)
        picked += jnp.dot(high, chosen, preferred_element_type=F32)
        picked = picked.reshape(HELD, ROWS, step)
        rows = lax.broadcasted_iota(jnp.int32, (ROWS, step), 0)
        seen_ref[:, first : first + step] = jnp.sum(
            jnp.where((rows == row)[None], picked, 0.0), axis=1
        )


def observed(state, obs_index):
    return pl.pallas_call(
        observe_kernel,
        out_shape=shape(HELD, obs_index.shape[1]),
        in_specs=whole(2),
        out_specs=whole(1)[0],
        compiler_params=params(32),
        name="observe",
    )(obs_index, state)


ORDER = (0, 1, EDGE, ROWS - 2, ROWS - 1) + tuple(range(2, ROWS - 2))
PLACE = {unit: at for at, unit in enumerate(ORDER)}


def pack_kernel(place_ref, state_ref, after_ref, *refs):
    own = place_ref[0]
    sent_refs, column_ref = refs[:OWNERS], refs[OWNERS]
    lane = lane_ids()
    even = lane % 2 == 0
    near_left = (lane < OUTER) & even
    near_right = (lane < OUTER) & ~even
    far_left = (lane >= OUTER) & (lane < OUTER + 2 * ROWS) & even
    far_right = (lane >= OUTER + 3) & (lane < OUTER + 3 + 2 * ROWS) & ~even
    own_lanes = (lane >= OWN) & (lane < OWN + 2 * ROWS + 4)

    def one_group(group, carry):
        near, far = [], []
        members = pl.ds(pl.multiple_of(group * 8, 8), 8)
        lines = pl.ds(pl.multiple_of(group * 8 * ROWS, 8 * ROWS), 8 * ROWS)
        for slot in range(OWNERS):
            block = lax.rem(own - slot + OWNERS, OWNERS)
            packed_near = jnp.zeros((8, LANES), F32)
            packed_far = jnp.zeros((8, LANES), F32)
            start = pl.multiple_of(block * LANES, LANES)
            column_ref[slot] = state_ref[lines, pl.ds(start, LANES)]
            for r in range(ROWS):
                value = column_ref[slot, pl.ds(r, 8, stride=ROWS), :]
                sent_refs[slot][PLACE[r], members] = value
                at = 2 * (r + 1)
                packed_near = jnp.where(
                    (lane == at) | (lane == at + 1), turned(value, at + 1), packed_near
                )
                at = OUTER + 2 * r
                packed_far = jnp.where(
                    (lane == at) | (lane == at + 3), turned(value, at + 2), packed_far
                )
            near.append(packed_near)
            far.append(packed_far)
        for slot in range(OWNERS):
            block = lax.rem(own - slot + OWNERS, OWNERS)
            left, right = (slot + 1) % OWNERS, (slot - 1) % OWNERS
            has_left = (block > 0).astype(F32)
            has_right = (block < OWNERS - 1).astype(F32)
            edge = jnp.where(own_lanes, turned(near[slot], OWN), 0.0)
            edge = jnp.where(near_left, near[left] * has_left, edge)
            edge = jnp.where(far_left, far[left] * has_left, edge)
            edge = jnp.where(near_right, near[right] * has_right, edge)
            edge = jnp.where(far_right, far[right] * has_right, edge)
            sent_refs[slot][PLACE[EDGE], members] = edge
        return carry

    lax.fori_loop(0, HELD // 8, one_group, 0)


def packed_blocks(place, state, after):
    return pl.pallas_call(
        pack_kernel,
        out_shape=[shape(SENT_ROWS, HELD, LANES)] * OWNERS,
        in_specs=[SCALARS] + whole(1) + [pl.BlockSpec(memory_space=pl.ANY)],
        out_specs=whole(OWNERS),
        scratch_shapes=[pltpu.VMEM((OWNERS, 8 * ROWS, LANES), F32)],
        compiler_params=params(16),
        name="pack",
    )(place, state, after)


def border_kernel(*refs):
    pieces, down_ref, up_ref = refs[:OWNERS], refs[OWNERS], refs[OWNERS + 1]
    for i, piece in enumerate(pieces):
        down_ref[i] = piece[0:3]
        up_ref[i] = piece[2:5]


def borders(pieces):
    return pl.pallas_call(
        border_kernel,
        grid=(1,),
        out_shape=[shape(OWNERS, 3, HELD, LANES)] * 2,
        in_specs=[pl.BlockSpec((5, HELD, LANES), lambda g: (0, 0, 0))] * OWNERS,
        out_specs=[pl.BlockSpec((OWNERS, 3, HELD, LANES), lambda g: (0, 0, 0, 0))] * 2,
        compiler_params=params(8),
        name="borders",
    )(*pieces)


def gram_kernel(place_ref, same_ref, other_ref, value_ref, scale_ref, out_ref):
    own = place_ref[0]
    total = jnp.sum(same_ref[...], axis=(0, 1)) + jnp.sum(other_ref[...], axis=(0, 1))
    mean = (total / MEMBERS)[None]
    scale = scale_ref[...]
    weight = scale / jnp.sqrt(F32(MEMBERS - 1))
    blocks = []
    for k in range(5):
        at = lax.rem(own + k, OWNERS) // 2
        block = same_ref[at] if k % 2 == 0 else other_ref[at]
        blocks.append((block - mean) * weight)
    innovation = scale * (value_ref[...] - mean)
    left = jnp.concatenate([blocks[0], jnp.broadcast_to(innovation, (8, mean.shape[1]))], axis=0)
    out_ref[0:40] = dot(left, jnp.concatenate(blocks[:4], axis=0), ((1,), (1,)))
    last = jnp.concatenate([blocks[4], jnp.zeros((96, mean.shape[1]), F32)], axis=0)
    opposite = dot(blocks[0], last, ((1,), (1,)))
    packed = opposite[0:8]
    for g in range(1, 4):
        packed += turned(opposite[8 * g : 8 * g + 8], HELD * g)
    out_ref[40:48] = packed


def gram_blocks(place, same, other, value, scale):
    return pl.pallas_call(
        gram_kernel,
        out_shape=shape(48, LANES),
        in_specs=[SCALARS] + whole(4),
        out_specs=whole(1)[0],
        compiler_params=params(16),
        name="gram",
    )(place, same, other, value, scale)


def root_kernel(place_ref, parts_ref, out_ref, half_ref):
    own = place_ref[0]
    lane = lane_ids()
    drive_row = jnp.zeros((8, MEMBERS), F32)
    nothing = jnp.zeros((8, LANES), F32)
    for i in range(OWNERS):
        at = lax.rem(own + i, OWNERS)
        for g in range(4):
            rows = parts_ref[at, 8 * g : 8 * g + 8]
            rows = jnp.where(lane < HELD, 0.5 * rows, rows)
            fifth = turned(parts_ref[at, 40:48], -HELD * g)
            fifth = jnp.where(lane < HELD, 0.5 * fifth, 0.0)
            line = jnp.concatenate([rows, fifth], axis=1)
            half_ref[i * HELD + 8 * g : i * HELD + 8 * g + 8] = pltpu.roll(line, HELD * i, 1)
        drive = jnp.where(lane < HELD, parts_ref[at, 32:40], 0.0)
        line = jnp.concatenate([drive, nothing], axis=1)
        drive_row += pltpu.roll(line, HELD * i, 1)
    half = half_ref[...]
    rows = lax.broadcasted_iota(jnp.int32, (MEMBERS, MEMBERS), 0)
    columns = lax.broadcasted_iota(jnp.int32, (MEMBERS, MEMBERS), 1)
    identity = (rows == columns).astype(F32)
    big = identity + (half + half.T)
    norm = jnp.sqrt(jnp.sum(big * big))
    upper = big / norm
    middle = 1.5 * identity - 0.5 * upper
    upper = dot(upper, middle)
    lower = middle
    for _ in range(NS_ITERS - 2):
        middle = 1.5 * identity - 0.5 * dot(lower, upper)
        upper = dot(upper, middle)
        lower = dot(middle, lower)
    middle = 1.5 * identity - 0.5 * dot(lower, upper)
    root = dot(middle, lower) / jnp.sqrt(norm)
    weights = dot(dot(drive_row, root, ((1,), (1,))), root, ((1,), (1,)))
    out_ref[...] = root + weights[0:1] / jnp.sqrt(F32(MEMBERS - 1))


def transform_of(place, parts):
    return pl.pallas_call(
        root_kernel,
        out_shape=shape(MEMBERS, MEMBERS),
        in_specs=[SCALARS] + whole(1),
        out_specs=whole(1)[0],
        scratch_shapes=[pltpu.VMEM((MEMBERS, MEMBERS), F32)],
        compiler_params=params(16),
        name="root",
    )(place, parts)


UNITS = ROWS + 5


def halves(array):
    high = array.astype(jnp.bfloat16)
    return high, (array - high.astype(F32)).astype(jnp.bfloat16)


def analyse_kernel(*refs):
    transform_ref = refs[0]
    piece_refs = refs[1 : 1 + OWNERS]
    above_ref, below_ref = refs[1 + OWNERS : 3 + OWNERS]
    out_refs = refs[3 + OWNERS :]
    high, low = halves(transform_ref[...])
    lane = lax.broadcasted_iota(jnp.int32, (MEMBERS, LANES), 1)

    def joined(find):
        return jnp.concatenate([find(i) for i in range(OWNERS)], axis=0)

    def cells(unit):
        if unit > SENT_ROWS + 1:
            return joined(lambda i: below_ref[i, unit - SENT_ROWS - 2])
        if unit >= SENT_ROWS:
            return joined(lambda i: above_ref[i, unit - SENT_ROWS + 1])
        found = joined(lambda i: piece_refs[i][PLACE[unit]])
        if unit == EDGE:
            top = joined(lambda i: above_ref[i, 0])
            bottom = joined(lambda i: below_ref[i, 2])
            first = (lane < 2) | ((lane >= OWN) & (lane < OWN + 2))
            last = 2 * ROWS + 2
            final = ((lane >= last) & (lane < last + 2)) | (
                (lane >= OWN + last) & (lane < OWN + last + 2)
            )
            found = jnp.where(first, turned(top, -2 * ROWS), found)
            found = jnp.where(final, turned(bottom, 2 * ROWS), found)
        return found

    def product(a, b):
        return jnp.dot(a, b, preferred_element_type=F32)

    for first in range(0, UNITS, 2):
        units = range(first, min(first + 2, UNITS))
        found = [cells(u) for u in units]
        state = found[0] if len(found) == 1 else jnp.concatenate(found, axis=1)
        mean = jnp.sum(state, axis=0, keepdims=True) / MEMBERS
        large, small = halves(state - mean)
        result = product(low, large) + product(high, small) + product(high, large) + mean
        for at, unit in enumerate(units):
            for i in range(OWNERS):
                out_refs[i][unit] = result[
                    i * HELD : (i + 1) * HELD, at * LANES : (at + 1) * LANES
                ]


def analysed(transform, pieces, above, below):
    return pl.pallas_call(
        analyse_kernel,
        out_shape=[shape(UNITS, HELD, LANES)] * OWNERS,
        in_specs=whole(3 + OWNERS),
        out_specs=whole(OWNERS),
        compiler_params=params(24),
        name="analyse",
    )(transform, *pieces, above, below)


FIELD_ROWS = 20
NEAR_K, INNER_K, OUTER_K, NEAR_S, NEAR_R, NEAR_MASK = range(6)


def field_kernel(place_ref, ksat_ref, storage_ref, recharge_ref, above_ref, below_ref, out_ref, edge_ref):
    own = place_ref[0]
    lane = lane_ids(1)
    even = lane % 2 == 0
    start = pl.multiple_of(own * LANES, LANES)
    left_start = pl.multiple_of(jnp.maximum(own - 1, 0) * LANES, LANES)
    right_start = pl.multiple_of(jnp.minimum(own + 1, OWNERS - 1) * LANES, LANES)
    has_left = own > 0
    has_right = own < OWNERS - 1
    packed = [jnp.zeros((1, LANES), F32) for _ in range(5)]
    for which, ref in enumerate((ksat_ref, storage_ref, recharge_ref)):
        for place in range(FIELD_ROWS):
            r = place - 2

            def row_of(first):
                if r < 0:
                    return above_ref[which, r + 2 : r + 3, pl.ds(first, LANES)]
                if r >= ROWS:
                    return below_ref[which, r - ROWS : r - ROWS + 1, pl.ds(first, LANES)]
                return ref[r : r + 1, pl.ds(first, LANES)]

            mine = row_of(start)
            out_ref[which, place] = jnp.broadcast_to(mine, (8, LANES))
            if r < -1 or r > ROWS:
                if which == 0:
                    out_ref[3, place] = jnp.zeros((8, LANES), F32)
                    out_ref[4, place] = jnp.zeros((8, LANES), F32)
                continue
            at = 2 * (r + 1)
            here = (lane == at) | (lane == at + 1)
            left = jnp.where(has_left, row_of(left_start), 0.0)
            right = jnp.where(has_right, row_of(right_start), 0.0)
            near = jnp.where(lane < LANES // 2, right, left)
            near = turned(near, at + 1)
            if which == 0:
                out_ref[3, place] = jnp.broadcast_to(turned(mine, 1), (8, LANES))
                beyond = jnp.where(lane == 0, turned(left, 1), turned(right, -1))
                out_ref[4, place] = jnp.broadcast_to(beyond, (8, LANES))
                inner = jnp.where(even, turned(mine, at), turned(mine, at + 2))
                outer = jnp.where(even, turned(left, at + 2), turned(right, at))
                packed[NEAR_K] = jnp.where(here, near, packed[NEAR_K])
                packed[INNER_K] = jnp.where(here, inner, packed[INNER_K])
                packed[OUTER_K] = jnp.where(here, outer, packed[OUTER_K])
            elif which == 1:
                packed[NEAR_S] = jnp.where(here, near, packed[NEAR_S])
            else:
                packed[NEAR_R] = jnp.where(here, near, packed[NEAR_R])
    for n in range(5):
        edge_ref[n] = jnp.broadcast_to(packed[n], (8, LANES))
    lane = lane_ids()
    keep = jnp.where(lane % 2 == 0, has_left.astype(F32), has_right.astype(F32))
    edge_ref[NEAR_MASK] = jnp.where((lane >= 2) & (lane < 2 * ROWS + 2), keep, 0.0)


def block_fields(place, ksat, storage, recharge, above, below):
    return pl.pallas_call(
        field_kernel,
        out_shape=[shape(5, FIELD_ROWS, 8, LANES), shape(6, 8, LANES)],
        in_specs=[SCALARS] + whole(5),
        out_specs=whole(2),
        compiler_params=params(8),
        name="fields",
    )(place, ksat, storage, recharge, above, below)


def logistic(x):
    return 0.5 * jnp.tanh(0.5 * x) + 0.5


BATCH = 16


def forecast_kernel(shift, place_ref, counts_ref, wide_ref, field_ref, edge_field_ref, cells_ref, out_ref, iterate, goal, edge_row):
    own = place_ref[0]
    has_above = place_ref[1].astype(F32)
    has_below = place_ref[2].astype(F32)
    owner = lax.rem(own + shift, OWNERS)
    lane = lane_ids()
    even = lane % 2 == 0
    first_lane = lane == 0
    ends = first_lane | (lane == LANES - 1)
    sat, store, rain, left, ghosts = range(5)
    tiles = BATCH // 8

    def rolled(array, amount):
        return pltpu.roll(array, amount % LANES, 2)

    def face(level, other, cond, other_cond):
        return 0.5 * (cond + other_cond) * (other - level)

    def swapped(packed):
        return jnp.where(even, rolled(packed, -1), rolled(packed, 1))

    def one_batch(batch, carry):
        first_member = owner * HELD + batch * BATCH
        most = counts_ref[first_member]
        for n in range(1, BATCH):
            most = jnp.maximum(most, counts_ref[first_member + n])
        counts = wide_ref[pl.ds(pl.multiple_of(first_member, BATCH), BATCH)]
        counts = counts.reshape(tiles, 8, LANES)
        members = pl.ds(pl.multiple_of(batch * BATCH, BATCH), BATCH)

        def begun(level, flux, storage):
            bend = jnp.tanh(level)
            held = storage * bend
            return level + DAMPING * flux / (1.0 + storage * (1.0 - bend * bend)), level + held + flux

        def swept(value, target, storage, sweep):
            bend = jnp.tanh(value)
            derivative = 1.0 + storage * (1.0 - bend * bend)
            moved = value - DAMPING * (value + storage * bend - target) / derivative
            return jnp.where(counts > sweep, moved, value)

        def unit_at(unit):
            return cells_ref[unit, members].reshape(tiles, 8, LANES)

        def cell_at(r):
            if r < 0:
                return unit_at(SENT_ROWS + r + 2)
            if r >= ROWS:
                return unit_at(SENT_ROWS + 2 + r - ROWS)
            return unit_at(r)

        packed = unit_at(EDGE)
        near = jnp.where(lane < OUTER, packed, 0.0)
        inner = jnp.where(even, rolled(packed, -OWN - 1), rolled(packed, -OWN + 1))
        outer = jnp.where(even, rolled(packed, 2 - OUTER), rolled(packed, -OUTER))
        near_k = edge_field_ref[NEAR_K] * logistic(near)
        inner_k = edge_field_ref[INNER_K] * logistic(inner)
        outer_k = edge_field_ref[OUTER_K] * logistic(outer)
        inward = face(near, inner, near_k, inner_k)
        side = swapped(inward)
        flux = inward + face(near, outer, near_k, outer_k)
        flux += face(near, rolled(near, 2), near_k, rolled(near_k, 2))
        flux += face(near, rolled(near, -2), near_k, rolled(near_k, -2))
        flux += edge_field_ref[NEAR_R]
        value, target = begun(near, flux, edge_field_ref[NEAR_S])
        edge_row[0] = value
        edge_row[1] = target

        def conduct(level, r):
            return field_ref[sat, r + 2] * logistic(level)

        level, cond = cell_at(-1), conduct(cell_at(-1), -1)
        above = face(cell_at(-2), level, conduct(cell_at(-2), -2), cond)
        for r in range(-1, ROWS + 1):
            lower_level = cell_at(r + 1)
            lower_cond = conduct(lower_level, r + 1)
            under = face(level, lower_level, cond, lower_cond)
            beside = rolled(level, 1)
            across = face(beside, level, field_ref[left, r + 2] * logistic(beside), cond)
            across = jnp.where(first_lane, 0.0, across)
            flux = under - above + (rolled(across, -1) - across)
            flux -= jnp.where(ends, rolled(side, -2 * (r + 1) - 1), 0.0)
            flux += field_ref[rain, r + 2]
            iterate[r + 1], goal[r + 1] = begun(level, flux, field_ref[store, r + 2])
            level, cond, above = lower_level, lower_cond, under

        def first_sweep(sweep, carry):
            for n in range(ROWS + 2):
                iterate[n] = swept(iterate[n], goal[n], field_ref[store, n + 1], sweep)
            edge_row[0] = swept(edge_row[0], edge_row[1], edge_field_ref[NEAR_S], sweep)
            return carry

        lax.fori_loop(1, most, first_sweep, 0)

        near = edge_row[0] * edge_field_ref[NEAR_MASK]
        side = swapped(near)
        level = iterate[1]
        cond = conduct(level, 0)
        before = iterate[0] * has_above
        above = face(before, level, conduct(before, -1), cond)
        for r in range(ROWS):
            lower_level = iterate[r + 2]
            if r == ROWS - 1:
                lower_level = lower_level * has_below
            lower_cond = conduct(lower_level, r + 1)
            under = face(level, lower_level, cond, lower_cond)
            beside = rolled(level, 1)
            across = face(beside, level, field_ref[left, r + 2] * logistic(beside), cond)
            across = jnp.where(first_lane, 0.0, across)
            flux = under - above + (rolled(across, -1) - across)
            ghost = rolled(side, -2 * (r + 1) - 1)
            entering = face(level, ghost, cond, field_ref[ghosts, r + 2] * logistic(ghost))
            flux += jnp.where(ends, entering, 0.0)
            flux += field_ref[rain, r + 2]
            iterate[r + 1], goal[r + 1] = begun(level, flux, field_ref[store, r + 2])
            level, cond, above = lower_level, lower_cond, under

        def second_sweep(sweep, carry):
            for n in range(1, ROWS + 1):
                iterate[n] = swept(iterate[n], goal[n], field_ref[store, n + 1], sweep)
            return carry

        lax.fori_loop(1, most, second_sweep, 0)
        for r in range(ROWS):
            for tile in range(tiles):
                start = (batch * BATCH + tile * 8) * ROWS + r
                out_ref[pl.ds(start, 8, stride=ROWS), :] = iterate[r + 1, tile]
        return carry

    lax.fori_loop(0, HELD // BATCH, one_batch, 0)


def forecast_of(shift, place, counts, wide_counts, fields, edge_fields, cells):
    return pl.pallas_call(
        functools.partial(forecast_kernel, shift),
        out_shape=shape(HELD * ROWS, LANES),
        in_specs=[SCALARS, SCALARS] + whole(4),
        out_specs=whole(1)[0],
        scratch_shapes=[
            pltpu.VMEM((ROWS + 2, BATCH // 8, 8, LANES), F32),
            pltpu.VMEM((ROWS + 2, BATCH // 8, 8, LANES), F32),
            pltpu.VMEM((2, BATCH // 8, 8, LANES), F32),
        ],
        compiler_params=params(8),
        name="forecast",
    )(place, counts, wide_counts, fields, edge_fields, cells)


def unpack_kernel(place_ref, *refs):
    own = place_ref[0]
    pieces, out_ref = refs[:OWNERS], refs[OWNERS]
    for i, piece in enumerate(pieces):
        block = lax.rem(own - i + OWNERS, OWNERS)
        start = pl.multiple_of(block * LANES, LANES)
        out_ref[:, pl.ds(start, LANES)] = piece[...]


def unpacked(place, pieces):
    parts = 4
    size = HELD * ROWS // parts
    return pl.pallas_call(
        unpack_kernel,
        grid=(parts,),
        out_shape=shape(HELD * ROWS, OWNERS * LANES),
        in_specs=[SCALARS] + [pl.BlockSpec((size, LANES), lambda g: (g, 0))] * OWNERS,
        out_specs=pl.BlockSpec((size, OWNERS * LANES), lambda g: (g, 0)),
        compiler_params=params(8),
        name="unpack",
    )(place, *pieces)


def shared(array, axis):
    peers = lax.axis_size(axis)
    copies = jnp.broadcast_to(array, (peers, *array.shape))
    return lax.all_to_all(copies, axis, split_axis=0, concat_axis=0, tiled=True)


def along(array, axis, step):
    peers = lax.axis_size(axis)
    return lax.ppermute(array, axis, [(i, (i + step) % peers) for i in range(peers)])


def to_strips_beside(array, step):
    peers = lax.axis_size(SPACE)
    pairs = [(i, i + step) for i in range(peers) if 0 <= i + step < peers]
    return lax.ppermute(array, SPACE, pairs)


def on_device(state, obs_index, obs_value, obs_scale, ksat, storage, recharge, newton_counts):
    members, rows, columns = state.shape
    flat = state.reshape(members * rows, columns)
    own = lax.axis_index(MEMBER)
    strip = lax.axis_index(SPACE)
    place = jnp.stack(
        [own, (strip > 0).astype(jnp.int32), (strip < lax.axis_size(SPACE) - 1).astype(jnp.int32)]
    ).astype(jnp.int32)

    seen = observed(flat, obs_index[None])
    same = shared(seen, MEMBER[0])

    cell_fields, _ = lax.optimization_barrier((jnp.stack([ksat, storage, recharge]), seen))
    fields_above = to_strips_beside(cell_fields[:, -2:], 1)
    fields_below = to_strips_beside(cell_fields[:, :2], -1)
    blocks = packed_blocks(place, flat, seen)
    fields, edge_fields = block_fields(place, ksat, storage, recharge, fields_above, fields_below)
    wide_counts = jnp.broadcast_to(newton_counts[:, None], (MEMBERS, LANES))
    same, blocks, fields, edge_fields, wide_counts = lax.optimization_barrier(
        (same, blocks, fields, edge_fields, wide_counts)
    )
    other = along(same, MEMBER[1], 1)

    pieces = [blocks[0]] + [None] * (OWNERS - 1)
    for i in (2, 6):
        pieces[i] = along(blocks[i], MEMBER, -i)
    part = gram_blocks(place, same, other, obs_value[None], obs_scale[None])
    part, blocks = lax.optimization_barrier((part, blocks))
    for i in (3, 5, 4, 1, 7):
        pieces[i] = along(blocks[i], MEMBER, -i)
    part = jnp.sum(shared(part, SPACE[0]), axis=0)
    part = jnp.sum(shared(part, SPACE[1]), axis=0)
    part, pieces = lax.optimization_barrier((part, pieces))
    down, up = borders(pieces)
    above = to_strips_beside(up, 1)
    below = to_strips_beside(down, -1)
    transform = transform_of(place, shared(part, MEMBER))
    cells = analysed(transform, pieces, above, below)

    arrived = [None] * OWNERS
    for i in (2, 6, 3, 5, 4, 1, 7, 0):
        moved = forecast_of(i, place, newton_counts, wide_counts, fields, edge_fields, cells[i])
        arrived[i] = along(moved, MEMBER, i) if i else moved
    return unpacked(place, arrived).reshape(members, rows, columns)


def solution(mesh):
    x = 4
    finer = Mesh(
        mesh.devices.reshape(4, 2, -1, x), ("member_0", "member_1", "space_0", "space_1")
    )
    placed = (
        P(MEMBER, SPACE, None),
        P(SPACE),
        P(SPACE),
        P(SPACE),
        P(SPACE, None),
        P(SPACE, None),
        P(SPACE, None),
        P(),
    )
    return jax.shard_map(
        on_device, mesh=finer, in_specs=placed, out_specs=P(MEMBER, SPACE, None), check_vma=False
    )
```

```python
import functools

import jax
import jax.numpy as jnp
from jax import lax
from jax.experimental import pallas as pl
from jax.experimental.pallas import tpu as pltpu
from jax.sharding import Mesh
from jax.sharding import PartitionSpec as P

NS_ITERS = 12
DAMPING = 0.3
MEMBER = ("member_0", "member_1")
SPACE = ("space_0", "space_1")
HIGHEST = lax.Precision.HIGHEST
F32 = jnp.float32

OWNERS = 8
HELD = 32
ROWS = 16
LANES = 128
MEMBERS = OWNERS * HELD
EDGE = ROWS
SENT_ROWS = ROWS + 1
OUTER = 36
OWN = 72


def shape(*dims, dtype=F32):
    return jax.ShapeDtypeStruct(dims, dtype)


def whole(count):
    return [pl.BlockSpec(memory_space=pltpu.VMEM)] * count


def params(mib):
    return pltpu.CompilerParams(vmem_limit_bytes=mib * 2**20)


SCALARS = pl.BlockSpec(memory_space=pltpu.SMEM)


def lane_ids(rows=8):
    return lax.broadcasted_iota(jnp.int32, (rows, LANES), 1)


def turned(array, amount):
    return pltpu.roll(array, amount % LANES, 1)


def dot(a, b, dims=((1,), (0,))):
    return lax.dot_general(a, b, (dims, ((), ())), precision=HIGHEST, preferred_element_type=F32)


def observe_kernel(index_ref, state_ref, seen_ref):
    values = state_ref[...]
    high = values.astype(jnp.bfloat16)
    rest = values - high.astype(F32)
    middle = rest.astype(jnp.bfloat16)
    low = (rest - middle.astype(F32)).astype(jnp.bfloat16)
    width = values.shape[1]
    step = 256
    for first in range(0, index_ref.shape[1], step):
        cell = index_ref[:, first : first + step]
        row = cell // width
        column = cell - row * width
        places = lax.broadcasted_iota(jnp.int32, (width, step), 0)
        chosen = (places == column).astype(F32).astype(jnp.bfloat16)
        picked = jnp.dot(low, chosen, preferred_element_type=F32)
        picked += jnp.dot(middle, chosen, preferred_element_type=F32)
        picked += jnp.dot(high, chosen, preferred_element_type=F32)
        picked = picked.reshape(HELD, ROWS, step)
        rows = lax.broadcasted_iota(jnp.int32, (ROWS, step), 0)
        seen_ref[:, first : first + step] = jnp.sum(
            jnp.where((rows == row)[None], picked, 0.0), axis=1
        )


def observed(state, obs_index):
    return pl.pallas_call(
        observe_kernel,
        out_shape=shape(HELD, obs_index.shape[1]),
        in_specs=whole(2),
        out_specs=whole(1)[0],
        compiler_params=params(20),
        name="observe",
    )(obs_index, state)


ORDER = (0, 1, EDGE, ROWS - 2, ROWS - 1) + tuple(range(2, ROWS - 2))
PLACE = {unit: at for at, unit in enumerate(ORDER)}


def pack_kernel(place_ref, state_ref, after_ref, *refs):
    own = place_ref[0]
    sent_refs, column_ref = refs[:OWNERS], refs[OWNERS]
    lane = lane_ids()
    even = lane % 2 == 0
    near_left = (lane < OUTER) & even
    near_right = (lane < OUTER) & ~even
    far_left = (lane >= OUTER) & (lane < OUTER + 2 * ROWS) & even
    far_right = (lane >= OUTER + 3) & (lane < OUTER + 3 + 2 * ROWS) & ~even
    own_lanes = (lane >= OWN) & (lane < OWN + 2 * ROWS + 4)

    def one_group(group, carry):
        near, far = [], []
        members = pl.ds(pl.multiple_of(group * 8, 8), 8)
        lines = pl.ds(pl.multiple_of(group * 8 * ROWS, 8 * ROWS), 8 * ROWS)
        for slot in range(OWNERS):
            block = lax.rem(own - slot + OWNERS, OWNERS)
            packed_near = jnp.zeros((8, LANES), F32)
            packed_far = jnp.zeros((8, LANES), F32)
            start = pl.multiple_of(block * LANES, LANES)
            column_ref[slot] = state_ref[lines, pl.ds(start, LANES)]
            for r in range(ROWS):
                value = column_ref[slot, pl.ds(r, 8, stride=ROWS), :]
                sent_refs[slot][PLACE[r], members] = value
                at = 2 * (r + 1)
                packed_near = jnp.where(
                    (lane == at) | (lane == at + 1), turned(value, at + 1), packed_near
                )
                at = OUTER + 2 * r
                packed_far = jnp.where(
                    (lane == at) | (lane == at + 3), turned(value, at + 2), packed_far
                )
            near.append(packed_near)
            far.append(packed_far)
        for slot in range(OWNERS):
            block = lax.rem(own - slot + OWNERS, OWNERS)
            left, right = (slot + 1) % OWNERS, (slot - 1) % OWNERS
            has_left = (block > 0).astype(F32)
            has_right = (block < OWNERS - 1).astype(F32)
            edge = jnp.where(own_lanes, turned(near[slot], OWN), 0.0)
            edge = jnp.where(near_left, near[left] * has_left, edge)
            edge = jnp.where(far_left, far[left] * has_left, edge)
            edge = jnp.where(near_right, near[right] * has_right, edge)
            edge = jnp.where(far_right, far[right] * has_right, edge)
            sent_refs[slot][PLACE[EDGE], members] = edge
        return carry

    lax.fori_loop(0, HELD // 8, one_group, 0)


def packed_blocks(place, state, after):
    return pl.pallas_call(
        pack_kernel,
        out_shape=[shape(SENT_ROWS, HELD, LANES)] * OWNERS,
        in_specs=[SCALARS] + whole(1) + [pl.BlockSpec(memory_space=pl.ANY)],
        out_specs=whole(OWNERS),
        scratch_shapes=[pltpu.VMEM((OWNERS, 8 * ROWS, LANES), F32)],
        compiler_params=params(8),
        name="pack",
    )(place, state, after)


BORDER = OWNERS * 3 * HELD
FIELD_LINES = 3 * 2 * OWNERS


def border_kernel(*refs):
    pieces, fields = refs[:OWNERS], refs[OWNERS : OWNERS + 3]
    down_ref, up_ref = refs[OWNERS + 3 :]
    size = 3 * HELD
    for i, piece in enumerate(pieces):
        down_ref[i * size : (i + 1) * size] = piece[0:3].reshape(size, LANES)
        up_ref[i * size : (i + 1) * size] = piece[2:5].reshape(size, LANES)
    for which, ref in enumerate(fields):
        for block in range(OWNERS):
            at = BORDER + (which * OWNERS + block) * 2
            lanes = slice(block * LANES, (block + 1) * LANES)
            down_ref[at : at + 2] = ref[0:2, lanes]
            up_ref[at : at + 2] = ref[ROWS - 2 : ROWS, lanes]


def borders(pieces, fields):
    size = BORDER + FIELD_LINES
    return pl.pallas_call(
        border_kernel,
        grid=(1,),
        out_shape=[shape(size, LANES)] * 2,
        in_specs=[pl.BlockSpec((5, HELD, LANES), lambda g: (0, 0, 0))] * OWNERS
        + [pl.BlockSpec((ROWS, OWNERS * LANES), lambda g: (0, 0))] * 3,
        out_specs=[pl.BlockSpec((size, LANES), lambda g: (0, 0))] * 2,
        compiler_params=params(6),
        name="borders",
    )(*pieces, *fields)


def gram_kernel(place_ref, same_ref, other_ref, value_ref, scale_ref, out_ref):
    own = place_ref[0]
    total = jnp.sum(same_ref[...], axis=(0, 1)) + jnp.sum(other_ref[...], axis=(0, 1))
    mean = (total / MEMBERS)[None]
    scale = scale_ref[...]
    weight = scale / jnp.sqrt(F32(MEMBERS - 1))
    blocks = []
    for k in range(5):
        at = lax.rem(own + k, OWNERS) // 2
        block = same_ref[at] if k % 2 == 0 else other_ref[at]
        blocks.append((block - mean) * weight)
    innovation = scale * (value_ref[...] - mean)
    left = jnp.concatenate([blocks[0], jnp.broadcast_to(innovation, (8, mean.shape[1]))], axis=0)
    out_ref[0:40] = dot(left, jnp.concatenate(blocks[:4], axis=0), ((1,), (1,)))
    last = jnp.concatenate([blocks[4], jnp.zeros((96, mean.shape[1]), F32)], axis=0)
    opposite = dot(blocks[0], last, ((1,), (1,)))
    packed = opposite[0:8]
    for g in range(1, 4):
        packed += turned(opposite[8 * g : 8 * g + 8], HELD * g)
    out_ref[40:48] = packed


def gram_blocks(place, same, other, value, scale):
    return pl.pallas_call(
        gram_kernel,
        out_shape=shape(48, LANES),
        in_specs=[SCALARS] + whole(4),
        out_specs=whole(1)[0],
        compiler_params=params(8),
        name="gram",
    )(place, same, other, value, scale)


def thirds(array):
    high = array.astype(jnp.bfloat16)
    rest = array - high.astype(F32)
    middle = rest.astype(jnp.bfloat16)
    return high, middle, (rest - middle.astype(F32)).astype(jnp.bfloat16)


def six_products(a, b):
    def product(i, j):
        return jnp.dot(a[i], b[j], preferred_element_type=F32)

    small = product(0, 2) + product(2, 0) + product(1, 1)
    return (small + (product(0, 1) + product(1, 0))) + product(0, 0)


def root_kernel(place_ref, parts_ref, out_ref, half_ref):
    own = place_ref[0]
    lane = lane_ids()
    drive_row = jnp.zeros((8, MEMBERS), F32)
    nothing = jnp.zeros((8, LANES), F32)
    for i in range(OWNERS):
        at = lax.rem(own + i, OWNERS)
        for g in range(4):
            rows = parts_ref[at, 8 * g : 8 * g + 8]
            rows = jnp.where(lane < HELD, 0.5 * rows, rows)
            fifth = turned(parts_ref[at, 40:48], -HELD * g)
            fifth = jnp.where(lane < HELD, 0.5 * fifth, 0.0)
            line = jnp.concatenate([rows, fifth], axis=1)
            half_ref[i * HELD + 8 * g : i * HELD + 8 * g + 8] = pltpu.roll(line, HELD * i, 1)
        drive = jnp.where(lane < HELD, parts_ref[at, 32:40], 0.0)
        line = jnp.concatenate([drive, nothing], axis=1)
        drive_row += pltpu.roll(line, HELD * i, 1)
    half = half_ref[...]
    rows = lax.broadcasted_iota(jnp.int32, (MEMBERS, MEMBERS), 0)
    columns = lax.broadcasted_iota(jnp.int32, (MEMBERS, MEMBERS), 1)
    identity = (rows == columns).astype(F32)
    big = identity + (half + half.T)
    norm = jnp.sqrt(jnp.sum(big * big))
    upper = big / norm
    middle = 1.5 * identity - 0.5 * upper
    middle_parts = thirds(middle)
    upper = six_products(thirds(upper), middle_parts)
    lower = middle
    lower_parts = middle_parts
    for _ in range(NS_ITERS - 2):
        upper_parts = thirds(upper)
        middle_parts = thirds(1.5 * identity - 0.5 * six_products(lower_parts, upper_parts))
        upper = six_products(upper_parts, middle_parts)
        lower = six_products(middle_parts, lower_parts)
        lower_parts = thirds(lower)
    middle = 1.5 * identity - 0.5 * six_products(lower_parts, thirds(upper))
    root = six_products(thirds(middle), lower_parts) / jnp.sqrt(norm)
    weights = dot(dot(drive_row, root, ((1,), (1,))), root, ((1,), (1,)))
    out_ref[...] = root + weights[0:1] / jnp.sqrt(F32(MEMBERS - 1))


def transform_of(place, parts):
    return pl.pallas_call(
        root_kernel,
        out_shape=shape(MEMBERS, MEMBERS),
        in_specs=[SCALARS] + whole(1),
        out_specs=whole(1)[0],
        scratch_shapes=[pltpu.VMEM((MEMBERS, MEMBERS), F32)],
        compiler_params=params(12),
        cost_estimate=pl.CostEstimate(flops=10**10, bytes_accessed=10**6, transcendentals=0),
        name="root",
    )(place, parts)


UNITS = ROWS + 5


def halves(array):
    high = array.astype(jnp.bfloat16)
    return high, (array - high.astype(F32)).astype(jnp.bfloat16)


def analyse_kernel(*refs):
    transform_ref = refs[0]
    piece_refs = refs[1 : 1 + OWNERS]
    above_ref, below_ref = refs[1 + OWNERS : 3 + OWNERS]
    out_refs = refs[3 + OWNERS :]
    high, low = halves(transform_ref[...])
    lane = lax.broadcasted_iota(jnp.int32, (MEMBERS, LANES), 1)

    def joined(find):
        return jnp.concatenate([find(i) for i in range(OWNERS)], axis=0)

    def border(ref, n):
        return joined(lambda i: ref[(i * 3 + n) * HELD : (i * 3 + n + 1) * HELD])

    def cells(unit):
        if unit > SENT_ROWS + 1:
            return border(below_ref, unit - SENT_ROWS - 2)
        if unit >= SENT_ROWS:
            return border(above_ref, unit - SENT_ROWS + 1)
        found = joined(lambda i: piece_refs[i][PLACE[unit]])
        if unit == EDGE:
            top = border(above_ref, 0)
            bottom = border(below_ref, 2)
            first = (lane < 2) | ((lane >= OWN) & (lane < OWN + 2))
            last = 2 * ROWS + 2
            final = ((lane >= last) & (lane < last + 2)) | (
                (lane >= OWN + last) & (lane < OWN + last + 2)
            )
            found = jnp.where(first, turned(top, -2 * ROWS), found)
            found = jnp.where(final, turned(bottom, 2 * ROWS), found)
        return found

    def product(a, b):
        return jnp.dot(a, b, preferred_element_type=F32)

    for first in range(0, UNITS, 2):
        units = range(first, min(first + 2, UNITS))
        found = [cells(u) for u in units]
        state = found[0] if len(found) == 1 else jnp.concatenate(found, axis=1)
        mean = jnp.sum(state, axis=0, keepdims=True) / MEMBERS
        large, small = halves(state - mean)
        result = product(low, large) + product(high, small) + product(high, large) + mean
        for at, unit in enumerate(units):
            for i in range(OWNERS):
                out_refs[i][unit] = result[
                    i * HELD : (i + 1) * HELD, at * LANES : (at + 1) * LANES
                ]


def analysed(transform, pieces, above, below):
    return pl.pallas_call(
        analyse_kernel,
        out_shape=[shape(UNITS, HELD, LANES)] * OWNERS,
        in_specs=whole(3 + OWNERS),
        out_specs=whole(OWNERS),
        compiler_params=params(14),
        name="analyse",
    )(transform, *pieces, above, below)


FIELD_ROWS = 20
NEAR_K, INNER_K, OUTER_K, NEAR_S, NEAR_R, NEAR_MASK = range(6)


def field_kernel(place_ref, ksat_ref, storage_ref, recharge_ref, above_ref, below_ref, out_ref, edge_ref):
    own = place_ref[0]
    lane = lane_ids(1)
    even = lane % 2 == 0
    left_block = jnp.maximum(own - 1, 0)
    right_block = jnp.minimum(own + 1, OWNERS - 1)
    has_left = own > 0
    has_right = own < OWNERS - 1
    packed = [jnp.zeros((1, LANES), F32) for _ in range(5)]
    for which, ref in enumerate((ksat_ref, storage_ref, recharge_ref)):
        for place in range(FIELD_ROWS):
            r = place - 2

            def row_of(block):
                line = (which * OWNERS + block) * 2
                if r < 0:
                    return above_ref[pl.ds(line + r + 2, 1)]
                if r >= ROWS:
                    return below_ref[pl.ds(line + r - ROWS, 1)]
                return ref[r : r + 1, pl.ds(pl.multiple_of(block * LANES, LANES), LANES)]

            mine = row_of(own)
            out_ref[which, place] = jnp.broadcast_to(mine, (8, LANES))
            if r < -1 or r > ROWS:
                if which == 0:
                    out_ref[3, place] = jnp.zeros((8, LANES), F32)
                    out_ref[4, place] = jnp.zeros((8, LANES), F32)
                continue
            at = 2 * (r + 1)
            here = (lane == at) | (lane == at + 1)
            left = jnp.where(has_left, row_of(left_block), 0.0)
            right = jnp.where(has_right, row_of(right_block), 0.0)
            near = jnp.where(lane < LANES // 2, right, left)
            near = turned(near, at + 1)
            if which == 0:
                out_ref[3, place] = jnp.broadcast_to(turned(mine, 1), (8, LANES))
                beyond = jnp.where(lane == 0, turned(left, 1), turned(right, -1))
                out_ref[4, place] = jnp.broadcast_to(beyond, (8, LANES))
                inner = jnp.where(even, turned(mine, at), turned(mine, at + 2))
                outer = jnp.where(even, turned(left, at + 2), turned(right, at))
                packed[NEAR_K] = jnp.where(here, near, packed[NEAR_K])
                packed[INNER_K] = jnp.where(here, inner, packed[INNER_K])
                packed[OUTER_K] = jnp.where(here, outer, packed[OUTER_K])
            elif which == 1:
                packed[NEAR_S] = jnp.where(here, near, packed[NEAR_S])
            else:
                packed[NEAR_R] = jnp.where(here, near, packed[NEAR_R])
    for n in range(5):
        edge_ref[n] = jnp.broadcast_to(packed[n], (8, LANES))
    lane = lane_ids()
    keep = jnp.where(lane % 2 == 0, has_left.astype(F32), has_right.astype(F32))
    edge_ref[NEAR_MASK] = jnp.where((lane >= 2) & (lane < 2 * ROWS + 2), keep, 0.0)


def block_fields(place, ksat, storage, recharge, above, below):
    last = pl.BlockSpec((FIELD_LINES, LANES), lambda g: (BORDER // FIELD_LINES, 0))
    mine = pl.BlockSpec((ROWS, OWNERS * LANES), lambda g: (0, 0))
    return pl.pallas_call(
        field_kernel,
        grid=(1,),
        out_shape=[shape(5, FIELD_ROWS, 8, LANES), shape(6, 8, LANES)],
        in_specs=[SCALARS] + [mine] * 3 + [last] * 2,
        out_specs=[
            pl.BlockSpec((5, FIELD_ROWS, 8, LANES), lambda g: (0, 0, 0, 0)),
            pl.BlockSpec((6, 8, LANES), lambda g: (0, 0, 0)),
        ],
        compiler_params=params(6),
        name="fields",
    )(place, ksat, storage, recharge, above, below)


def logistic(x):
    return 0.5 * jnp.tanh(0.5 * x) + 0.5


BATCH = 16


def forecast_kernel(shifts, place_ref, counts_ref, wide_ref, field_ref, edge_field_ref, *refs):
    cells_refs, out_refs = refs[: len(shifts)], refs[len(shifts) : 2 * len(shifts)]
    iterate, goal, edge_row = refs[2 * len(shifts) :]
    own = place_ref[0]
    has_above = place_ref[1].astype(F32)
    has_below = place_ref[2].astype(F32)
    lane = lane_ids()
    even = lane % 2 == 0
    first_lane = lane == 0
    ends = first_lane | (lane == LANES - 1)
    sat, store, rain, left, ghosts = range(5)
    tiles = BATCH // 8

    def rolled(array, amount):
        return pltpu.roll(array, amount % LANES, 2)

    def face(level, other, cond, other_cond):
        return 0.5 * (cond + other_cond) * (other - level)

    def swapped(packed):
        return jnp.where(even, rolled(packed, -1), rolled(packed, 1))

    def one_batch(which, batch, carry):
        cells_ref, out_ref = cells_refs[which], out_refs[which]
        owner = lax.rem(own + shifts[which], OWNERS)
        first_member = owner * HELD + batch * BATCH
        most = counts_ref[first_member]
        for n in range(1, BATCH):
            most = jnp.maximum(most, counts_ref[first_member + n])
        counts = wide_ref[pl.ds(pl.multiple_of(first_member, BATCH), BATCH)]
        counts = counts.reshape(tiles, 8, LANES)
        members = pl.ds(pl.multiple_of(batch * BATCH, BATCH), BATCH)

        def begun(level, flux, storage):
            bend = jnp.tanh(level)
            held = storage * bend
            return level + DAMPING * flux / (1.0 + storage * (1.0 - bend * bend)), level + held + flux

        def swept(value, target, storage, sweep):
            bend = jnp.tanh(value)
            derivative = 1.0 + storage * (1.0 - bend * bend)
            moved = value - DAMPING * (value + storage * bend - target) / derivative
            return jnp.where(counts > sweep, moved, value)

        def unit_at(unit):
            return cells_ref[unit, members].reshape(tiles, 8, LANES)

        def cell_at(r):
            if r < 0:
                return unit_at(SENT_ROWS + r + 2)
            if r >= ROWS:
                return unit_at(SENT_ROWS + 2 + r - ROWS)
            return unit_at(r)

        packed = unit_at(EDGE)
        near = jnp.where(lane < OUTER, packed, 0.0)
        inner = jnp.where(even, rolled(packed, -OWN - 1), rolled(packed, -OWN + 1))
        outer = jnp.where(even, rolled(packed, 2 - OUTER), rolled(packed, -OUTER))
        near_k = edge_field_ref[NEAR_K] * logistic(near)
        inner_k = edge_field_ref[INNER_K] * logistic(inner)
        outer_k = edge_field_ref[OUTER_K] * logistic(outer)
        inward = face(near, inner, near_k, inner_k)
        side = swapped(inward)
        flux = inward + face(near, outer, near_k, outer_k)
        flux += face(near, rolled(near, 2), near_k, rolled(near_k, 2))
        flux += face(near, rolled(near, -2), near_k, rolled(near_k, -2))
        flux += edge_field_ref[NEAR_R]
        value, target = begun(near, flux, edge_field_ref[NEAR_S])
        edge_row[0] = value
        edge_row[1] = target

        def conduct(level, r):
            return field_ref[sat, r + 2] * logistic(level)

        level, cond = cell_at(-1), conduct(cell_at(-1), -1)
        above = face(cell_at(-2), level, conduct(cell_at(-2), -2), cond)
        for r in range(-1, ROWS + 1):
            lower_level = cell_at(r + 1)
            lower_cond = conduct(lower_level, r + 1)
            under = face(level, lower_level, cond, lower_cond)
            beside = rolled(level, 1)
            across = face(beside, level, field_ref[left, r + 2] * logistic(beside), cond)
            across = jnp.where(first_lane, 0.0, across)
            flux = under - above + (rolled(across, -1) - across)
            flux -= jnp.where(ends, rolled(side, -2 * (r + 1) - 1), 0.0)
            flux += field_ref[rain, r + 2]
            iterate[r + 1], goal[r + 1] = begun(level, flux, field_ref[store, r + 2])
            level, cond, above = lower_level, lower_cond, under

        def first_sweep(sweep, carry):
            for n in range(ROWS + 2):
                iterate[n] = swept(iterate[n], goal[n], field_ref[store, n + 1], sweep)
            edge_row[0] = swept(edge_row[0], edge_row[1], edge_field_ref[NEAR_S], sweep)
            return carry

        lax.fori_loop(1, most, first_sweep, 0)

        near = edge_row[0] * edge_field_ref[NEAR_MASK]
        side = swapped(near)
        level = iterate[1]
        cond = conduct(level, 0)
        before = iterate[0] * has_above
        above = face(before, level, conduct(before, -1), cond)
        for r in range(ROWS):
            lower_level = iterate[r + 2]
            if r == ROWS - 1:
                lower_level = lower_level * has_below
            lower_cond = conduct(lower_level, r + 1)
            under = face(level, lower_level, cond, lower_cond)
            beside = rolled(level, 1)
            across = face(beside, level, field_ref[left, r + 2] * logistic(beside), cond)
            across = jnp.where(first_lane, 0.0, across)
            flux = under - above + (rolled(across, -1) - across)
            ghost = rolled(side, -2 * (r + 1) - 1)
            entering = face(level, ghost, cond, field_ref[ghosts, r + 2] * logistic(ghost))
            flux += jnp.where(ends, entering, 0.0)
            flux += field_ref[rain, r + 2]
            iterate[r + 1], goal[r + 1] = begun(level, flux, field_ref[store, r + 2])
            level, cond, above = lower_level, lower_cond, under

        def second_sweep(sweep, carry):
            for n in range(1, ROWS + 1):
                iterate[n] = swept(iterate[n], goal[n], field_ref[store, n + 1], sweep)
            return carry

        lax.fori_loop(1, most, second_sweep, 0)
        for r in range(ROWS):
            for tile in range(tiles):
                start = (batch * BATCH + tile * 8) * ROWS + r
                out_ref[pl.ds(start, 8, stride=ROWS), :] = iterate[r + 1, tile]
        return carry

    for which in range(len(shifts)):
        lax.fori_loop(0, HELD // BATCH, functools.partial(one_batch, which), 0)


def forecasts(shifts, place, counts, wide_counts, fields, edge_fields, cells):
    many = len(shifts)
    return pl.pallas_call(
        functools.partial(forecast_kernel, shifts),
        out_shape=[shape(HELD * ROWS, LANES)] * many,
        in_specs=[SCALARS, SCALARS] + whole(3 + many),
        out_specs=whole(many),
        scratch_shapes=[
            pltpu.VMEM((ROWS + 2, BATCH // 8, 8, LANES), F32),
            pltpu.VMEM((ROWS + 2, BATCH // 8, 8, LANES), F32),
            pltpu.VMEM((2, BATCH // 8, 8, LANES), F32),
        ],
        compiler_params=params(6),
        cost_estimate=pl.CostEstimate(flops=1, bytes_accessed=1, transcendentals=0),
        name="forecast",
    )(place, counts, wide_counts, fields, edge_fields, *cells)


def unpack_kernel(place_ref, *refs):
    own = place_ref[0]
    pieces, out_ref = refs[:OWNERS], refs[OWNERS]
    for i, piece in enumerate(pieces):
        block = lax.rem(own - i + OWNERS, OWNERS)
        start = pl.multiple_of(block * LANES, LANES)
        out_ref[:, pl.ds(start, LANES)] = piece[...]


def unpacked(place, pieces):
    parts = 4
    size = HELD * ROWS // parts
    return pl.pallas_call(
        unpack_kernel,
        grid=(parts,),
        out_shape=shape(HELD * ROWS, OWNERS * LANES),
        in_specs=[SCALARS] + [pl.BlockSpec((size, LANES), lambda g: (g, 0))] * OWNERS,
        out_specs=pl.BlockSpec((size, OWNERS * LANES), lambda g: (g, 0)),
        compiler_params=params(8),
        name="unpack",
    )(place, *pieces)


def shared(array, axis):
    peers = lax.axis_size(axis)
    copies = jnp.broadcast_to(array, (peers, *array.shape))
    return lax.all_to_all(copies, axis, split_axis=0, concat_axis=0, tiled=True)


def along(array, axis, step):
    peers = lax.axis_size(axis)
    return lax.ppermute(array, axis, [(i, (i + step) % peers) for i in range(peers)])


def to_strips_beside(array, step):
    peers = lax.axis_size(SPACE)
    pairs = [(i, i + step) for i in range(peers) if 0 <= i + step < peers]
    return lax.ppermute(array, SPACE, pairs)


def on_device(state, obs_index, obs_value, obs_scale, ksat, storage, recharge, newton_counts):
    members, rows, columns = state.shape
    flat = state.reshape(members * rows, columns)
    own = lax.axis_index(MEMBER)
    strip = lax.axis_index(SPACE)
    place = jnp.stack(
        [own, (strip > 0).astype(jnp.int32), (strip < lax.axis_size(SPACE) - 1).astype(jnp.int32)]
    ).astype(jnp.int32)

    seen = observed(flat, obs_index[None])
    same = shared(seen, MEMBER[0])

    blocks = packed_blocks(place, flat, seen)
    wide_counts = jnp.broadcast_to(newton_counts[:, None], (MEMBERS, LANES))
    same, blocks, wide_counts = lax.optimization_barrier((same, blocks, wide_counts))
    other = along(same, MEMBER[1], 1)

    pieces = [blocks[0]] + [None] * (OWNERS - 1)
    for i in (2, 6):
        pieces[i] = along(blocks[i], MEMBER, -i)
    part = gram_blocks(place, same, other, obs_value[None], obs_scale[None])
    part, blocks = lax.optimization_barrier((part, blocks))
    for i in (3, 5, 4, 1, 7):
        pieces[i] = along(blocks[i], MEMBER, -i)
    part = jnp.sum(shared(part, SPACE[0]), axis=0)
    part = jnp.sum(shared(part, SPACE[1]), axis=0)
    part, pieces = lax.optimization_barrier((part, pieces))
    parts = shared(part, MEMBER)
    down, up = borders(pieces, (ksat, storage, recharge))
    parts, down, up = lax.optimization_barrier((parts, down, up))
    above = to_strips_beside(up, 1)
    below = to_strips_beside(down, -1)
    transform = transform_of(place, parts)
    fields, edge_fields = block_fields(place, ksat, storage, recharge, above, below)
    cells = analysed(transform, pieces, above, below)

    arrived = [None] * OWNERS
    for shifts in ((2,), (6,), (3, 5), (4, 1), (7, 0)):
        moved = forecasts(
            shifts, place, newton_counts, wide_counts, fields, edge_fields, [cells[i] for i in shifts]
        )
        moved, cells = lax.optimization_barrier((moved, cells))
        for i, field in zip(shifts, moved):
            arrived[i] = along(field, MEMBER, i) if i else field
    return unpacked(place, arrived).reshape(members, rows, columns)


def solution(mesh):
    x = 4
    finer = Mesh(
        mesh.devices.reshape(4, 2, -1, x), ("member_0", "member_1", "space_0", "space_1")
    )
    placed = (
        P(MEMBER, SPACE, None),
        P(SPACE),
        P(SPACE),
        P(SPACE),
        P(SPACE, None),
        P(SPACE, None),
        P(SPACE, None),
        P(),
    )
    return jax.shard_map(
        on_device, mesh=finer, in_specs=placed, out_specs=P(MEMBER, SPACE, None), check_vma=False
    )
```

```python
import functools

import jax
import jax.numpy as jnp
from jax import lax
from jax.experimental import pallas as pl
from jax.experimental.pallas import tpu as pltpu
from jax.sharding import Mesh
from jax.sharding import PartitionSpec as P

NS_ITERS = 12
DAMPING = 0.3
MEMBER = ("member_0", "member_1")
SPACE = ("space_0", "space_1")
HIGHEST = lax.Precision.HIGHEST
F32 = jnp.float32

OWNERS = 8
HELD = 32
ROWS = 16
LANES = 128
MEMBERS = OWNERS * HELD
EDGE = ROWS
SENT_ROWS = ROWS + 1
OUTER = 36
OWN = 72


def shape(*dims, dtype=F32):
    return jax.ShapeDtypeStruct(dims, dtype)


def whole(count):
    return [pl.BlockSpec(memory_space=pltpu.VMEM)] * count


def params(mib):
    return pltpu.CompilerParams(vmem_limit_bytes=mib * 2**20)


SCALARS = pl.BlockSpec(memory_space=pltpu.SMEM)


def lane_ids(rows=8):
    return lax.broadcasted_iota(jnp.int32, (rows, LANES), 1)


def turned(array, amount):
    return pltpu.roll(array, amount % LANES, 1)


def dot(a, b, dims=((1,), (0,))):
    return lax.dot_general(a, b, (dims, ((), ())), precision=HIGHEST, preferred_element_type=F32)


def observe_kernel(index_ref, state_ref, seen_ref):
    values = state_ref[...]
    high = values.astype(jnp.bfloat16)
    rest = values - high.astype(F32)
    middle = rest.astype(jnp.bfloat16)
    low = (rest - middle.astype(F32)).astype(jnp.bfloat16)
    width = values.shape[1]
    step = 256
    for first in range(0, index_ref.shape[1], step):
        cell = index_ref[:, first : first + step]
        row = cell // width
        column = cell - row * width
        places = lax.broadcasted_iota(jnp.int32, (width, step), 0)
        chosen = (places == column).astype(F32).astype(jnp.bfloat16)
        picked = jnp.dot(low, chosen, preferred_element_type=F32)
        picked += jnp.dot(middle, chosen, preferred_element_type=F32)
        picked += jnp.dot(high, chosen, preferred_element_type=F32)
        picked = picked.reshape(HELD, ROWS, step)
        rows = lax.broadcasted_iota(jnp.int32, (ROWS, step), 0)
        seen = jnp.sum(jnp.where((rows == row)[None], picked, 0.0), axis=1)
        for copy in range(seen_ref.shape[0]):
            seen_ref[copy, :, first : first + step] = seen


def observed(state, obs_index, copies):
    return pl.pallas_call(
        observe_kernel,
        out_shape=shape(copies, HELD, obs_index.shape[1]),
        in_specs=whole(2),
        out_specs=whole(1)[0],
        compiler_params=params(20),
        name="observe",
    )(obs_index, state)


ORDER = (0, 1, EDGE, ROWS - 2, ROWS - 1) + tuple(range(2, ROWS - 2))
PLACE = {unit: at for at, unit in enumerate(ORDER)}


def pack_kernel(place_ref, state_ref, after_ref, *refs):
    own = place_ref[0]
    sent_refs, column_ref = refs[:OWNERS], refs[OWNERS]
    lane = lane_ids()
    even = lane % 2 == 0
    near_left = (lane < OUTER) & even
    near_right = (lane < OUTER) & ~even
    far_left = (lane >= OUTER) & (lane < OUTER + 2 * ROWS) & even
    far_right = (lane >= OUTER + 3) & (lane < OUTER + 3 + 2 * ROWS) & ~even
    own_lanes = (lane >= OWN) & (lane < OWN + 2 * ROWS + 4)

    def one_group(group, carry):
        near, far = [], []
        members = pl.ds(pl.multiple_of(group * 8, 8), 8)
        lines = pl.ds(pl.multiple_of(group * 8 * ROWS, 8 * ROWS), 8 * ROWS)
        for slot in range(OWNERS):
            block = lax.rem(own - slot + OWNERS, OWNERS)
            packed_near = jnp.zeros((8, LANES), F32)
            packed_far = jnp.zeros((8, LANES), F32)
            start = pl.multiple_of(block * LANES, LANES)
            column_ref[slot] = state_ref[lines, pl.ds(start, LANES)]
            for r in range(ROWS):
                value = column_ref[slot, pl.ds(r, 8, stride=ROWS), :]
                sent_refs[slot][PLACE[r], members] = value
                at = 2 * (r + 1)
                packed_near = jnp.where(
                    (lane == at) | (lane == at + 1), turned(value, at + 1), packed_near
                )
                at = OUTER + 2 * r
                packed_far = jnp.where(
                    (lane == at) | (lane == at + 3), turned(value, at + 2), packed_far
                )
            near.append(packed_near)
            far.append(packed_far)
        for slot in range(OWNERS):
            block = lax.rem(own - slot + OWNERS, OWNERS)
            left, right = (slot + 1) % OWNERS, (slot - 1) % OWNERS
            has_left = (block > 0).astype(F32)
            has_right = (block < OWNERS - 1).astype(F32)
            edge = jnp.where(own_lanes, turned(near[slot], OWN), 0.0)
            edge = jnp.where(near_left, near[left] * has_left, edge)
            edge = jnp.where(far_left, far[left] * has_left, edge)
            edge = jnp.where(near_right, near[right] * has_right, edge)
            edge = jnp.where(far_right, far[right] * has_right, edge)
            sent_refs[slot][PLACE[EDGE], members] = edge
        return carry

    lax.fori_loop(0, HELD // 8, one_group, 0)


def packed_blocks(place, state, after):
    return pl.pallas_call(
        pack_kernel,
        out_shape=[shape(SENT_ROWS, HELD, LANES)] * OWNERS,
        in_specs=[SCALARS] + whole(1) + [pl.BlockSpec(memory_space=pl.ANY)],
        out_specs=whole(OWNERS),
        scratch_shapes=[pltpu.VMEM((OWNERS, 8 * ROWS, LANES), F32)],
        compiler_params=params(8),
        name="pack",
    )(place, state, after)


BORDER = OWNERS * 3 * HELD
FIELD_LINES = 3 * 2 * OWNERS


def border_kernel(*refs):
    pieces, fields = refs[:OWNERS], refs[OWNERS : OWNERS + 3]
    down_ref, up_ref = refs[OWNERS + 3 :]
    size = 3 * HELD
    for i, piece in enumerate(pieces):
        down_ref[i * size : (i + 1) * size] = piece[0:3].reshape(size, LANES)
        up_ref[i * size : (i + 1) * size] = piece[2:5].reshape(size, LANES)
    for which, ref in enumerate(fields):
        for block in range(OWNERS):
            at = BORDER + (which * OWNERS + block) * 2
            lanes = slice(block * LANES, (block + 1) * LANES)
            down_ref[at : at + 2] = ref[0:2, lanes]
            up_ref[at : at + 2] = ref[ROWS - 2 : ROWS, lanes]


def borders(pieces, fields):
    size = BORDER + FIELD_LINES
    return pl.pallas_call(
        border_kernel,
        grid=(1,),
        out_shape=[shape(size, LANES)] * 2,
        in_specs=[pl.BlockSpec((5, HELD, LANES), lambda g: (0, 0, 0))] * OWNERS
        + [pl.BlockSpec((ROWS, OWNERS * LANES), lambda g: (0, 0))] * 3,
        out_specs=[pl.BlockSpec((size, LANES), lambda g: (0, 0))] * 2,
        compiler_params=params(6),
        name="borders",
    )(*pieces, *fields)


def gram_kernel(place_ref, same_ref, other_ref, value_ref, scale_ref, out_ref):
    own = place_ref[0]
    total = jnp.sum(same_ref[...], axis=(0, 1)) + jnp.sum(other_ref[...], axis=(0, 1))
    mean = (total / MEMBERS)[None]
    scale = scale_ref[...]
    weight = scale / jnp.sqrt(F32(MEMBERS - 1))
    blocks = []
    for k in range(5):
        at = lax.rem(own + k, OWNERS) // 2
        block = same_ref[at] if k % 2 == 0 else other_ref[at]
        blocks.append((block - mean) * weight)
    innovation = scale * (value_ref[...] - mean)
    left = jnp.concatenate([blocks[0], jnp.broadcast_to(innovation, (8, mean.shape[1]))], axis=0)
    main = dot(left, jnp.concatenate(blocks[:4], axis=0), ((1,), (1,)))
    last = jnp.concatenate([blocks[4], jnp.zeros((96, mean.shape[1]), F32)], axis=0)
    opposite = dot(blocks[0], last, ((1,), (1,)))
    packed = opposite[0:8]
    for g in range(1, 4):
        packed += turned(opposite[8 * g : 8 * g + 8], HELD * g)
    for copy in range(out_ref.shape[0]):
        out_ref[copy, 0:40] = main
        out_ref[copy, 40:48] = packed


def gram_blocks(place, same, other, value, scale, copies):
    return pl.pallas_call(
        gram_kernel,
        out_shape=shape(copies, 48, LANES),
        in_specs=[SCALARS] + whole(4),
        out_specs=whole(1)[0],
        compiler_params=params(8),
        cost_estimate=pl.CostEstimate(flops=10**10, bytes_accessed=10**6, transcendentals=0),
        name="gram",
    )(place, same, other, value, scale)


def thirds(array):
    high = array.astype(jnp.bfloat16)
    rest = array - high.astype(F32)
    middle = rest.astype(jnp.bfloat16)
    return high, middle, (rest - middle.astype(F32)).astype(jnp.bfloat16)


def six_products(a, b):
    def product(i, j):
        return jnp.dot(a[i], b[j], preferred_element_type=F32)

    small = product(0, 2) + product(2, 0) + product(1, 1)
    return (small + (product(0, 1) + product(1, 0))) + product(0, 0)


def three_products(a, b):
    def product(i, j):
        return jnp.dot(a[i], b[j], preferred_element_type=F32)

    return (product(0, 1) + product(1, 0)) + product(0, 0)


def root_kernel(place_ref, parts_ref, out_ref, half_ref):
    own = place_ref[0]
    lane = lane_ids()
    drive_row = jnp.zeros((8, MEMBERS), F32)
    nothing = jnp.zeros((8, LANES), F32)
    for i in range(OWNERS):
        at = lax.rem(own + i, OWNERS)
        for g in range(4):
            rows = parts_ref[at, 8 * g : 8 * g + 8]
            rows = jnp.where(lane < HELD, 0.5 * rows, rows)
            fifth = turned(parts_ref[at, 40:48], -HELD * g)
            fifth = jnp.where(lane < HELD, 0.5 * fifth, 0.0)
            line = jnp.concatenate([rows, fifth], axis=1)
            half_ref[i * HELD + 8 * g : i * HELD + 8 * g + 8] = pltpu.roll(line, HELD * i, 1)
        drive = jnp.where(lane < HELD, parts_ref[at, 32:40], 0.0)
        line = jnp.concatenate([drive, nothing], axis=1)
        drive_row += pltpu.roll(line, HELD * i, 1)
    half = half_ref[...]
    rows = lax.broadcasted_iota(jnp.int32, (MEMBERS, MEMBERS), 0)
    columns = lax.broadcasted_iota(jnp.int32, (MEMBERS, MEMBERS), 1)
    identity = (rows == columns).astype(F32)
    big = identity + (half + half.T)
    norm = jnp.sqrt(jnp.sum(big * big))
    upper = big / norm
    middle = 1.5 * identity - 0.5 * upper
    middle_parts = thirds(middle)
    upper = six_products(thirds(upper), middle_parts)
    lower = middle
    lower_parts = middle_parts
    for _ in range(NS_ITERS - 2):
        upper_parts = thirds(upper)
        middle_parts = thirds(1.5 * identity - 0.5 * three_products(lower_parts, upper_parts))
        upper = six_products(upper_parts, middle_parts)
        lower = six_products(middle_parts, lower_parts)
        lower_parts = thirds(lower)
    middle = 1.5 * identity - 0.5 * three_products(lower_parts, thirds(upper))
    root = six_products(thirds(middle), lower_parts) / jnp.sqrt(norm)
    weights = dot(dot(drive_row, root, ((1,), (1,))), root, ((1,), (1,)))
    out_ref[...] = root + weights[0:1] / jnp.sqrt(F32(MEMBERS - 1))


def transform_of(place, parts):
    return pl.pallas_call(
        root_kernel,
        out_shape=shape(MEMBERS, MEMBERS),
        in_specs=[SCALARS] + whole(1),
        out_specs=whole(1)[0],
        scratch_shapes=[pltpu.VMEM((MEMBERS, MEMBERS), F32)],
        compiler_params=params(12),
        cost_estimate=pl.CostEstimate(flops=10**10, bytes_accessed=10**6, transcendentals=0),
        name="root",
    )(place, parts)


FIELD_ROWS = 20
NEAR_K, INNER_K, OUTER_K, NEAR_S, NEAR_R, NEAR_MASK = range(6)


def spread_fields(place_ref, ksat_ref, storage_ref, recharge_ref, above_ref, below_ref, out_ref, edge_ref):
    own = place_ref[0]
    lane = lane_ids(1)
    even = lane % 2 == 0
    left_block = jnp.maximum(own - 1, 0)
    right_block = jnp.minimum(own + 1, OWNERS - 1)
    has_left = own > 0
    has_right = own < OWNERS - 1
    packed = [jnp.zeros((1, LANES), F32) for _ in range(5)]
    for which, ref in enumerate((ksat_ref, storage_ref, recharge_ref)):
        for place in range(FIELD_ROWS):
            r = place - 2

            def row_of(block):
                line = BORDER + (which * OWNERS + block) * 2
                if r < 0:
                    return above_ref[pl.ds(line + r + 2, 1)]
                if r >= ROWS:
                    return below_ref[pl.ds(line + r - ROWS, 1)]
                return ref[r : r + 1, pl.ds(pl.multiple_of(block * LANES, LANES), LANES)]

            mine = row_of(own)
            out_ref[which, place] = jnp.broadcast_to(mine, (8, LANES))
            if r < -1 or r > ROWS:
                if which == 0:
                    out_ref[3, place] = jnp.zeros((8, LANES), F32)
                    out_ref[4, place] = jnp.zeros((8, LANES), F32)
                continue
            at = 2 * (r + 1)
            here = (lane == at) | (lane == at + 1)
            left = jnp.where(has_left, row_of(left_block), 0.0)
            right = jnp.where(has_right, row_of(right_block), 0.0)
            near = jnp.where(lane < LANES // 2, right, left)
            near = turned(near, at + 1)
            if which == 0:
                out_ref[3, place] = jnp.broadcast_to(turned(mine, 1), (8, LANES))
                beyond = jnp.where(lane == 0, turned(left, 1), turned(right, -1))
                out_ref[4, place] = jnp.broadcast_to(beyond, (8, LANES))
                inner = jnp.where(even, turned(mine, at), turned(mine, at + 2))
                outer = jnp.where(even, turned(left, at + 2), turned(right, at))
                packed[NEAR_K] = jnp.where(here, near, packed[NEAR_K])
                packed[INNER_K] = jnp.where(here, inner, packed[INNER_K])
                packed[OUTER_K] = jnp.where(here, outer, packed[OUTER_K])
            elif which == 1:
                packed[NEAR_S] = jnp.where(here, near, packed[NEAR_S])
            else:
                packed[NEAR_R] = jnp.where(here, near, packed[NEAR_R])
    for n in range(5):
        edge_ref[n] = jnp.broadcast_to(packed[n], (8, LANES))
    lane = lane_ids()
    keep = jnp.where(lane % 2 == 0, has_left.astype(F32), has_right.astype(F32))
    edge_ref[NEAR_MASK] = jnp.where((lane >= 2) & (lane < 2 * ROWS + 2), keep, 0.0)


UNITS = ROWS + 5


def halves(array):
    high = array.astype(jnp.bfloat16)
    return high, (array - high.astype(F32)).astype(jnp.bfloat16)


def analyse_kernel(*refs):
    place_ref, ksat_ref, storage_ref, recharge_ref, transform_ref = refs[:5]
    piece_refs = refs[5 : 5 + OWNERS]
    above_ref, below_ref, field_ref, edge_field_ref = refs[5 + OWNERS : 9 + OWNERS]
    out_refs = refs[9 + OWNERS :]
    spread_fields(
        place_ref, ksat_ref, storage_ref, recharge_ref, above_ref, below_ref, field_ref, edge_field_ref
    )
    high, low = halves(transform_ref[...])
    lane = lax.broadcasted_iota(jnp.int32, (MEMBERS, LANES), 1)

    def joined(find):
        return jnp.concatenate([find(i) for i in range(OWNERS)], axis=0)

    def border(ref, n):
        return joined(lambda i: ref[(i * 3 + n) * HELD : (i * 3 + n + 1) * HELD])

    def cells(unit):
        if unit > SENT_ROWS + 1:
            return border(below_ref, unit - SENT_ROWS - 2)
        if unit >= SENT_ROWS:
            return border(above_ref, unit - SENT_ROWS + 1)
        found = joined(lambda i: piece_refs[i][PLACE[unit]])
        if unit == EDGE:
            top = border(above_ref, 0)
            bottom = border(below_ref, 2)
            first = (lane < 2) | ((lane >= OWN) & (lane < OWN + 2))
            last = 2 * ROWS + 2
            final = ((lane >= last) & (lane < last + 2)) | (
                (lane >= OWN + last) & (lane < OWN + last + 2)
            )
            found = jnp.where(first, turned(top, -2 * ROWS), found)
            found = jnp.where(final, turned(bottom, 2 * ROWS), found)
        return found

    def product(a, b):
        return jnp.dot(a, b, preferred_element_type=F32)

    for first in range(0, UNITS, 2):
        units = range(first, min(first + 2, UNITS))
        found = [cells(u) for u in units]
        state = found[0] if len(found) == 1 else jnp.concatenate(found, axis=1)
        mean = jnp.sum(state, axis=0, keepdims=True) / MEMBERS
        large, small = halves(state - mean)
        result = product(low, large) + product(high, small) + product(high, large) + mean
        for at, unit in enumerate(units):
            for i in range(OWNERS):
                out_refs[i][unit] = result[
                    i * HELD : (i + 1) * HELD, at * LANES : (at + 1) * LANES
                ]


def analysed(place, cell_fields, transform, pieces, above, below):
    found = pl.pallas_call(
        analyse_kernel,
        out_shape=[shape(5, FIELD_ROWS, 8, LANES), shape(6, 8, LANES)]
        + [shape(UNITS, HELD, LANES)] * OWNERS,
        in_specs=[SCALARS] + whole(6 + OWNERS),
        out_specs=whole(2 + OWNERS),
        compiler_params=params(14),
        name="analyse",
    )(place, *cell_fields, transform, *pieces, above, below)
    return found[0], found[1], found[2:]


def logistic(x):
    return 0.5 * jnp.tanh(0.5 * x) + 0.5


BATCH = 16


def forecast_kernel(shifts, place_ref, counts_ref, wide_ref, field_ref, edge_field_ref, *refs):
    cells_refs, out_refs = refs[: len(shifts)], refs[len(shifts) : 2 * len(shifts)]
    iterate, goal, edge_row = refs[2 * len(shifts) :]
    own = place_ref[0]
    has_above = place_ref[1].astype(F32)
    has_below = place_ref[2].astype(F32)
    lane = lane_ids()
    even = lane % 2 == 0
    first_lane = lane == 0
    ends = first_lane | (lane == LANES - 1)
    sat, store, rain, left, ghosts = range(5)
    tiles = BATCH // 8

    def rolled(array, amount):
        return pltpu.roll(array, amount % LANES, 2)

    def face(level, other, cond, other_cond):
        return 0.5 * (cond + other_cond) * (other - level)

    def swapped(packed):
        return jnp.where(even, rolled(packed, -1), rolled(packed, 1))

    def one_batch(which, batch, carry):
        cells_ref, out_ref = cells_refs[which], out_refs[which]
        owner = lax.rem(own + shifts[which], OWNERS)
        first_member = owner * HELD + batch * BATCH
        most = counts_ref[first_member]
        for n in range(1, BATCH):
            most = jnp.maximum(most, counts_ref[first_member + n])
        counts = wide_ref[pl.ds(pl.multiple_of(first_member, BATCH), BATCH)]
        counts = counts.reshape(tiles, 8, LANES)
        members = pl.ds(pl.multiple_of(batch * BATCH, BATCH), BATCH)

        def begun(level, flux, storage):
            bend = jnp.tanh(level)
            held = storage * bend
            return level + DAMPING * flux / (1.0 + storage * (1.0 - bend * bend)), level + held + flux

        def swept(value, target, storage, sweep):
            bend = jnp.tanh(value)
            derivative = 1.0 + storage * (1.0 - bend * bend)
            moved = value - DAMPING * (value + storage * bend - target) / derivative
            return jnp.where(counts > sweep, moved, value)

        def unit_at(unit):
            return cells_ref[unit, members].reshape(tiles, 8, LANES)

        def cell_at(r):
            if r < 0:
                return unit_at(SENT_ROWS + r + 2)
            if r >= ROWS:
                return unit_at(SENT_ROWS + 2 + r - ROWS)
            return unit_at(r)

        packed = unit_at(EDGE)
        near = jnp.where(lane < OUTER, packed, 0.0)
        inner = jnp.where(even, rolled(packed, -OWN - 1), rolled(packed, -OWN + 1))
        outer = jnp.where(even, rolled(packed, 2 - OUTER), rolled(packed, -OUTER))
        near_k = edge_field_ref[NEAR_K] * logistic(near)
        inner_k = edge_field_ref[INNER_K] * logistic(inner)
        outer_k = edge_field_ref[OUTER_K] * logistic(outer)
        inward = face(near, inner, near_k, inner_k)
        side = swapped(inward)
        flux = inward + face(near, outer, near_k, outer_k)
        flux += face(near, rolled(near, 2), near_k, rolled(near_k, 2))
        flux += face(near, rolled(near, -2), near_k, rolled(near_k, -2))
        flux += edge_field_ref[NEAR_R]
        value, target = begun(near, flux, edge_field_ref[NEAR_S])
        edge_row[0] = value
        edge_row[1] = target

        def conduct(level, r):
            return field_ref[sat, r + 2] * logistic(level)

        level, cond = cell_at(-1), conduct(cell_at(-1), -1)
        above = face(cell_at(-2), level, conduct(cell_at(-2), -2), cond)
        for r in range(-1, ROWS + 1):
            lower_level = cell_at(r + 1)
            lower_cond = conduct(lower_level, r + 1)
            under = face(level, lower_level, cond, lower_cond)
            beside = rolled(level, 1)
            across = face(beside, level, field_ref[left, r + 2] * logistic(beside), cond)
            across = jnp.where(first_lane, 0.0, across)
            flux = under - above + (rolled(across, -1) - across)
            flux -= jnp.where(ends, rolled(side, -2 * (r + 1) - 1), 0.0)
            flux += field_ref[rain, r + 2]
            iterate[r + 1], goal[r + 1] = begun(level, flux, field_ref[store, r + 2])
            level, cond, above = lower_level, lower_cond, under

        def first_sweep(sweep, carry):
            for n in range(ROWS + 2):
                iterate[n] = swept(iterate[n], goal[n], field_ref[store, n + 1], sweep)
            edge_row[0] = swept(edge_row[0], edge_row[1], edge_field_ref[NEAR_S], sweep)
            return carry

        lax.fori_loop(1, most, first_sweep, 0)

        near = edge_row[0] * edge_field_ref[NEAR_MASK]
        side = swapped(near)
        level = iterate[1]
        cond = conduct(level, 0)
        before = iterate[0] * has_above
        above = face(before, level, conduct(before, -1), cond)
        for r in range(ROWS):
            lower_level = iterate[r + 2]
            if r == ROWS - 1:
                lower_level = lower_level * has_below
            lower_cond = conduct(lower_level, r + 1)
            under = face(level, lower_level, cond, lower_cond)
            beside = rolled(level, 1)
            across = face(beside, level, field_ref[left, r + 2] * logistic(beside), cond)
            across = jnp.where(first_lane, 0.0, across)
            flux = under - above + (rolled(across, -1) - across)
            ghost = rolled(side, -2 * (r + 1) - 1)
            entering = face(level, ghost, cond, field_ref[ghosts, r + 2] * logistic(ghost))
            flux += jnp.where(ends, entering, 0.0)
            flux += field_ref[rain, r + 2]
            iterate[r + 1], goal[r + 1] = begun(level, flux, field_ref[store, r + 2])
            level, cond, above = lower_level, lower_cond, under

        def second_sweep(sweep, carry):
            for n in range(1, ROWS + 1):
                iterate[n] = swept(iterate[n], goal[n], field_ref[store, n + 1], sweep)
            return carry

        lax.fori_loop(1, most, second_sweep, 0)
        for r in range(ROWS):
            for tile in range(tiles):
                start = (batch * BATCH + tile * 8) * ROWS + r
                out_ref[pl.ds(start, 8, stride=ROWS), :] = iterate[r + 1, tile]
        return carry

    for which in range(len(shifts)):
        lax.fori_loop(0, HELD // BATCH, functools.partial(one_batch, which), 0)


def forecasts(shifts, place, counts, wide_counts, fields, edge_fields, cells):
    many = len(shifts)
    return pl.pallas_call(
        functools.partial(forecast_kernel, shifts),
        out_shape=[shape(HELD * ROWS, LANES)] * many,
        in_specs=[SCALARS, SCALARS] + whole(3 + many),
        out_specs=whole(many),
        scratch_shapes=[
            pltpu.VMEM((ROWS + 2, BATCH // 8, 8, LANES), F32),
            pltpu.VMEM((ROWS + 2, BATCH // 8, 8, LANES), F32),
            pltpu.VMEM((2, BATCH // 8, 8, LANES), F32),
        ],
        compiler_params=params(6),
        cost_estimate=pl.CostEstimate(flops=1, bytes_accessed=1, transcendentals=0),
        name="forecast",
    )(place, counts, wide_counts, fields, edge_fields, *cells)


def unpack_kernel(many, place_ref, *refs):
    out_ref = refs[-1]
    step = pl.program_id(0)
    for n in range(many):

        @pl.when(step == n)
        def _():
            out_ref[...] = refs[n][...]


def unpacked(place, shifts, pieces, begun=None):
    many = len(shifts)

    def column(step, place_ref):
        block = jnp.int32(0)
        for n, shift in enumerate(shifts):
            own = place_ref[0] - shift + OWNERS
            block = jnp.where(step == n, lax.rem(own, OWNERS), block)
        return 0, block

    extra = [] if begun is None else [begun]
    return pl.pallas_call(
        functools.partial(unpack_kernel, many),
        grid_spec=pltpu.PrefetchScalarGridSpec(
            num_scalar_prefetch=1,
            grid=(many,),
            in_specs=whole(many) + [pl.BlockSpec(memory_space=pl.ANY)] * len(extra),
            out_specs=pl.BlockSpec((HELD * ROWS, LANES), column),
        ),
        out_shape=shape(HELD * ROWS, OWNERS * LANES),
        input_output_aliases={1 + many: 0} if extra else {},
        compiler_params=params(6),
        name="unpack",
    )(place, *pieces, *extra)


def exchanged(copies, axis):
    return lax.all_to_all(copies, axis, split_axis=0, concat_axis=0, tiled=True)


def shared(array, axis):
    return exchanged(jnp.broadcast_to(array, (lax.axis_size(axis), *array.shape)), axis)


def along(array, axis, step):
    peers = lax.axis_size(axis)
    return lax.ppermute(array, axis, [(i, (i + step) % peers) for i in range(peers)])


def to_strips_beside(array, step):
    peers = lax.axis_size(SPACE)
    pairs = [(i, i + step) for i in range(peers) if 0 <= i + step < peers]
    return lax.ppermute(array, SPACE, pairs)


def on_device(state, obs_index, obs_value, obs_scale, ksat, storage, recharge, newton_counts):
    members, rows, columns = state.shape
    flat = state.reshape(members * rows, columns)
    own = lax.axis_index(MEMBER)
    strip = lax.axis_index(SPACE)
    place = jnp.stack(
        [own, (strip > 0).astype(jnp.int32), (strip < lax.axis_size(SPACE) - 1).astype(jnp.int32)]
    ).astype(jnp.int32)

    seen = observed(flat, obs_index[None], lax.axis_size(MEMBER[0]))
    same = exchanged(seen, MEMBER[0])

    blocks = packed_blocks(place, flat, seen)
    wide_counts = jnp.broadcast_to(newton_counts[:, None], (MEMBERS, LANES))
    same, blocks, wide_counts = lax.optimization_barrier((same, blocks, wide_counts))
    other = along(same, MEMBER[1], 1)

    pieces = [blocks[0]] + [None] * (OWNERS - 1)
    for i in (2, 6, 3, 5):
        pieces[i] = along(blocks[i], MEMBER, -i)
    copies = lax.axis_size(SPACE[0])
    part = gram_blocks(place, same, other, obs_value[None], obs_scale[None], copies)
    part, blocks = lax.optimization_barrier((part, blocks))
    for i in (4, 1, 7):
        pieces[i] = along(blocks[i], MEMBER, -i)
    part = jnp.sum(exchanged(part, SPACE[0]), axis=0)
    part = jnp.sum(shared(part, SPACE[1]), axis=0)
    parts = shared(part, MEMBER)
    cell_fields = (ksat, storage, recharge)
    down, up = borders(pieces, cell_fields)
    parts, down, up = lax.optimization_barrier((parts, down, up))
    above = to_strips_beside(up, 1)
    below = to_strips_beside(down, -1)
    transform = transform_of(place, parts)
    fields, edge_fields, cells = analysed(place, cell_fields, transform, pieces, above, below)

    arrived = [None] * OWNERS
    for shifts in ((2,), (6,), (3, 5), (4, 1), (7, 0)):
        moved = forecasts(
            shifts, place, newton_counts, wide_counts, fields, edge_fields, [cells[i] for i in shifts]
        )
        moved, cells = lax.optimization_barrier((moved, cells))
        for i, field in zip(shifts, moved):
            arrived[i] = along(field, MEMBER, i) if i else field
    early, late = (0, 2, 6, 3, 5), (4, 1, 7)
    result = unpacked(place, early, [arrived[i] for i in early])
    result = unpacked(place, late, [arrived[i] for i in late], result)
    return result.reshape(members, rows, columns)


def solution(mesh):
    x = 4
    finer = Mesh(
        mesh.devices.reshape(4, 2, -1, x), ("member_0", "member_1", "space_0", "space_1")
    )
    placed = (
        P(MEMBER, SPACE, None),
        P(SPACE),
        P(SPACE),
        P(SPACE),
        P(SPACE, None),
        P(SPACE, None),
        P(SPACE, None),
        P(),
    )
    return jax.shard_map(
        on_device, mesh=finer, in_specs=placed, out_specs=P(MEMBER, SPACE, None), check_vma=False
    )
```

```python
import functools

import jax
import jax.numpy as jnp
from jax import lax
from jax.experimental import pallas as pl
from jax.experimental.pallas import tpu as pltpu
from jax.sharding import Mesh
from jax.sharding import PartitionSpec as P

NS_ITERS = 12
DAMPING = 0.3
MEMBER = ("member_0", "member_1")
SPACE = ("space_0", "space_1")
HIGHEST = lax.Precision.HIGHEST
F32 = jnp.float32

OWNERS = 8
HELD = 32
ROWS = 16
LANES = 128
MEMBERS = OWNERS * HELD
EDGE = ROWS
SENT_ROWS = ROWS + 1
OUTER = 36
OWN = 72


def shape(*dims, dtype=F32):
    return jax.ShapeDtypeStruct(dims, dtype)


def whole(count):
    return [pl.BlockSpec(memory_space=pltpu.VMEM)] * count


def params(mib):
    return pltpu.CompilerParams(vmem_limit_bytes=mib * 2**20)


SCALARS = pl.BlockSpec(memory_space=pltpu.SMEM)


def relative(own, place, sign=1):
    chip, core = lax.div(own, 2), lax.rem(own, 2)
    chips = OWNERS // 2
    other = lax.rem(chip + sign * (place // 2) + chips, chips)
    return 2 * other + (1 - core if place % 2 else core)


def lane_ids(rows=8):
    return lax.broadcasted_iota(jnp.int32, (rows, LANES), 1)


def turned(array, amount):
    return pltpu.roll(array, amount % LANES, 1)


def dot(a, b, dims=((1,), (0,))):
    return lax.dot_general(a, b, (dims, ((), ())), precision=HIGHEST, preferred_element_type=F32)


def observe_kernel(index_ref, state_ref, seen_ref):
    values = state_ref[...]
    high = values.astype(jnp.bfloat16)
    rest = values - high.astype(F32)
    middle = rest.astype(jnp.bfloat16)
    low = (rest - middle.astype(F32)).astype(jnp.bfloat16)
    width = values.shape[1]
    step = 256
    for first in range(0, index_ref.shape[1], step):
        cell = index_ref[:, first : first + step]
        row = cell // width
        column = cell - row * width
        places = lax.broadcasted_iota(jnp.int32, (width, step), 0)
        chosen = (places == column).astype(F32).astype(jnp.bfloat16)
        picked = jnp.dot(low, chosen, preferred_element_type=F32)
        picked += jnp.dot(middle, chosen, preferred_element_type=F32)
        picked += jnp.dot(high, chosen, preferred_element_type=F32)
        picked = picked.reshape(HELD, ROWS, step)
        rows = lax.broadcasted_iota(jnp.int32, (ROWS, step), 0)
        seen = jnp.sum(jnp.where((rows == row)[None], picked, 0.0), axis=1)
        for copy in range(seen_ref.shape[0]):
            seen_ref[copy, :, first : first + step] = seen


def observed(state, obs_index, copies):
    return pl.pallas_call(
        observe_kernel,
        out_shape=shape(copies, HELD, obs_index.shape[1]),
        in_specs=whole(2),
        out_specs=whole(1)[0],
        compiler_params=params(20),
        name="observe",
    )(obs_index, state)


ORDER = (0, 1, EDGE, ROWS - 2, ROWS - 1) + tuple(range(2, ROWS - 2))
PLACE = {unit: at for at, unit in enumerate(ORDER)}


def pack_kernel(place_ref, state_ref, after_ref, *refs):
    own = place_ref[0]
    sent_refs, column_ref = refs[:2], refs[2]
    lane = lane_ids()
    even = lane % 2 == 0
    near_left = (lane < OUTER) & even
    near_right = (lane < OUTER) & ~even
    far_left = (lane >= OUTER) & (lane < OUTER + 2 * ROWS) & even
    far_right = (lane >= OUTER + 3) & (lane < OUTER + 3 + 2 * ROWS) & ~even
    own_lanes = (lane >= OWN) & (lane < OWN + 2 * ROWS + 4)

    def one_group(group, carry):
        near, far = [], []
        members = pl.ds(pl.multiple_of(group * 8, 8), 8)
        lines = pl.ds(pl.multiple_of(group * 8 * ROWS, 8 * ROWS), 8 * ROWS)
        for slot in range(OWNERS):
            block = relative(own, slot, -1)
            packed_near = jnp.zeros((8, LANES), F32)
            packed_far = jnp.zeros((8, LANES), F32)
            start = pl.multiple_of(block * LANES, LANES)
            column_ref[slot] = state_ref[lines, pl.ds(start, LANES)]
            for r in range(ROWS):
                value = column_ref[slot, pl.ds(r, 8, stride=ROWS), :]
                sent_refs[slot % 2][slot // 2, PLACE[r], members] = value
                at = 2 * (r + 1)
                packed_near = jnp.where(
                    (lane == at) | (lane == at + 1), turned(value, at + 1), packed_near
                )
                at = OUTER + 2 * r
                packed_far = jnp.where(
                    (lane == at) | (lane == at + 3), turned(value, at + 2), packed_far
                )
            near.append(packed_near)
            far.append(packed_far)
        for slot in range(OWNERS):
            block = relative(own, slot, -1)
            odd = lax.rem(block, 2) == 1
            beside, further = slot ^ 1, ((slot ^ 1) + 2) % OWNERS
            nearer = ((slot ^ 1) - 2) % OWNERS
            has_left = (block > 0).astype(F32)
            has_right = (block < OWNERS - 1).astype(F32)

            def left(packed):
                return jnp.where(odd, packed[beside], packed[further]) * has_left

            def right(packed):
                return jnp.where(odd, packed[nearer], packed[beside]) * has_right

            edge = jnp.where(own_lanes, turned(near[slot], OWN), 0.0)
            edge = jnp.where(near_left, left(near), edge)
            edge = jnp.where(far_left, left(far), edge)
            edge = jnp.where(near_right, right(near), edge)
            edge = jnp.where(far_right, right(far), edge)
            sent_refs[slot % 2][slot // 2, PLACE[EDGE], members] = edge
        return carry

    lax.fori_loop(0, HELD // 8, one_group, 0)


def packed_blocks(place, state, after):
    return pl.pallas_call(
        pack_kernel,
        out_shape=[shape(OWNERS // 2, SENT_ROWS, HELD, LANES)] * 2,
        in_specs=[SCALARS] + whole(1) + [pl.BlockSpec(memory_space=pl.ANY)],
        out_specs=whole(2),
        scratch_shapes=[pltpu.VMEM((OWNERS, 8 * ROWS, LANES), F32)],
        compiler_params=params(8),
        name="pack",
    )(place, state, after)


BORDER = OWNERS * 3 * HELD
FIELD_LINES = 3 * 2 * OWNERS


def border_kernel(*refs):
    chips = OWNERS // 2
    pieces, fields = refs[:chips], refs[chips : chips + 3]
    down_ref, up_ref = refs[chips + 3 :]
    size = 3 * HELD
    for i in range(OWNERS):
        piece = pieces[i // 2]
        down_ref[i * size : (i + 1) * size] = piece[i % 2, 0:3].reshape(size, LANES)
        up_ref[i * size : (i + 1) * size] = piece[i % 2, 2:5].reshape(size, LANES)
    for which, ref in enumerate(fields):
        for block in range(OWNERS):
            at = BORDER + (which * OWNERS + block) * 2
            lanes = slice(block * LANES, (block + 1) * LANES)
            down_ref[at : at + 2] = ref[0:2, lanes]
            up_ref[at : at + 2] = ref[ROWS - 2 : ROWS, lanes]


def borders(pieces, fields):
    size = BORDER + FIELD_LINES
    return pl.pallas_call(
        border_kernel,
        grid=(1,),
        out_shape=[shape(size, LANES)] * 2,
        in_specs=[pl.BlockSpec((2, 5, HELD, LANES), lambda g: (0, 0, 0, 0))] * (OWNERS // 2)
        + [pl.BlockSpec((ROWS, OWNERS * LANES), lambda g: (0, 0))] * 3,
        out_specs=[pl.BlockSpec((size, LANES), lambda g: (0, 0))] * 2,
        compiler_params=params(6),
        name="borders",
    )(*pieces, *fields)


def gram_kernel(place_ref, same_ref, other_ref, value_ref, scale_ref, out_ref):
    own = place_ref[0]
    total = jnp.sum(same_ref[...], axis=(0, 1)) + jnp.sum(other_ref[...], axis=(0, 1))
    mean = (total / MEMBERS)[None]
    scale = scale_ref[...]
    weight = scale / jnp.sqrt(F32(MEMBERS - 1))
    blocks = []
    for k in range(5):
        at = lax.rem(own + k, OWNERS) // 2
        block = same_ref[at] if k % 2 == 0 else other_ref[at]
        blocks.append((block - mean) * weight)
    innovation = scale * (value_ref[...] - mean)
    left = jnp.concatenate([blocks[0], jnp.broadcast_to(innovation, (8, mean.shape[1]))], axis=0)
    main = dot(left, jnp.concatenate(blocks[:4], axis=0), ((1,), (1,)))
    last = jnp.concatenate([blocks[4], jnp.zeros((96, mean.shape[1]), F32)], axis=0)
    opposite = dot(blocks[0], last, ((1,), (1,)))
    packed = opposite[0:8]
    for g in range(1, 4):
        packed += turned(opposite[8 * g : 8 * g + 8], HELD * g)
    for copy in range(out_ref.shape[0]):
        out_ref[copy, 0:40] = main
        out_ref[copy, 40:48] = packed


def gram_blocks(place, same, other, value, scale, copies):
    return pl.pallas_call(
        gram_kernel,
        out_shape=shape(copies, 48, LANES),
        in_specs=[SCALARS] + whole(4),
        out_specs=whole(1)[0],
        compiler_params=params(8),
        cost_estimate=pl.CostEstimate(flops=10**10, bytes_accessed=10**6, transcendentals=0),
        name="gram",
    )(place, same, other, value, scale)


def thirds(array):
    high = array.astype(jnp.bfloat16)
    rest = array - high.astype(F32)
    middle = rest.astype(jnp.bfloat16)
    return high, middle, (rest - middle.astype(F32)).astype(jnp.bfloat16)


def six_products(a, b):
    def product(i, j):
        return jnp.dot(a[i], b[j], preferred_element_type=F32)

    small = product(0, 2) + product(2, 0) + product(1, 1)
    return (small + (product(0, 1) + product(1, 0))) + product(0, 0)


def three_products(a, b):
    def product(i, j):
        return jnp.dot(a[i], b[j], preferred_element_type=F32)

    return (product(0, 1) + product(1, 0)) + product(0, 0)


def root_kernel(place_ref, parts_ref, out_ref, half_ref):
    own = place_ref[0]
    lane = lane_ids()
    drive_row = jnp.zeros((8, MEMBERS), F32)
    nothing = jnp.zeros((8, LANES), F32)
    for i in range(OWNERS):
        for g in range(4):
            rows = parts_ref[i, 8 * g : 8 * g + 8]
            rows = jnp.where(lane < HELD, 0.5 * rows, rows)
            fifth = turned(parts_ref[i, 40:48], -HELD * g)
            fifth = jnp.where(lane < HELD, 0.5 * fifth, 0.0)
            line = jnp.concatenate([rows, fifth], axis=1)
            half_ref[i * HELD + 8 * g : i * HELD + 8 * g + 8] = pltpu.roll(line, HELD * i, 1)
        drive = jnp.where(lane < HELD, parts_ref[relative(own, i), 32:40], 0.0)
        line = jnp.concatenate([drive, nothing], axis=1)
        drive_row += pltpu.roll(line, HELD * i, 1)
    half = half_ref[...]
    rows = lax.broadcasted_iota(jnp.int32, (MEMBERS, MEMBERS), 0)
    columns = lax.broadcasted_iota(jnp.int32, (MEMBERS, MEMBERS), 1)
    identity = (rows == columns).astype(F32)
    big = identity + (half + half.T)
    norm = jnp.sqrt(jnp.sum(big * big))
    upper = big / norm
    middle = 1.5 * identity - 0.5 * upper
    middle_parts = thirds(middle)
    upper = six_products(thirds(upper), middle_parts)
    lower = middle
    lower_parts = middle_parts
    for _ in range(NS_ITERS - 2):
        upper_parts = thirds(upper)
        middle_parts = thirds(1.5 * identity - 0.5 * three_products(lower_parts, upper_parts))
        upper = six_products(upper_parts, middle_parts)
        lower = six_products(middle_parts, lower_parts)
        lower_parts = thirds(lower)
    middle = 1.5 * identity - 0.5 * three_products(lower_parts, thirds(upper))
    root = six_products(thirds(middle), lower_parts) / jnp.sqrt(norm)

    def rows_in_order(matrix):
        half_ref[...] = matrix
        starts = [pl.multiple_of(relative(own, i) * HELD, HELD) for i in range(OWNERS)]
        return jnp.concatenate([half_ref[pl.ds(start, HELD)] for start in starts], axis=0)

    root = rows_in_order(rows_in_order(root).T)
    weights = dot(dot(drive_row, root, ((1,), (1,))), root, ((1,), (1,)))
    out_ref[...] = root + weights[0:1] / jnp.sqrt(F32(MEMBERS - 1))


def transform_of(place, parts):
    return pl.pallas_call(
        root_kernel,
        out_shape=shape(MEMBERS, MEMBERS),
        in_specs=[SCALARS] + whole(1),
        out_specs=whole(1)[0],
        scratch_shapes=[pltpu.VMEM((MEMBERS, MEMBERS), F32)],
        compiler_params=params(12),
        cost_estimate=pl.CostEstimate(flops=10**10, bytes_accessed=10**6, transcendentals=0),
        name="root",
    )(place, parts)


FIELD_ROWS = 20
NEAR_K, INNER_K, OUTER_K, NEAR_S, NEAR_R, NEAR_MASK = range(6)


def spread_fields(place_ref, ksat_ref, storage_ref, recharge_ref, above_ref, below_ref, out_ref, edge_ref):
    own = place_ref[0]
    lane = lane_ids(1)
    even = lane % 2 == 0
    left_block = jnp.maximum(own - 1, 0)
    right_block = jnp.minimum(own + 1, OWNERS - 1)
    has_left = own > 0
    has_right = own < OWNERS - 1
    packed = [jnp.zeros((1, LANES), F32) for _ in range(5)]
    for which, ref in enumerate((ksat_ref, storage_ref, recharge_ref)):
        for place in range(FIELD_ROWS):
            r = place - 2

            def row_of(block):
                line = BORDER + (which * OWNERS + block) * 2
                if r < 0:
                    return above_ref[pl.ds(line + r + 2, 1)]
                if r >= ROWS:
                    return below_ref[pl.ds(line + r - ROWS, 1)]
                return ref[r : r + 1, pl.ds(pl.multiple_of(block * LANES, LANES), LANES)]

            mine = row_of(own)
            out_ref[which, place] = jnp.broadcast_to(mine, (8, LANES))
            if r < -1 or r > ROWS:
                if which == 0:
                    out_ref[3, place] = jnp.zeros((8, LANES), F32)
                    out_ref[4, place] = jnp.zeros((8, LANES), F32)
                continue
            at = 2 * (r + 1)
            here = (lane == at) | (lane == at + 1)
            left = jnp.where(has_left, row_of(left_block), 0.0)
            right = jnp.where(has_right, row_of(right_block), 0.0)
            near = jnp.where(lane < LANES // 2, right, left)
            near = turned(near, at + 1)
            if which == 0:
                out_ref[3, place] = jnp.broadcast_to(turned(mine, 1), (8, LANES))
                beyond = jnp.where(lane == 0, turned(left, 1), turned(right, -1))
                out_ref[4, place] = jnp.broadcast_to(beyond, (8, LANES))
                inner = jnp.where(even, turned(mine, at), turned(mine, at + 2))
                outer = jnp.where(even, turned(left, at + 2), turned(right, at))
                packed[NEAR_K] = jnp.where(here, near, packed[NEAR_K])
                packed[INNER_K] = jnp.where(here, inner, packed[INNER_K])
                packed[OUTER_K] = jnp.where(here, outer, packed[OUTER_K])
            elif which == 1:
                packed[NEAR_S] = jnp.where(here, near, packed[NEAR_S])
            else:
                packed[NEAR_R] = jnp.where(here, near, packed[NEAR_R])
    for n in range(5):
        edge_ref[n] = jnp.broadcast_to(packed[n], (8, LANES))
    lane = lane_ids()
    keep = jnp.where(lane % 2 == 0, has_left.astype(F32), has_right.astype(F32))
    edge_ref[NEAR_MASK] = jnp.where((lane >= 2) & (lane < 2 * ROWS + 2), keep, 0.0)


UNITS = ROWS + 5


def halves(array):
    high = array.astype(jnp.bfloat16)
    return high, (array - high.astype(F32)).astype(jnp.bfloat16)


def analyse_kernel(*refs):
    place_ref, ksat_ref, storage_ref, recharge_ref, transform_ref = refs[:5]
    chips = OWNERS // 2
    piece_refs = refs[5 : 5 + chips]
    above_ref, below_ref, field_ref, edge_field_ref = refs[5 + chips : 9 + chips]
    out_refs = refs[9 + chips :]
    spread_fields(
        place_ref, ksat_ref, storage_ref, recharge_ref, above_ref, below_ref, field_ref, edge_field_ref
    )
    high, low = halves(transform_ref[...])
    lane = lax.broadcasted_iota(jnp.int32, (MEMBERS, LANES), 1)

    def joined(find):
        return jnp.concatenate([find(i) for i in range(OWNERS)], axis=0)

    def border(ref, n):
        return joined(lambda i: ref[(i * 3 + n) * HELD : (i * 3 + n + 1) * HELD])

    def cells(unit):
        if unit > SENT_ROWS + 1:
            return border(below_ref, unit - SENT_ROWS - 2)
        if unit >= SENT_ROWS:
            return border(above_ref, unit - SENT_ROWS + 1)
        found = joined(lambda i: piece_refs[i // 2][i % 2, PLACE[unit]])
        if unit == EDGE:
            top = border(above_ref, 0)
            bottom = border(below_ref, 2)
            first = (lane < 2) | ((lane >= OWN) & (lane < OWN + 2))
            last = 2 * ROWS + 2
            final = ((lane >= last) & (lane < last + 2)) | (
                (lane >= OWN + last) & (lane < OWN + last + 2)
            )
            found = jnp.where(first, turned(top, -2 * ROWS), found)
            found = jnp.where(final, turned(bottom, 2 * ROWS), found)
        return found

    def product(a, b):
        return jnp.dot(a, b, preferred_element_type=F32)

    for first in range(0, UNITS, 2):
        units = range(first, min(first + 2, UNITS))
        found = [cells(u) for u in units]
        state = found[0] if len(found) == 1 else jnp.concatenate(found, axis=1)
        mean = jnp.sum(state, axis=0, keepdims=True) / MEMBERS
        large, small = halves(state - mean)
        result = product(low, large) + product(high, small) + product(high, large) + mean
        for at, unit in enumerate(units):
            for i in range(OWNERS):
                out_refs[i][unit] = result[
                    i * HELD : (i + 1) * HELD, at * LANES : (at + 1) * LANES
                ]


def analysed(place, cell_fields, transform, pieces, above, below):
    found = pl.pallas_call(
        analyse_kernel,
        out_shape=[shape(5, FIELD_ROWS, 8, LANES), shape(6, 8, LANES)]
        + [shape(UNITS, HELD, LANES)] * OWNERS,
        in_specs=[SCALARS] + whole(6 + OWNERS // 2),
        out_specs=whole(2 + OWNERS),
        compiler_params=params(14),
        name="analyse",
    )(place, *cell_fields, transform, *pieces, above, below)
    return found[0], found[1], found[2:]


def logistic(x):
    return 0.5 * jnp.tanh(0.5 * x) + 0.5


BATCH = 16


def forecast_kernel(shifts, place_ref, counts_ref, wide_ref, field_ref, edge_field_ref, *refs):
    cells_refs, out_refs = refs[: len(shifts)], refs[len(shifts) : 2 * len(shifts)]
    iterate, goal, edge_row = refs[2 * len(shifts) :]
    own = place_ref[0]
    has_above = place_ref[1].astype(F32)
    has_below = place_ref[2].astype(F32)
    lane = lane_ids()
    even = lane % 2 == 0
    first_lane = lane == 0
    ends = first_lane | (lane == LANES - 1)
    sat, store, rain, left, ghosts = range(5)
    tiles = BATCH // 8

    def rolled(array, amount):
        return pltpu.roll(array, amount % LANES, 2)

    def face(level, other, cond, other_cond):
        return 0.5 * (cond + other_cond) * (other - level)

    def swapped(packed):
        return jnp.where(even, rolled(packed, -1), rolled(packed, 1))

    def one_batch(which, batch, carry):
        cells_ref, out_ref = cells_refs[which], out_refs[which]
        owner = relative(own, shifts[which])
        first_member = owner * HELD + batch * BATCH
        most = counts_ref[first_member]
        for n in range(1, BATCH):
            most = jnp.maximum(most, counts_ref[first_member + n])
        counts = wide_ref[pl.ds(pl.multiple_of(first_member, BATCH), BATCH)]
        counts = counts.reshape(tiles, 8, LANES)
        members = pl.ds(pl.multiple_of(batch * BATCH, BATCH), BATCH)

        def begun(level, flux, storage):
            bend = jnp.tanh(level)
            held = storage * bend
            return level + DAMPING * flux / (1.0 + storage * (1.0 - bend * bend)), level + held + flux

        def swept(value, target, storage, sweep):
            bend = jnp.tanh(value)
            derivative = 1.0 + storage * (1.0 - bend * bend)
            moved = value - DAMPING * (value + storage * bend - target) / derivative
            return jnp.where(counts > sweep, moved, value)

        def unit_at(unit):
            return cells_ref[unit, members].reshape(tiles, 8, LANES)

        def cell_at(r):
            if r < 0:
                return unit_at(SENT_ROWS + r + 2)
            if r >= ROWS:
                return unit_at(SENT_ROWS + 2 + r - ROWS)
            return unit_at(r)

        packed = unit_at(EDGE)
        near = jnp.where(lane < OUTER, packed, 0.0)
        inner = jnp.where(even, rolled(packed, -OWN - 1), rolled(packed, -OWN + 1))
        outer = jnp.where(even, rolled(packed, 2 - OUTER), rolled(packed, -OUTER))
        near_k = edge_field_ref[NEAR_K] * logistic(near)
        inner_k = edge_field_ref[INNER_K] * logistic(inner)
        outer_k = edge_field_ref[OUTER_K] * logistic(outer)
        inward = face(near, inner, near_k, inner_k)
        side = swapped(inward)
        flux = inward + face(near, outer, near_k, outer_k)
        flux += face(near, rolled(near, 2), near_k, rolled(near_k, 2))
        flux += face(near, rolled(near, -2), near_k, rolled(near_k, -2))
        flux += edge_field_ref[NEAR_R]
        value, target = begun(near, flux, edge_field_ref[NEAR_S])
        edge_row[0] = value
        edge_row[1] = target

        def conduct(level, r):
            return field_ref[sat, r + 2] * logistic(level)

        level, cond = cell_at(-1), conduct(cell_at(-1), -1)
        above = face(cell_at(-2), level, conduct(cell_at(-2), -2), cond)
        for r in range(-1, ROWS + 1):
            lower_level = cell_at(r + 1)
            lower_cond = conduct(lower_level, r + 1)
            under = face(level, lower_level, cond, lower_cond)
            beside = rolled(level, 1)
            across = face(beside, level, field_ref[left, r + 2] * logistic(beside), cond)
            across = jnp.where(first_lane, 0.0, across)
            flux = under - above + (rolled(across, -1) - across)
            flux -= jnp.where(ends, rolled(side, -2 * (r + 1) - 1), 0.0)
            flux += field_ref[rain, r + 2]
            iterate[r + 1], goal[r + 1] = begun(level, flux, field_ref[store, r + 2])
            level, cond, above = lower_level, lower_cond, under

        def first_sweep(sweep, carry):
            for n in range(ROWS + 2):
                iterate[n] = swept(iterate[n], goal[n], field_ref[store, n + 1], sweep)
            edge_row[0] = swept(edge_row[0], edge_row[1], edge_field_ref[NEAR_S], sweep)
            return carry

        lax.fori_loop(1, most, first_sweep, 0)

        near = edge_row[0] * edge_field_ref[NEAR_MASK]
        side = swapped(near)
        level = iterate[1]
        cond = conduct(level, 0)
        before = iterate[0] * has_above
        above = face(before, level, conduct(before, -1), cond)
        for r in range(ROWS):
            lower_level = iterate[r + 2]
            if r == ROWS - 1:
                lower_level = lower_level * has_below
            lower_cond = conduct(lower_level, r + 1)
            under = face(level, lower_level, cond, lower_cond)
            beside = rolled(level, 1)
            across = face(beside, level, field_ref[left, r + 2] * logistic(beside), cond)
            across = jnp.where(first_lane, 0.0, across)
            flux = under - above + (rolled(across, -1) - across)
            ghost = rolled(side, -2 * (r + 1) - 1)
            entering = face(level, ghost, cond, field_ref[ghosts, r + 2] * logistic(ghost))
            flux += jnp.where(ends, entering, 0.0)
            flux += field_ref[rain, r + 2]
            iterate[r + 1], goal[r + 1] = begun(level, flux, field_ref[store, r + 2])
            level, cond, above = lower_level, lower_cond, under

        def second_sweep(sweep, carry):
            for n in range(1, ROWS + 1):
                iterate[n] = swept(iterate[n], goal[n], field_ref[store, n + 1], sweep)
            return carry

        lax.fori_loop(1, most, second_sweep, 0)
        for r in range(ROWS):
            for tile in range(tiles):
                start = (batch * BATCH + tile * 8) * ROWS + r
                out_ref[pl.ds(start, 8, stride=ROWS), :] = iterate[r + 1, tile]
        return carry

    for which in range(len(shifts)):
        lax.fori_loop(0, HELD // BATCH, functools.partial(one_batch, which), 0)


def forecasts(shifts, place, counts, wide_counts, fields, edge_fields, cells):
    many = len(shifts)
    return pl.pallas_call(
        functools.partial(forecast_kernel, shifts),
        out_shape=[shape(HELD * ROWS, LANES)] * many,
        in_specs=[SCALARS, SCALARS] + whole(3 + many),
        out_specs=whole(many),
        scratch_shapes=[
            pltpu.VMEM((ROWS + 2, BATCH // 8, 8, LANES), F32),
            pltpu.VMEM((ROWS + 2, BATCH // 8, 8, LANES), F32),
            pltpu.VMEM((2, BATCH // 8, 8, LANES), F32),
        ],
        compiler_params=params(6),
        cost_estimate=pl.CostEstimate(flops=1, bytes_accessed=1, transcendentals=0),
        name="forecast",
    )(place, counts, wide_counts, fields, edge_fields, *cells)


def unpack_kernel(many, place_ref, *refs):
    out_ref = refs[-1]
    step = pl.program_id(0)
    for n in range(many):

        @pl.when(step == n)
        def _():
            out_ref[...] = refs[n][...]


def unpacked(place, shifts, pieces, begun=None):
    many = len(shifts)

    def column(step, place_ref):
        block = jnp.int32(0)
        for n, shift in enumerate(shifts):
            block = jnp.where(step == n, relative(place_ref[0], shift, -1), block)
        return 0, block

    extra = [] if begun is None else [begun]
    return pl.pallas_call(
        functools.partial(unpack_kernel, many),
        grid_spec=pltpu.PrefetchScalarGridSpec(
            num_scalar_prefetch=1,
            grid=(many,),
            in_specs=whole(many) + [pl.BlockSpec(memory_space=pl.ANY)] * len(extra),
            out_specs=pl.BlockSpec((HELD * ROWS, LANES), column),
        ),
        out_shape=shape(HELD * ROWS, OWNERS * LANES),
        input_output_aliases={1 + many: 0} if extra else {},
        compiler_params=params(6),
        name="unpack",
    )(place, *pieces, *extra)


def exchanged(copies, axis):
    return lax.all_to_all(copies, axis, split_axis=0, concat_axis=0, tiled=True)


def shared(array, axis):
    return exchanged(jnp.broadcast_to(array, (lax.axis_size(axis), *array.shape)), axis)


def along(array, axis, step):
    peers = lax.axis_size(axis)
    return lax.ppermute(array, axis, [(i, (i + step) % peers) for i in range(peers)])


def to_owner(array, place):
    chips = OWNERS // 2
    pairs = [(i, 2 * ((i // 2 + place // 2) % chips) + (i % 2 ^ place % 2)) for i in range(OWNERS)]
    return lax.ppermute(array, MEMBER, pairs)


def to_strips_beside(array, step):
    peers = lax.axis_size(SPACE)
    pairs = [(i, i + step) for i in range(peers) if 0 <= i + step < peers]
    return lax.ppermute(array, SPACE, pairs)


def on_device(state, obs_index, obs_value, obs_scale, ksat, storage, recharge, newton_counts):
    members, rows, columns = state.shape
    flat = state.reshape(members * rows, columns)
    own = lax.axis_index(MEMBER)
    strip = lax.axis_index(SPACE)
    place = jnp.stack(
        [own, (strip > 0).astype(jnp.int32), (strip < lax.axis_size(SPACE) - 1).astype(jnp.int32)]
    ).astype(jnp.int32)

    seen = observed(flat, obs_index[None], lax.axis_size(MEMBER[0]))
    same = exchanged(seen, MEMBER[0])

    kept, given = packed_blocks(place, flat, seen)
    wide_counts = jnp.broadcast_to(newton_counts[:, None], (MEMBERS, LANES))
    same, kept, given, wide_counts = lax.optimization_barrier((same, kept, given, wide_counts))
    other = along(same, MEMBER[1], 1)
    taken = along(given, MEMBER[1], 1)
    joint = [jnp.stack([kept[n], taken[n]]) for n in range(OWNERS // 2)]

    pieces = [joint[0]] + [along(joint[n], MEMBER[0], -n) for n in range(1, OWNERS // 2)]
    copies = lax.axis_size(SPACE[0])
    part = gram_blocks(place, same, other, obs_value[None], obs_scale[None], copies)
    part = jnp.sum(exchanged(part, SPACE[0]), axis=0)
    part = jnp.sum(shared(part, SPACE[1]), axis=0)
    parts = shared(part, MEMBER)
    cell_fields = (ksat, storage, recharge)
    down, up = borders(pieces, cell_fields)
    parts, down, up = lax.optimization_barrier((parts, down, up))
    above = to_strips_beside(up, 1)
    below = to_strips_beside(down, -1)
    transform = transform_of(place, parts)
    fields, edge_fields, cells = analysed(place, cell_fields, transform, pieces, above, below)

    arrived = [None] * OWNERS
    for shifts in ((2,), (6,), (4, 5), (3, 7), (1, 0)):
        moved = forecasts(
            shifts, place, newton_counts, wide_counts, fields, edge_fields, [cells[i] for i in shifts]
        )
        moved, cells = lax.optimization_barrier((moved, cells))
        for i, field in zip(shifts, moved):
            arrived[i] = to_owner(field, i) if i else field
    early, late = (0, 2, 6, 4, 5), (3, 7, 1)
    result = unpacked(place, early, [arrived[i] for i in early])
    result = unpacked(place, late, [arrived[i] for i in late], result)
    return result.reshape(members, rows, columns)


def solution(mesh):
    x = 4
    finer = Mesh(
        mesh.devices.reshape(4, 2, -1, x), ("member_0", "member_1", "space_0", "space_1")
    )
    placed = (
        P(MEMBER, SPACE, None),
        P(SPACE),
        P(SPACE),
        P(SPACE),
        P(SPACE, None),
        P(SPACE, None),
        P(SPACE, None),
        P(),
    )
    return jax.shard_map(
        on_device, mesh=finer, in_specs=placed, out_specs=P(MEMBER, SPACE, None), check_vma=False
    )
```

```python
import functools

import jax
import jax.numpy as jnp
from jax import lax
from jax.experimental import pallas as pl
from jax.experimental.pallas import tpu as pltpu
from jax.sharding import Mesh
from jax.sharding import PartitionSpec as P

NS_ITERS = 12
DAMPING = 0.3
MEMBER = ("member_0", "member_1")
SPACE = ("space_0", "space_1")
HIGHEST = lax.Precision.HIGHEST
F32 = jnp.float32

OWNERS = 8
HELD = 32
ROWS = 16
LANES = 128
MEMBERS = OWNERS * HELD
EDGE = ROWS
SENT_ROWS = ROWS + 1
OUTER = 36
OWN = 72


def shape(*dims, dtype=F32):
    return jax.ShapeDtypeStruct(dims, dtype)


def whole(count):
    return [pl.BlockSpec(memory_space=pltpu.VMEM)] * count


def params(mib):
    return pltpu.CompilerParams(vmem_limit_bytes=mib * 2**20)


SCALARS = pl.BlockSpec(memory_space=pltpu.SMEM)


def relative(own, place, sign=1):
    chip, core = lax.div(own, 2), lax.rem(own, 2)
    chips = OWNERS // 2
    other = lax.rem(chip + sign * (place // 2) + chips, chips)
    return 2 * other + (1 - core if place % 2 else core)


def lane_ids(rows=8):
    return lax.broadcasted_iota(jnp.int32, (rows, LANES), 1)


def turned(array, amount):
    return pltpu.roll(array, amount % LANES, 1)


def dot(a, b, dims=((1,), (0,))):
    return lax.dot_general(a, b, (dims, ((), ())), precision=HIGHEST, preferred_element_type=F32)


def observe_kernel(index_ref, state_ref, seen_ref):
    values = state_ref[...]
    high = values.astype(jnp.bfloat16)
    rest = values - high.astype(F32)
    middle = rest.astype(jnp.bfloat16)
    low = (rest - middle.astype(F32)).astype(jnp.bfloat16)
    width = values.shape[1]
    step = 256
    for first in range(0, index_ref.shape[1], step):
        cell = index_ref[:, first : first + step]
        row = cell // width
        column = cell - row * width
        places = lax.broadcasted_iota(jnp.int32, (width, step), 0)
        chosen = (places == column).astype(F32).astype(jnp.bfloat16)
        picked = jnp.dot(low, chosen, preferred_element_type=F32)
        picked += jnp.dot(middle, chosen, preferred_element_type=F32)
        picked += jnp.dot(high, chosen, preferred_element_type=F32)
        picked = picked.reshape(HELD, ROWS, step)
        rows = lax.broadcasted_iota(jnp.int32, (ROWS, step), 0)
        seen = jnp.sum(jnp.where((rows == row)[None], picked, 0.0), axis=1)
        for copy in range(seen_ref.shape[0]):
            seen_ref[copy, :, first : first + step] = seen


def observed(state, obs_index, copies):
    return pl.pallas_call(
        observe_kernel,
        out_shape=shape(copies, HELD, obs_index.shape[1]),
        in_specs=whole(2),
        out_specs=whole(1)[0],
        compiler_params=params(20),
        name="observe",
    )(obs_index, state)


ORDER = (0, 1, EDGE, ROWS - 2, ROWS - 1) + tuple(range(2, ROWS - 2))
PLACE = {unit: at for at, unit in enumerate(ORDER)}


def pack_kernel(place_ref, state_ref, after_ref, *refs):
    own = place_ref[0]
    sent_refs, column_ref = refs[:2], refs[2]
    lane = lane_ids()
    even = lane % 2 == 0
    near_left = (lane < OUTER) & even
    near_right = (lane < OUTER) & ~even
    far_left = (lane >= OUTER) & (lane < OUTER + 2 * ROWS) & even
    far_right = (lane >= OUTER + 3) & (lane < OUTER + 3 + 2 * ROWS) & ~even
    own_lanes = (lane >= OWN) & (lane < OWN + 2 * ROWS + 4)

    def one_group(group, carry):
        near, far = [], []
        members = pl.ds(pl.multiple_of(group * 8, 8), 8)
        lines = pl.ds(pl.multiple_of(group * 8 * ROWS, 8 * ROWS), 8 * ROWS)
        for slot in range(OWNERS):
            block = relative(own, slot, -1)
            packed_near = jnp.zeros((8, LANES), F32)
            packed_far = jnp.zeros((8, LANES), F32)
            start = pl.multiple_of(block * LANES, LANES)
            column_ref[slot] = state_ref[lines, pl.ds(start, LANES)]
            for r in range(ROWS):
                value = column_ref[slot, pl.ds(r, 8, stride=ROWS), :]
                sent_refs[slot % 2][slot // 2, PLACE[r], members] = value
                at = 2 * (r + 1)
                packed_near = jnp.where(
                    (lane == at) | (lane == at + 1), turned(value, at + 1), packed_near
                )
                at = OUTER + 2 * r
                packed_far = jnp.where(
                    (lane == at) | (lane == at + 3), turned(value, at + 2), packed_far
                )
            near.append(packed_near)
            far.append(packed_far)
        for slot in range(OWNERS):
            block = relative(own, slot, -1)
            odd = lax.rem(block, 2) == 1
            beside, further = slot ^ 1, ((slot ^ 1) + 2) % OWNERS
            nearer = ((slot ^ 1) - 2) % OWNERS
            has_left = (block > 0).astype(F32)
            has_right = (block < OWNERS - 1).astype(F32)

            def left(packed):
                return jnp.where(odd, packed[beside], packed[further]) * has_left

            def right(packed):
                return jnp.where(odd, packed[nearer], packed[beside]) * has_right

            edge = jnp.where(own_lanes, turned(near[slot], OWN), 0.0)
            edge = jnp.where(near_left, left(near), edge)
            edge = jnp.where(far_left, left(far), edge)
            edge = jnp.where(near_right, right(near), edge)
            edge = jnp.where(far_right, right(far), edge)
            sent_refs[slot % 2][slot // 2, PLACE[EDGE], members] = edge
        return carry

    lax.fori_loop(0, HELD // 8, one_group, 0)


def packed_blocks(place, state, after):
    return pl.pallas_call(
        pack_kernel,
        out_shape=[shape(OWNERS // 2, SENT_ROWS, HELD, LANES)] * 2,
        in_specs=[SCALARS] + whole(1) + [pl.BlockSpec(memory_space=pl.ANY)],
        out_specs=whole(2),
        scratch_shapes=[pltpu.VMEM((OWNERS, 8 * ROWS, LANES), F32)],
        compiler_params=params(8),
        name="pack",
    )(place, state, after)


BORDER = OWNERS * 3 * HELD
FIELD_LINES = 3 * 2 * OWNERS


def border_kernel(*refs):
    chips = OWNERS // 2
    pieces, fields = refs[:chips], refs[chips : chips + 3]
    down_ref, up_ref = refs[chips + 3 :]
    size = 3 * HELD
    for i in range(OWNERS):
        piece = pieces[i // 2]
        down_ref[i * size : (i + 1) * size] = piece[i % 2, 0:3].reshape(size, LANES)
        up_ref[i * size : (i + 1) * size] = piece[i % 2, 2:5].reshape(size, LANES)
    for which, ref in enumerate(fields):
        for block in range(OWNERS):
            at = BORDER + (which * OWNERS + block) * 2
            lanes = slice(block * LANES, (block + 1) * LANES)
            down_ref[at : at + 2] = ref[0:2, lanes]
            up_ref[at : at + 2] = ref[ROWS - 2 : ROWS, lanes]


def borders(pieces, fields):
    size = BORDER + FIELD_LINES
    return pl.pallas_call(
        border_kernel,
        grid=(1,),
        out_shape=[shape(size, LANES)] * 2,
        in_specs=[pl.BlockSpec((2, 5, HELD, LANES), lambda g: (0, 0, 0, 0))] * (OWNERS // 2)
        + [pl.BlockSpec((ROWS, OWNERS * LANES), lambda g: (0, 0))] * 3,
        out_specs=[pl.BlockSpec((size, LANES), lambda g: (0, 0))] * 2,
        compiler_params=params(6),
        name="borders",
    )(*pieces, *fields)


def gram_kernel(place_ref, same_ref, other_ref, value_ref, scale_ref, out_ref):
    own = place_ref[0]
    total = jnp.sum(same_ref[...], axis=(0, 1)) + jnp.sum(other_ref[...], axis=(0, 1))
    mean = (total / MEMBERS)[None]
    scale = scale_ref[...]
    weight = scale / jnp.sqrt(F32(MEMBERS - 1))
    blocks = []
    for k in range(5):
        at = lax.rem(own + k, OWNERS) // 2
        block = same_ref[at] if k % 2 == 0 else other_ref[at]
        blocks.append((block - mean) * weight)
    innovation = scale * (value_ref[...] - mean)
    left = jnp.concatenate([blocks[0], jnp.broadcast_to(innovation, (8, mean.shape[1]))], axis=0)
    main = dot(left, jnp.concatenate(blocks[:4], axis=0), ((1,), (1,)))
    last = jnp.concatenate([blocks[4], jnp.zeros((96, mean.shape[1]), F32)], axis=0)
    opposite = dot(blocks[0], last, ((1,), (1,)))
    packed = opposite[0:8]
    for g in range(1, 4):
        packed += turned(opposite[8 * g : 8 * g + 8], HELD * g)
    for copy in range(out_ref.shape[0]):
        out_ref[copy, 0:40] = main
        out_ref[copy, 40:48] = packed


def gram_blocks(place, same, other, value, scale, copies):
    return pl.pallas_call(
        gram_kernel,
        out_shape=shape(copies, 48, LANES),
        in_specs=[SCALARS] + whole(4),
        out_specs=whole(1)[0],
        compiler_params=params(8),
        cost_estimate=pl.CostEstimate(flops=10**10, bytes_accessed=10**6, transcendentals=0),
        name="gram",
    )(place, same, other, value, scale)


def thirds(array):
    high = array.astype(jnp.bfloat16)
    rest = array - high.astype(F32)
    middle = rest.astype(jnp.bfloat16)
    return high, middle, (rest - middle.astype(F32)).astype(jnp.bfloat16)


def six_products(a, b):
    def product(i, j):
        return jnp.dot(a[i], b[j], preferred_element_type=F32)

    small = product(0, 2) + product(2, 0) + product(1, 1)
    return (small + (product(0, 1) + product(1, 0))) + product(0, 0)


def three_products(a, b):
    def product(i, j):
        return jnp.dot(a[i], b[j], preferred_element_type=F32)

    return (product(0, 1) + product(1, 0)) + product(0, 0)


def root_kernel(place_ref, parts_ref, out_ref, half_ref):
    own = place_ref[0]
    lane = lane_ids()
    drive_row = jnp.zeros((8, MEMBERS), F32)
    nothing = jnp.zeros((8, LANES), F32)
    for i in range(OWNERS):
        for g in range(4):
            rows = parts_ref[i, 8 * g : 8 * g + 8]
            rows = jnp.where(lane < HELD, 0.5 * rows, rows)
            fifth = turned(parts_ref[i, 40:48], -HELD * g)
            fifth = jnp.where(lane < HELD, 0.5 * fifth, 0.0)
            line = jnp.concatenate([rows, fifth], axis=1)
            half_ref[i * HELD + 8 * g : i * HELD + 8 * g + 8] = pltpu.roll(line, HELD * i, 1)
        drive = jnp.where(lane < HELD, parts_ref[relative(own, i), 32:40], 0.0)
        line = jnp.concatenate([drive, nothing], axis=1)
        drive_row += pltpu.roll(line, HELD * i, 1)
    half = half_ref[...]
    rows = lax.broadcasted_iota(jnp.int32, (MEMBERS, MEMBERS), 0)
    columns = lax.broadcasted_iota(jnp.int32, (MEMBERS, MEMBERS), 1)
    identity = (rows == columns).astype(F32)
    big = identity + (half + half.T)
    norm = jnp.sqrt(jnp.sum(big * big))
    upper = big / norm
    middle = 1.5 * identity - 0.5 * upper
    middle_parts = thirds(middle)
    upper = six_products(thirds(upper), middle_parts)
    lower = middle
    lower_parts = middle_parts
    for _ in range(NS_ITERS - 2):
        upper_parts = thirds(upper)
        middle_parts = thirds(1.5 * identity - 0.5 * three_products(lower_parts, upper_parts))
        upper = six_products(upper_parts, middle_parts)
        lower = six_products(middle_parts, lower_parts)
        lower_parts = thirds(lower)
    middle = 1.5 * identity - 0.5 * three_products(lower_parts, thirds(upper))
    root = six_products(thirds(middle), lower_parts) / jnp.sqrt(norm)

    def rows_in_order(matrix):
        half_ref[...] = matrix
        starts = [pl.multiple_of(relative(own, i) * HELD, HELD) for i in range(OWNERS)]
        return jnp.concatenate([half_ref[pl.ds(start, HELD)] for start in starts], axis=0)

    root = rows_in_order(rows_in_order(root).T)
    weights = dot(dot(drive_row, root, ((1,), (1,))), root, ((1,), (1,)))
    out_ref[...] = root + weights[0:1] / jnp.sqrt(F32(MEMBERS - 1))


def transform_of(place, parts):
    return pl.pallas_call(
        root_kernel,
        out_shape=shape(MEMBERS, MEMBERS),
        in_specs=[SCALARS] + whole(1),
        out_specs=whole(1)[0],
        scratch_shapes=[pltpu.VMEM((MEMBERS, MEMBERS), F32)],
        compiler_params=params(12),
        cost_estimate=pl.CostEstimate(flops=10**10, bytes_accessed=10**6, transcendentals=0),
        name="root",
    )(place, parts)


FIELD_ROWS = 20
NEAR_K, INNER_K, OUTER_K, NEAR_S, NEAR_R, NEAR_MASK = range(6)


def spread_fields(place_ref, ksat_ref, storage_ref, recharge_ref, above_ref, below_ref, out_ref, edge_ref):
    own = place_ref[0]
    lane = lane_ids(1)
    even = lane % 2 == 0
    left_block = jnp.maximum(own - 1, 0)
    right_block = jnp.minimum(own + 1, OWNERS - 1)
    has_left = own > 0
    has_right = own < OWNERS - 1
    packed = [jnp.zeros((1, LANES), F32) for _ in range(5)]
    for which, ref in enumerate((ksat_ref, storage_ref, recharge_ref)):
        for place in range(FIELD_ROWS):
            r = place - 2

            def row_of(block):
                line = BORDER + (which * OWNERS + block) * 2
                if r < 0:
                    return above_ref[pl.ds(line + r + 2, 1)]
                if r >= ROWS:
                    return below_ref[pl.ds(line + r - ROWS, 1)]
                return ref[r : r + 1, pl.ds(pl.multiple_of(block * LANES, LANES), LANES)]

            mine = row_of(own)
            out_ref[which, place] = jnp.broadcast_to(mine, (8, LANES))
            if r < -1 or r > ROWS:
                if which == 0:
                    out_ref[3, place] = jnp.zeros((8, LANES), F32)
                    out_ref[4, place] = jnp.zeros((8, LANES), F32)
                continue
            at = 2 * (r + 1)
            here = (lane == at) | (lane == at + 1)
            left = jnp.where(has_left, row_of(left_block), 0.0)
            right = jnp.where(has_right, row_of(right_block), 0.0)
            near = jnp.where(lane < LANES // 2, right, left)
            near = turned(near, at + 1)
            if which == 0:
                out_ref[3, place] = jnp.broadcast_to(turned(mine, 1), (8, LANES))
                beyond = jnp.where(lane == 0, turned(left, 1), turned(right, -1))
                out_ref[4, place] = jnp.broadcast_to(beyond, (8, LANES))
                inner = jnp.where(even, turned(mine, at), turned(mine, at + 2))
                outer = jnp.where(even, turned(left, at + 2), turned(right, at))
                packed[NEAR_K] = jnp.where(here, near, packed[NEAR_K])
                packed[INNER_K] = jnp.where(here, inner, packed[INNER_K])
                packed[OUTER_K] = jnp.where(here, outer, packed[OUTER_K])
            elif which == 1:
                packed[NEAR_S] = jnp.where(here, near, packed[NEAR_S])
            else:
                packed[NEAR_R] = jnp.where(here, near, packed[NEAR_R])
    for n in range(5):
        edge_ref[n] = jnp.broadcast_to(packed[n], (8, LANES))
    lane = lane_ids()
    keep = jnp.where(lane % 2 == 0, has_left.astype(F32), has_right.astype(F32))
    edge_ref[NEAR_MASK] = jnp.where((lane >= 2) & (lane < 2 * ROWS + 2), keep, 0.0)


UNITS = ROWS + 5


def halves(array):
    high = array.astype(jnp.bfloat16)
    return high, (array - high.astype(F32)).astype(jnp.bfloat16)


def analyse_kernel(*refs):
    place_ref, ksat_ref, storage_ref, recharge_ref, transform_ref = refs[:5]
    chips = OWNERS // 2
    piece_refs = refs[5 : 5 + chips]
    above_ref, below_ref, field_ref, edge_field_ref = refs[5 + chips : 9 + chips]
    out_refs = refs[9 + chips :]
    spread_fields(
        place_ref, ksat_ref, storage_ref, recharge_ref, above_ref, below_ref, field_ref, edge_field_ref
    )
    high, low = halves(transform_ref[...])
    lane = lax.broadcasted_iota(jnp.int32, (MEMBERS, LANES), 1)

    def joined(find):
        return jnp.concatenate([find(i) for i in range(OWNERS)], axis=0)

    def border(ref, n):
        return joined(lambda i: ref[(i * 3 + n) * HELD : (i * 3 + n + 1) * HELD])

    def cells(unit):
        if unit > SENT_ROWS + 1:
            return border(below_ref, unit - SENT_ROWS - 2)
        if unit >= SENT_ROWS:
            return border(above_ref, unit - SENT_ROWS + 1)
        found = joined(lambda i: piece_refs[i // 2][i % 2, PLACE[unit]])
        if unit == EDGE:
            top = border(above_ref, 0)
            bottom = border(below_ref, 2)
            first = (lane < 2) | ((lane >= OWN) & (lane < OWN + 2))
            last = 2 * ROWS + 2
            final = ((lane >= last) & (lane < last + 2)) | (
                (lane >= OWN + last) & (lane < OWN + last + 2)
            )
            found = jnp.where(first, turned(top, -2 * ROWS), found)
            found = jnp.where(final, turned(bottom, 2 * ROWS), found)
        return found

    def product(a, b):
        return jnp.dot(a, b, preferred_element_type=F32)

    for first in range(0, UNITS, 2):
        units = range(first, min(first + 2, UNITS))
        found = [cells(u) for u in units]
        state = found[0] if len(found) == 1 else jnp.concatenate(found, axis=1)
        mean = jnp.sum(state, axis=0, keepdims=True) / MEMBERS
        large, small = halves(state - mean)
        result = product(low, large) + product(high, small) + product(high, large) + mean
        for at, unit in enumerate(units):
            for i in range(OWNERS):
                out_refs[i][unit] = result[
                    i * HELD : (i + 1) * HELD, at * LANES : (at + 1) * LANES
                ]


def analysed(place, cell_fields, transform, pieces, above, below):
    found = pl.pallas_call(
        analyse_kernel,
        out_shape=[shape(5, FIELD_ROWS, 8, LANES), shape(6, 8, LANES)]
        + [shape(UNITS, HELD, LANES)] * OWNERS,
        in_specs=[SCALARS] + whole(6 + OWNERS // 2),
        out_specs=whole(2 + OWNERS),
        compiler_params=params(14),
        name="analyse",
    )(place, *cell_fields, transform, *pieces, above, below)
    return found[0], found[1], found[2:]


def logistic(x):
    return 0.5 * jnp.tanh(0.5 * x) + 0.5


BATCH = 16


def forecast_kernel(shifts, place_ref, counts_ref, wide_ref, field_ref, edge_field_ref, *refs):
    cells_refs, out_refs = refs[: len(shifts)], refs[len(shifts) : 2 * len(shifts)]
    iterate, goal, edge_row = refs[2 * len(shifts) :]
    own = place_ref[0]
    has_above = place_ref[1].astype(F32)
    has_below = place_ref[2].astype(F32)
    lane = lane_ids()
    even = lane % 2 == 0
    first_lane = lane == 0
    ends = first_lane | (lane == LANES - 1)
    sat, store, rain, left, ghosts = range(5)
    tiles = BATCH // 8

    def rolled(array, amount):
        return pltpu.roll(array, amount % LANES, 2)

    def face(level, other, cond, other_cond):
        return 0.5 * (cond + other_cond) * (other - level)

    def swapped(packed):
        return jnp.where(even, rolled(packed, -1), rolled(packed, 1))

    def one_batch(which, batch, carry):
        cells_ref, out_ref = cells_refs[which], out_refs[which]
        owner = relative(own, shifts[which])
        first_member = owner * HELD + batch * BATCH
        most = counts_ref[first_member]
        for n in range(1, BATCH):
            most = jnp.maximum(most, counts_ref[first_member + n])
        counts = wide_ref[pl.ds(pl.multiple_of(first_member, BATCH), BATCH)]
        counts = counts.reshape(tiles, 8, LANES)
        members = pl.ds(pl.multiple_of(batch * BATCH, BATCH), BATCH)

        def begun(level, flux, storage):
            bend = jnp.tanh(level)
            held = storage * bend
            derivative = (1.0 + storage) - held * bend
            return level + DAMPING * flux / derivative, level + held + flux

        def swept(value, target, storage, sweep):
            bend = jnp.tanh(value)
            held = storage * bend
            derivative = (1.0 + storage) - held * bend
            moved = value - DAMPING * (value + held - target) / derivative
            return jnp.where(counts > sweep, moved, value)

        def unit_at(unit):
            return cells_ref[unit, members].reshape(tiles, 8, LANES)

        def cell_at(r):
            if r < 0:
                return unit_at(SENT_ROWS + r + 2)
            if r >= ROWS:
                return unit_at(SENT_ROWS + 2 + r - ROWS)
            return unit_at(r)

        packed = unit_at(EDGE)
        near = jnp.where(lane < OUTER, packed, 0.0)
        inner = jnp.where(even, rolled(packed, -OWN - 1), rolled(packed, -OWN + 1))
        outer = jnp.where(even, rolled(packed, 2 - OUTER), rolled(packed, -OUTER))
        near_k = edge_field_ref[NEAR_K] * logistic(near)
        inner_k = edge_field_ref[INNER_K] * logistic(inner)
        outer_k = edge_field_ref[OUTER_K] * logistic(outer)
        inward = face(near, inner, near_k, inner_k)
        side = swapped(inward)
        flux = inward + face(near, outer, near_k, outer_k)
        flux += face(near, rolled(near, 2), near_k, rolled(near_k, 2))
        flux += face(near, rolled(near, -2), near_k, rolled(near_k, -2))
        flux += edge_field_ref[NEAR_R]
        value, target = begun(near, flux, edge_field_ref[NEAR_S])
        edge_row[0] = value
        edge_row[1] = target

        def conduct(level, r):
            return field_ref[sat, r + 2] * logistic(level)

        level, cond = cell_at(-1), conduct(cell_at(-1), -1)
        above = face(cell_at(-2), level, conduct(cell_at(-2), -2), cond)
        for r in range(-1, ROWS + 1):
            lower_level = cell_at(r + 1)
            lower_cond = conduct(lower_level, r + 1)
            under = face(level, lower_level, cond, lower_cond)
            beside = rolled(level, 1)
            across = face(beside, level, field_ref[left, r + 2] * logistic(beside), cond)
            across = jnp.where(first_lane, 0.0, across)
            flux = under - above + (rolled(across, -1) - across)
            flux -= jnp.where(ends, rolled(side, -2 * (r + 1) - 1), 0.0)
            flux += field_ref[rain, r + 2]
            iterate[r + 1], goal[r + 1] = begun(level, flux, field_ref[store, r + 2])
            level, cond, above = lower_level, lower_cond, under

        def first_sweep(sweep, carry):
            for n in range(ROWS + 2):
                iterate[n] = swept(iterate[n], goal[n], field_ref[store, n + 1], sweep)
            edge_row[0] = swept(edge_row[0], edge_row[1], edge_field_ref[NEAR_S], sweep)
            return carry

        lax.fori_loop(1, most, first_sweep, 0)

        near = edge_row[0] * edge_field_ref[NEAR_MASK]
        side = swapped(near)
        level = iterate[1]
        cond = conduct(level, 0)
        before = iterate[0] * has_above
        above = face(before, level, conduct(before, -1), cond)
        for r in range(ROWS):
            lower_level = iterate[r + 2]
            if r == ROWS - 1:
                lower_level = lower_level * has_below
            lower_cond = conduct(lower_level, r + 1)
            under = face(level, lower_level, cond, lower_cond)
            beside = rolled(level, 1)
            across = face(beside, level, field_ref[left, r + 2] * logistic(beside), cond)
            across = jnp.where(first_lane, 0.0, across)
            flux = under - above + (rolled(across, -1) - across)
            ghost = rolled(side, -2 * (r + 1) - 1)
            entering = face(level, ghost, cond, field_ref[ghosts, r + 2] * logistic(ghost))
            flux += jnp.where(ends, entering, 0.0)
            flux += field_ref[rain, r + 2]
            iterate[r + 1], goal[r + 1] = begun(level, flux, field_ref[store, r + 2])
            level, cond, above = lower_level, lower_cond, under

        def second_sweep(sweep, carry):
            for n in range(1, ROWS + 1):
                iterate[n] = swept(iterate[n], goal[n], field_ref[store, n + 1], sweep)
            return carry

        lax.fori_loop(1, most, second_sweep, 0)
        for r in range(ROWS):
            for tile in range(tiles):
                start = (batch * BATCH + tile * 8) * ROWS + r
                out_ref[pl.ds(start, 8, stride=ROWS), :] = iterate[r + 1, tile]
        return carry

    for which in range(len(shifts)):
        lax.fori_loop(0, HELD // BATCH, functools.partial(one_batch, which), 0)


def forecasts(shifts, place, counts, wide_counts, fields, edge_fields, cells):
    many = len(shifts)
    return pl.pallas_call(
        functools.partial(forecast_kernel, shifts),
        out_shape=[shape(HELD * ROWS, LANES)] * many,
        in_specs=[SCALARS, SCALARS] + whole(3 + many),
        out_specs=whole(many),
        scratch_shapes=[
            pltpu.VMEM((ROWS + 2, BATCH // 8, 8, LANES), F32),
            pltpu.VMEM((ROWS + 2, BATCH // 8, 8, LANES), F32),
            pltpu.VMEM((2, BATCH // 8, 8, LANES), F32),
        ],
        compiler_params=params(6),
        cost_estimate=pl.CostEstimate(flops=1, bytes_accessed=1, transcendentals=0),
        name="forecast",
    )(place, counts, wide_counts, fields, edge_fields, *cells)


def unpack_kernel(many, place_ref, *refs):
    out_ref = refs[-1]
    step = pl.program_id(0)
    for n in range(many):

        @pl.when(step == n)
        def _():
            out_ref[...] = refs[n][...]


def unpacked(place, shifts, pieces, begun=None):
    many = len(shifts)

    def column(step, place_ref):
        block = jnp.int32(0)
        for n, shift in enumerate(shifts):
            block = jnp.where(step == n, relative(place_ref[0], shift, -1), block)
        return 0, block

    extra = [] if begun is None else [begun]
    return pl.pallas_call(
        functools.partial(unpack_kernel, many),
        grid_spec=pltpu.PrefetchScalarGridSpec(
            num_scalar_prefetch=1,
            grid=(many,),
            in_specs=whole(many) + [pl.BlockSpec(memory_space=pl.ANY)] * len(extra),
            out_specs=pl.BlockSpec((HELD * ROWS, LANES), column),
        ),
        out_shape=shape(HELD * ROWS, OWNERS * LANES),
        input_output_aliases={1 + many: 0} if extra else {},
        compiler_params=params(6),
        name="unpack",
    )(place, *pieces, *extra)


def exchanged(copies, axis):
    return lax.all_to_all(copies, axis, split_axis=0, concat_axis=0, tiled=True)


def shared(array, axis):
    return exchanged(jnp.broadcast_to(array, (lax.axis_size(axis), *array.shape)), axis)


def along(array, axis, step):
    peers = lax.axis_size(axis)
    return lax.ppermute(array, axis, [(i, (i + step) % peers) for i in range(peers)])


def to_owner(array, place):
    chips = OWNERS // 2
    pairs = [(i, 2 * ((i // 2 + place // 2) % chips) + (i % 2 ^ place % 2)) for i in range(OWNERS)]
    return lax.ppermute(array, MEMBER, pairs)


def to_strips_beside(array, step):
    peers = lax.axis_size(SPACE)
    pairs = [(i, i + step) for i in range(peers) if 0 <= i + step < peers]
    return lax.ppermute(array, SPACE, pairs)


def on_device(state, obs_index, obs_value, obs_scale, ksat, storage, recharge, newton_counts):
    members, rows, columns = state.shape
    flat = state.reshape(members * rows, columns)
    own = lax.axis_index(MEMBER)
    strip = lax.axis_index(SPACE)
    place = jnp.stack(
        [own, (strip > 0).astype(jnp.int32), (strip < lax.axis_size(SPACE) - 1).astype(jnp.int32)]
    ).astype(jnp.int32)

    seen = observed(flat, obs_index[None], lax.axis_size(MEMBER[0]))
    same = exchanged(seen, MEMBER[0])

    kept, given = packed_blocks(place, flat, seen)
    wide_counts = jnp.broadcast_to(newton_counts[:, None], (MEMBERS, LANES))
    same, kept, given, wide_counts = lax.optimization_barrier((same, kept, given, wide_counts))
    other = along(same, MEMBER[1], 1)
    taken = along(given, MEMBER[1], 1)
    joint = [jnp.stack([kept[n], taken[n]]) for n in range(OWNERS // 2)]

    pieces = [joint[0]] + [along(joint[n], MEMBER[0], -n) for n in range(1, OWNERS // 2)]
    copies = lax.axis_size(SPACE[0])
    part = gram_blocks(place, same, other, obs_value[None], obs_scale[None], copies)
    part = jnp.sum(exchanged(part, SPACE[0]), axis=0)
    part = jnp.sum(shared(part, SPACE[1]), axis=0)
    part, pieces = lax.optimization_barrier((part, pieces))
    parts = shared(part, MEMBER)
    cell_fields = (ksat, storage, recharge)
    down, up = borders(pieces, cell_fields)
    parts, down, up = lax.optimization_barrier((parts, down, up))
    above = to_strips_beside(up, 1)
    below = to_strips_beside(down, -1)
    transform = transform_of(place, parts)
    fields, edge_fields, cells = analysed(place, cell_fields, transform, pieces, above, below)

    arrived = [None] * OWNERS
    for shifts in ((2, 6), (4, 5), (3, 7), (1, 0)):
        moved = forecasts(
            shifts, place, newton_counts, wide_counts, fields, edge_fields, [cells[i] for i in shifts]
        )
        moved, cells = lax.optimization_barrier((moved, cells))
        for i, field in zip(shifts, moved):
            arrived[i] = to_owner(field, i) if i else field
    early, late = (0, 2, 6, 4, 5), (3, 7, 1)
    result = unpacked(place, early, [arrived[i] for i in early])
    result = unpacked(place, late, [arrived[i] for i in late], result)
    return result.reshape(members, rows, columns)


def solution(mesh):
    x = 4
    finer = Mesh(
        mesh.devices.reshape(4, 2, -1, x), ("member_0", "member_1", "space_0", "space_1")
    )
    placed = (
        P(MEMBER, SPACE, None),
        P(SPACE),
        P(SPACE),
        P(SPACE),
        P(SPACE, None),
        P(SPACE, None),
        P(SPACE, None),
        P(),
    )
    return jax.shard_map(
        on_device, mesh=finer, in_specs=placed, out_specs=P(MEMBER, SPACE, None), check_vma=False
    )
```

```python
import functools

import jax
import jax.numpy as jnp
from jax import lax
from jax.experimental import pallas as pl
from jax.experimental.pallas import tpu as pltpu
from jax.sharding import Mesh
from jax.sharding import PartitionSpec as P

NS_ITERS = 12
DAMPING = 0.3
MEMBER = ("member_0", "member_1")
SPACE = ("space_0", "space_1")
HIGHEST = lax.Precision.HIGHEST
F32 = jnp.float32

OWNERS = 8
HELD = 32
ROWS = 16
LANES = 128
MEMBERS = OWNERS * HELD
EDGE = ROWS
SENT_ROWS = ROWS + 1
OUTER = 36
OWN = 72


def shape(*dims, dtype=F32):
    return jax.ShapeDtypeStruct(dims, dtype)


def whole(count):
    return [pl.BlockSpec(memory_space=pltpu.VMEM)] * count


def params(mib):
    return pltpu.CompilerParams(vmem_limit_bytes=mib * 2**20)


SCALARS = pl.BlockSpec(memory_space=pltpu.SMEM)


def relative(own, place, sign=1):
    chip, core = lax.div(own, 2), lax.rem(own, 2)
    chips = OWNERS // 2
    other = lax.rem(chip + sign * (place // 2) + chips, chips)
    return 2 * other + (1 - core if place % 2 else core)


def lane_ids(rows=8):
    return lax.broadcasted_iota(jnp.int32, (rows, LANES), 1)


def turned(array, amount):
    return pltpu.roll(array, amount % LANES, 1)


def dot(a, b, dims=((1,), (0,))):
    return lax.dot_general(a, b, (dims, ((), ())), precision=HIGHEST, preferred_element_type=F32)


def observe_kernel(index_ref, state_ref, seen_ref):
    values = state_ref[...]
    high = values.astype(jnp.bfloat16)
    rest = values - high.astype(F32)
    middle = rest.astype(jnp.bfloat16)
    low = (rest - middle.astype(F32)).astype(jnp.bfloat16)
    width = values.shape[1]
    step = 256
    for first in range(0, index_ref.shape[1], step):
        cell = index_ref[:, first : first + step]
        row = cell // width
        column = cell - row * width
        places = lax.broadcasted_iota(jnp.int32, (width, step), 0)
        chosen = (places == column).astype(F32).astype(jnp.bfloat16)
        picked = jnp.dot(low, chosen, preferred_element_type=F32)
        picked += jnp.dot(middle, chosen, preferred_element_type=F32)
        picked += jnp.dot(high, chosen, preferred_element_type=F32)
        picked = picked.reshape(HELD, ROWS, step)
        rows = lax.broadcasted_iota(jnp.int32, (ROWS, step), 0)
        seen = jnp.sum(jnp.where((rows == row)[None], picked, 0.0), axis=1)
        for copy in range(seen_ref.shape[0]):
            seen_ref[copy, :, first : first + step] = seen


def observed(state, obs_index, copies):
    return pl.pallas_call(
        observe_kernel,
        out_shape=shape(copies, HELD, obs_index.shape[1]),
        in_specs=whole(2),
        out_specs=whole(1)[0],
        compiler_params=params(20),
        name="observe",
    )(obs_index, state)


ORDER = (0, 1, EDGE, ROWS - 2, ROWS - 1) + tuple(range(2, ROWS - 2))
PLACE = {unit: at for at, unit in enumerate(ORDER)}


def pack_kernel(place_ref, state_ref, after_ref, *refs):
    own = place_ref[0]
    sent_refs, column_ref = refs[:2], refs[2]
    lane = lane_ids()
    even = lane % 2 == 0
    near_left = (lane < OUTER) & even
    near_right = (lane < OUTER) & ~even
    far_left = (lane >= OUTER) & (lane < OUTER + 2 * ROWS) & even
    far_right = (lane >= OUTER + 3) & (lane < OUTER + 3 + 2 * ROWS) & ~even
    own_lanes = (lane >= OWN) & (lane < OWN + 2 * ROWS + 4)

    def one_group(group, carry):
        near, far = [], []
        members = pl.ds(pl.multiple_of(group * 8, 8), 8)
        lines = pl.ds(pl.multiple_of(group * 8 * ROWS, 8 * ROWS), 8 * ROWS)
        for slot in range(OWNERS):
            block = relative(own, slot, -1)
            packed_near = jnp.zeros((8, LANES), F32)
            packed_far = jnp.zeros((8, LANES), F32)
            start = pl.multiple_of(block * LANES, LANES)
            column_ref[slot] = state_ref[lines, pl.ds(start, LANES)]
            for r in range(ROWS):
                value = column_ref[slot, pl.ds(r, 8, stride=ROWS), :]
                sent_refs[slot % 2][slot // 2, PLACE[r], members] = value
                at = 2 * (r + 1)
                packed_near = jnp.where(
                    (lane == at) | (lane == at + 1), turned(value, at + 1), packed_near
                )
                at = OUTER + 2 * r
                packed_far = jnp.where(
                    (lane == at) | (lane == at + 3), turned(value, at + 2), packed_far
                )
            near.append(packed_near)
            far.append(packed_far)
        for slot in range(OWNERS):
            block = relative(own, slot, -1)
            odd = lax.rem(block, 2) == 1
            beside, further = slot ^ 1, ((slot ^ 1) + 2) % OWNERS
            nearer = ((slot ^ 1) - 2) % OWNERS
            has_left = (block > 0).astype(F32)
            has_right = (block < OWNERS - 1).astype(F32)

            def left(packed):
                return jnp.where(odd, packed[beside], packed[further]) * has_left

            def right(packed):
                return jnp.where(odd, packed[nearer], packed[beside]) * has_right

            edge = jnp.where(own_lanes, turned(near[slot], OWN), 0.0)
            edge = jnp.where(near_left, left(near), edge)
            edge = jnp.where(far_left, left(far), edge)
            edge = jnp.where(near_right, right(near), edge)
            edge = jnp.where(far_right, right(far), edge)
            sent_refs[slot % 2][slot // 2, PLACE[EDGE], members] = edge
        return carry

    lax.fori_loop(0, HELD // 8, one_group, 0)


def packed_blocks(place, state, after):
    return pl.pallas_call(
        pack_kernel,
        out_shape=[shape(OWNERS // 2, SENT_ROWS, HELD, LANES)] * 2,
        in_specs=[SCALARS] + whole(1) + [pl.BlockSpec(memory_space=pl.ANY)],
        out_specs=whole(2),
        scratch_shapes=[pltpu.VMEM((OWNERS, 8 * ROWS, LANES), F32)],
        compiler_params=params(8),
        name="pack",
    )(place, state, after)


BORDER = OWNERS * 3 * HELD
FIELD_LINES = 3 * 2 * OWNERS


def border_kernel(*refs):
    chips = OWNERS // 2
    pieces, fields = refs[:chips], refs[chips : chips + 3]
    down_ref, up_ref = refs[chips + 3 :]
    size = 3 * HELD
    for i in range(OWNERS):
        piece = pieces[i // 2]
        down_ref[i * size : (i + 1) * size] = piece[i % 2, 0:3].reshape(size, LANES)
        up_ref[i * size : (i + 1) * size] = piece[i % 2, 2:5].reshape(size, LANES)
    for which, ref in enumerate(fields):
        for block in range(OWNERS):
            at = BORDER + (which * OWNERS + block) * 2
            lanes = slice(block * LANES, (block + 1) * LANES)
            down_ref[at : at + 2] = ref[0:2, lanes]
            up_ref[at : at + 2] = ref[ROWS - 2 : ROWS, lanes]


def borders(pieces, fields):
    size = BORDER + FIELD_LINES
    return pl.pallas_call(
        border_kernel,
        grid=(1,),
        out_shape=[shape(size, LANES)] * 2,
        in_specs=[pl.BlockSpec((2, 5, HELD, LANES), lambda g: (0, 0, 0, 0))] * (OWNERS // 2)
        + [pl.BlockSpec((ROWS, OWNERS * LANES), lambda g: (0, 0))] * 3,
        out_specs=[pl.BlockSpec((size, LANES), lambda g: (0, 0))] * 2,
        compiler_params=params(6),
        name="borders",
    )(*pieces, *fields)


def gram_kernel(place_ref, same_ref, other_ref, value_ref, scale_ref, out_ref):
    own = place_ref[0]
    total = jnp.sum(same_ref[...], axis=(0, 1)) + jnp.sum(other_ref[...], axis=(0, 1))
    mean = (total / MEMBERS)[None]
    scale = scale_ref[...]
    weight = scale / jnp.sqrt(F32(MEMBERS - 1))
    blocks = []
    for k in range(5):
        at = lax.rem(own + k, OWNERS) // 2
        block = same_ref[at] if k % 2 == 0 else other_ref[at]
        blocks.append((block - mean) * weight)
    innovation = scale * (value_ref[...] - mean)
    left = jnp.concatenate([blocks[0], jnp.broadcast_to(innovation, (8, mean.shape[1]))], axis=0)
    main = dot(left, jnp.concatenate(blocks[:4], axis=0), ((1,), (1,)))
    last = jnp.concatenate([blocks[4], jnp.zeros((96, mean.shape[1]), F32)], axis=0)
    opposite = dot(blocks[0], last, ((1,), (1,)))
    packed = opposite[0:8]
    for g in range(1, 4):
        packed += turned(opposite[8 * g : 8 * g + 8], HELD * g)
    for copy in range(out_ref.shape[0]):
        out_ref[copy, 0:40] = main
        out_ref[copy, 40:48] = packed


def gram_blocks(place, same, other, value, scale, copies):
    return pl.pallas_call(
        gram_kernel,
        out_shape=shape(copies, 48, LANES),
        in_specs=[SCALARS] + whole(4),
        out_specs=whole(1)[0],
        compiler_params=params(8),
        cost_estimate=pl.CostEstimate(flops=10**10, bytes_accessed=10**6, transcendentals=0),
        name="gram",
    )(place, same, other, value, scale)


def thirds(array):
    high = array.astype(jnp.bfloat16)
    rest = array - high.astype(F32)
    middle = rest.astype(jnp.bfloat16)
    return high, middle, (rest - middle.astype(F32)).astype(jnp.bfloat16)


def six_products(a, b):
    def product(i, j):
        return jnp.dot(a[i], b[j], preferred_element_type=F32)

    small = product(0, 2) + product(2, 0) + product(1, 1)
    return (small + (product(0, 1) + product(1, 0))) + product(0, 0)


def three_products(a, b):
    def product(i, j):
        return jnp.dot(a[i], b[j], preferred_element_type=F32)

    return (product(0, 1) + product(1, 0)) + product(0, 0)


def root_kernel(place_ref, parts_ref, out_ref, half_ref):
    own = place_ref[0]
    lane = lane_ids()
    drive_row = jnp.zeros((8, MEMBERS), F32)
    nothing = jnp.zeros((8, LANES), F32)
    for i in range(OWNERS):
        for g in range(4):
            rows = parts_ref[i, 8 * g : 8 * g + 8]
            rows = jnp.where(lane < HELD, 0.5 * rows, rows)
            fifth = turned(parts_ref[i, 40:48], -HELD * g)
            fifth = jnp.where(lane < HELD, 0.5 * fifth, 0.0)
            line = jnp.concatenate([rows, fifth], axis=1)
            half_ref[i * HELD + 8 * g : i * HELD + 8 * g + 8] = pltpu.roll(line, HELD * i, 1)
        drive = jnp.where(lane < HELD, parts_ref[relative(own, i), 32:40], 0.0)
        line = jnp.concatenate([drive, nothing], axis=1)
        drive_row += pltpu.roll(line, HELD * i, 1)
    half = half_ref[...]
    rows = lax.broadcasted_iota(jnp.int32, (MEMBERS, MEMBERS), 0)
    columns = lax.broadcasted_iota(jnp.int32, (MEMBERS, MEMBERS), 1)
    identity = (rows == columns).astype(F32)
    big = identity + (half + half.T)
    norm = jnp.sqrt(jnp.sum(big * big))
    upper = big / norm
    middle = 1.5 * identity - 0.5 * upper
    middle_parts = thirds(middle)
    upper = six_products(thirds(upper), middle_parts)
    lower = middle
    lower_parts = middle_parts
    for _ in range(NS_ITERS - 2):
        upper_parts = thirds(upper)
        middle_parts = thirds(1.5 * identity - 0.5 * three_products(lower_parts, upper_parts))
        upper = six_products(upper_parts, middle_parts)
        lower = six_products(middle_parts, lower_parts)
        lower_parts = thirds(lower)
    middle = 1.5 * identity - 0.5 * three_products(lower_parts, thirds(upper))
    root = six_products(thirds(middle), lower_parts) / jnp.sqrt(norm)

    def rows_in_order(matrix):
        half_ref[...] = matrix
        starts = [pl.multiple_of(relative(own, i) * HELD, HELD) for i in range(OWNERS)]
        return jnp.concatenate([half_ref[pl.ds(start, HELD)] for start in starts], axis=0)

    root = rows_in_order(rows_in_order(root).T)
    weights = dot(dot(drive_row, root, ((1,), (1,))), root, ((1,), (1,)))
    out_ref[...] = root + weights[0:1] / jnp.sqrt(F32(MEMBERS - 1))


def transform_of(place, parts):
    return pl.pallas_call(
        root_kernel,
        out_shape=shape(MEMBERS, MEMBERS),
        in_specs=[SCALARS] + whole(1),
        out_specs=whole(1)[0],
        scratch_shapes=[pltpu.VMEM((MEMBERS, MEMBERS), F32)],
        compiler_params=params(12),
        cost_estimate=pl.CostEstimate(flops=10**10, bytes_accessed=10**6, transcendentals=0),
        name="root",
    )(place, parts)


FIELD_ROWS = 20
NEAR_K, INNER_K, OUTER_K, NEAR_S, NEAR_R, NEAR_MASK = range(6)


def spread_fields(place_ref, ksat_ref, storage_ref, recharge_ref, above_ref, below_ref, out_ref, edge_ref):
    own = place_ref[0]
    lane = lane_ids(1)
    even = lane % 2 == 0
    left_block = jnp.maximum(own - 1, 0)
    right_block = jnp.minimum(own + 1, OWNERS - 1)
    has_left = own > 0
    has_right = own < OWNERS - 1
    packed = [jnp.zeros((1, LANES), F32) for _ in range(5)]
    for which, ref in enumerate((ksat_ref, storage_ref, recharge_ref)):
        for place in range(FIELD_ROWS):
            r = place - 2

            def row_of(block):
                line = BORDER + (which * OWNERS + block) * 2
                if r < 0:
                    return above_ref[pl.ds(line + r + 2, 1)]
                if r >= ROWS:
                    return below_ref[pl.ds(line + r - ROWS, 1)]
                return ref[r : r + 1, pl.ds(pl.multiple_of(block * LANES, LANES), LANES)]

            mine = row_of(own)
            out_ref[which, place] = jnp.broadcast_to(mine, (8, LANES))
            if r < -1 or r > ROWS:
                if which == 0:
                    out_ref[3, place] = jnp.zeros((8, LANES), F32)
                    out_ref[4, place] = jnp.zeros((8, LANES), F32)
                continue
            at = 2 * (r + 1)
            here = (lane == at) | (lane == at + 1)
            left = jnp.where(has_left, row_of(left_block), 0.0)
            right = jnp.where(has_right, row_of(right_block), 0.0)
            near = jnp.where(lane < LANES // 2, right, left)
            near = turned(near, at + 1)
            if which == 0:
                out_ref[3, place] = jnp.broadcast_to(turned(mine, 1), (8, LANES))
                beyond = jnp.where(lane == 0, turned(left, 1), turned(right, -1))
                out_ref[4, place] = jnp.broadcast_to(beyond, (8, LANES))
                inner = jnp.where(even, turned(mine, at), turned(mine, at + 2))
                outer = jnp.where(even, turned(left, at + 2), turned(right, at))
                packed[NEAR_K] = jnp.where(here, near, packed[NEAR_K])
                packed[INNER_K] = jnp.where(here, inner, packed[INNER_K])
                packed[OUTER_K] = jnp.where(here, outer, packed[OUTER_K])
            elif which == 1:
                packed[NEAR_S] = jnp.where(here, near, packed[NEAR_S])
            else:
                packed[NEAR_R] = jnp.where(here, near, packed[NEAR_R])
    for n in range(5):
        edge_ref[n] = jnp.broadcast_to(packed[n], (8, LANES))
    lane = lane_ids()
    keep = jnp.where(lane % 2 == 0, has_left.astype(F32), has_right.astype(F32))
    edge_ref[NEAR_MASK] = jnp.where((lane >= 2) & (lane < 2 * ROWS + 2), keep, 0.0)


UNITS = ROWS + 5


def halves(array):
    high = array.astype(jnp.bfloat16)
    return high, (array - high.astype(F32)).astype(jnp.bfloat16)


def analyse_kernel(*refs):
    place_ref, ksat_ref, storage_ref, recharge_ref, transform_ref = refs[:5]
    chips = OWNERS // 2
    piece_refs = refs[5 : 5 + chips]
    above_ref, below_ref, field_ref, edge_field_ref = refs[5 + chips : 9 + chips]
    out_refs = refs[9 + chips :]
    spread_fields(
        place_ref, ksat_ref, storage_ref, recharge_ref, above_ref, below_ref, field_ref, edge_field_ref
    )
    high, low = halves(transform_ref[...])
    lane = lax.broadcasted_iota(jnp.int32, (MEMBERS, LANES), 1)

    def joined(find):
        return jnp.concatenate([find(i) for i in range(OWNERS)], axis=0)

    def border(ref, n):
        return joined(lambda i: ref[(i * 3 + n) * HELD : (i * 3 + n + 1) * HELD])

    def cells(unit):
        if unit > SENT_ROWS + 1:
            return border(below_ref, unit - SENT_ROWS - 2)
        if unit >= SENT_ROWS:
            return border(above_ref, unit - SENT_ROWS + 1)
        found = joined(lambda i: piece_refs[i // 2][i % 2, PLACE[unit]])
        if unit == EDGE:
            top = border(above_ref, 0)
            bottom = border(below_ref, 2)
            first = (lane < 2) | ((lane >= OWN) & (lane < OWN + 2))
            last = 2 * ROWS + 2
            final = ((lane >= last) & (lane < last + 2)) | (
                (lane >= OWN + last) & (lane < OWN + last + 2)
            )
            found = jnp.where(first, turned(top, -2 * ROWS), found)
            found = jnp.where(final, turned(bottom, 2 * ROWS), found)
        return found

    def product(a, b):
        return jnp.dot(a, b, preferred_element_type=F32)

    for first in range(0, UNITS, 2):
        units = range(first, min(first + 2, UNITS))
        found = [cells(u) for u in units]
        state = found[0] if len(found) == 1 else jnp.concatenate(found, axis=1)
        mean = jnp.sum(state, axis=0, keepdims=True) / MEMBERS
        large, small = halves(state - mean)
        result = product(low, large) + product(high, small) + product(high, large) + mean
        for at, unit in enumerate(units):
            for i in range(OWNERS):
                out_refs[i][unit] = result[
                    i * HELD : (i + 1) * HELD, at * LANES : (at + 1) * LANES
                ]


def analysed(place, cell_fields, transform, pieces, above, below):
    found = pl.pallas_call(
        analyse_kernel,
        out_shape=[shape(5, FIELD_ROWS, 8, LANES), shape(6, 8, LANES)]
        + [shape(UNITS, HELD, LANES)] * OWNERS,
        in_specs=[SCALARS] + whole(6 + OWNERS // 2),
        out_specs=whole(2 + OWNERS),
        compiler_params=params(14),
        name="analyse",
    )(place, *cell_fields, transform, *pieces, above, below)
    return found[0], found[1], found[2:]


def logistic(x):
    return 0.5 * jnp.tanh(0.5 * x) + 0.5


BATCH = 16


def forecast_kernel(shifts, place_ref, counts_ref, wide_ref, field_ref, edge_field_ref, *refs):
    cells_refs, out_refs = refs[: len(shifts)], refs[len(shifts) : 2 * len(shifts)]
    iterate, goal, edge_row = refs[2 * len(shifts) :]
    own = place_ref[0]
    has_above = place_ref[1].astype(F32)
    has_below = place_ref[2].astype(F32)
    lane = lane_ids()
    even = lane % 2 == 0
    first_lane = lane == 0
    ends = first_lane | (lane == LANES - 1)
    sat, store, rain, left, ghosts = range(5)
    tiles = BATCH // 8

    def rolled(array, amount):
        return pltpu.roll(array, amount % LANES, 2)

    def face(level, other, cond, other_cond):
        return 0.5 * (cond + other_cond) * (other - level)

    def swapped(packed):
        return jnp.where(even, rolled(packed, -1), rolled(packed, 1))

    def one_batch(which, batch, carry):
        cells_ref, out_ref = cells_refs[which], out_refs[which]
        owner = relative(own, shifts[which])
        first_member = owner * HELD + batch * BATCH
        most = counts_ref[first_member]
        for n in range(1, BATCH):
            most = jnp.maximum(most, counts_ref[first_member + n])
        counts = wide_ref[pl.ds(pl.multiple_of(first_member, BATCH), BATCH)]
        counts = counts.reshape(tiles, 8, LANES)
        members = pl.ds(pl.multiple_of(batch * BATCH, BATCH), BATCH)

        def begun(level, flux, storage):
            bend = jnp.tanh(level)
            held = storage * bend
            derivative = (1.0 + storage) - held * bend
            return level + DAMPING * flux / derivative, level + held + flux

        def swept(value, target, storage, sweep):
            bend = jnp.tanh(value)
            held = storage * bend
            derivative = (1.0 + storage) - held * bend
            moved = value - DAMPING * (value + held - target) / derivative
            return jnp.where(counts > sweep, moved, value)

        def unit_at(unit):
            return cells_ref[unit, members].reshape(tiles, 8, LANES)

        def cell_at(r):
            if r < 0:
                return unit_at(SENT_ROWS + r + 2)
            if r >= ROWS:
                return unit_at(SENT_ROWS + 2 + r - ROWS)
            return unit_at(r)

        packed = unit_at(EDGE)
        near = jnp.where(lane < OUTER, packed, 0.0)
        inner = jnp.where(even, rolled(packed, -OWN - 1), rolled(packed, -OWN + 1))
        outer = jnp.where(even, rolled(packed, 2 - OUTER), rolled(packed, -OUTER))
        near_k = edge_field_ref[NEAR_K] * logistic(near)
        inner_k = edge_field_ref[INNER_K] * logistic(inner)
        outer_k = edge_field_ref[OUTER_K] * logistic(outer)
        inward = face(near, inner, near_k, inner_k)
        side = swapped(inward)
        flux = inward + face(near, outer, near_k, outer_k)
        flux += face(near, rolled(near, 2), near_k, rolled(near_k, 2))
        flux += face(near, rolled(near, -2), near_k, rolled(near_k, -2))
        flux += edge_field_ref[NEAR_R]
        value, target = begun(near, flux, edge_field_ref[NEAR_S])
        edge_row[0] = value
        edge_row[1] = target

        def conduct(level, r):
            return field_ref[sat, r + 2] * logistic(level)

        level, cond = cell_at(-1), conduct(cell_at(-1), -1)
        above = face(cell_at(-2), level, conduct(cell_at(-2), -2), cond)
        for r in range(-1, ROWS + 1):
            lower_level = cell_at(r + 1)
            lower_cond = conduct(lower_level, r + 1)
            under = face(level, lower_level, cond, lower_cond)
            beside = rolled(level, 1)
            across = face(beside, level, field_ref[left, r + 2] * logistic(beside), cond)
            across = jnp.where(first_lane, 0.0, across)
            flux = under - above + (rolled(across, -1) - across)
            flux -= jnp.where(ends, rolled(side, -2 * (r + 1) - 1), 0.0)
            flux += field_ref[rain, r + 2]
            iterate[r + 1], goal[r + 1] = begun(level, flux, field_ref[store, r + 2])
            level, cond, above = lower_level, lower_cond, under

        def first_sweep(sweep, carry):
            for n in range(ROWS + 2):
                iterate[n] = swept(iterate[n], goal[n], field_ref[store, n + 1], sweep)
            edge_row[0] = swept(edge_row[0], edge_row[1], edge_field_ref[NEAR_S], sweep)
            return carry

        lax.fori_loop(1, most, first_sweep, 0)

        near = edge_row[0] * edge_field_ref[NEAR_MASK]
        side = swapped(near)
        level = iterate[1]
        cond = conduct(level, 0)
        before = iterate[0] * has_above
        above = face(before, level, conduct(before, -1), cond)
        for r in range(ROWS):
            lower_level = iterate[r + 2]
            if r == ROWS - 1:
                lower_level = lower_level * has_below
            lower_cond = conduct(lower_level, r + 1)
            under = face(level, lower_level, cond, lower_cond)
            beside = rolled(level, 1)
            across = face(beside, level, field_ref[left, r + 2] * logistic(beside), cond)
            across = jnp.where(first_lane, 0.0, across)
            flux = under - above + (rolled(across, -1) - across)
            ghost = rolled(side, -2 * (r + 1) - 1)
            entering = face(level, ghost, cond, field_ref[ghosts, r + 2] * logistic(ghost))
            flux += jnp.where(ends, entering, 0.0)
            flux += field_ref[rain, r + 2]
            iterate[r + 1], goal[r + 1] = begun(level, flux, field_ref[store, r + 2])
            level, cond, above = lower_level, lower_cond, under

        def second_sweep(sweep, carry):
            for n in range(1, ROWS + 1):
                iterate[n] = swept(iterate[n], goal[n], field_ref[store, n + 1], sweep)
            return carry

        lax.fori_loop(1, most, second_sweep, 0)
        for r in range(ROWS):
            for tile in range(tiles):
                start = (batch * BATCH + tile * 8) * ROWS + r
                out_ref[pl.ds(start, 8, stride=ROWS), :] = iterate[r + 1, tile]
        return carry

    for which in range(len(shifts)):
        lax.fori_loop(0, HELD // BATCH, functools.partial(one_batch, which), 0)


def forecasts(shifts, place, counts, wide_counts, fields, edge_fields, cells):
    many = len(shifts)
    return pl.pallas_call(
        functools.partial(forecast_kernel, shifts),
        out_shape=[shape(HELD * ROWS, LANES)] * many,
        in_specs=[SCALARS, SCALARS] + whole(3 + many),
        out_specs=whole(many),
        scratch_shapes=[
            pltpu.VMEM((ROWS + 2, BATCH // 8, 8, LANES), F32),
            pltpu.VMEM((ROWS + 2, BATCH // 8, 8, LANES), F32),
            pltpu.VMEM((2, BATCH // 8, 8, LANES), F32),
        ],
        compiler_params=params(6),
        cost_estimate=pl.CostEstimate(flops=1, bytes_accessed=1, transcendentals=0),
        name="forecast",
    )(place, counts, wide_counts, fields, edge_fields, *cells)


def unpack_kernel(many, place_ref, *refs):
    out_ref = refs[-1]
    step = pl.program_id(0)
    for n in range(many):

        @pl.when(step == n)
        def _():
            out_ref[...] = refs[n][...]


def unpacked(place, shifts, pieces, begun=None):
    many = len(shifts)

    def column(step, place_ref):
        block = jnp.int32(0)
        for n, shift in enumerate(shifts):
            block = jnp.where(step == n, relative(place_ref[0], shift, -1), block)
        return 0, block

    extra = [] if begun is None else [begun]
    return pl.pallas_call(
        functools.partial(unpack_kernel, many),
        grid_spec=pltpu.PrefetchScalarGridSpec(
            num_scalar_prefetch=1,
            grid=(many,),
            in_specs=whole(many) + [pl.BlockSpec(memory_space=pl.ANY)] * len(extra),
            out_specs=pl.BlockSpec((HELD * ROWS, LANES), column),
        ),
        out_shape=shape(HELD * ROWS, OWNERS * LANES),
        input_output_aliases={1 + many: 0} if extra else {},
        compiler_params=params(6),
        name="unpack",
    )(place, *pieces, *extra)


def exchanged(copies, axis):
    return lax.all_to_all(copies, axis, split_axis=0, concat_axis=0, tiled=True)


def shared(array, axis):
    return exchanged(jnp.broadcast_to(array, (lax.axis_size(axis), *array.shape)), axis)


def along(array, axis, step):
    peers = lax.axis_size(axis)
    return lax.ppermute(array, axis, [(i, (i + step) % peers) for i in range(peers)])


def to_owner(array, place):
    chips = OWNERS // 2
    pairs = [(i, 2 * ((i // 2 + place // 2) % chips) + (i % 2 ^ place % 2)) for i in range(OWNERS)]
    return lax.ppermute(array, MEMBER, pairs)


def to_strips_beside(array, step):
    peers = lax.axis_size(SPACE)
    pairs = [(i, i + step) for i in range(peers) if 0 <= i + step < peers]
    return lax.ppermute(array, SPACE, pairs)


def on_device(state, obs_index, obs_value, obs_scale, ksat, storage, recharge, newton_counts):
    members, rows, columns = state.shape
    flat = state.reshape(members * rows, columns)
    own = lax.axis_index(MEMBER)
    strip = lax.axis_index(SPACE)
    place = jnp.stack(
        [own, (strip > 0).astype(jnp.int32), (strip < lax.axis_size(SPACE) - 1).astype(jnp.int32)]
    ).astype(jnp.int32)

    seen = observed(flat, obs_index[None], lax.axis_size(MEMBER[0]))
    same = exchanged(seen, MEMBER[0])

    kept, given = packed_blocks(place, flat, seen)
    wide_counts = jnp.broadcast_to(newton_counts[:, None], (MEMBERS, LANES))
    same, kept, given, wide_counts = lax.optimization_barrier((same, kept, given, wide_counts))
    other = along(same, MEMBER[1], 1)
    taken = along(given, MEMBER[1], 1)
    joint = [jnp.stack([kept[n], taken[n]]) for n in range(OWNERS // 2)]

    pieces = [joint[0]] + [along(joint[n], MEMBER[0], -n) for n in range(1, OWNERS // 2)]
    copies = lax.axis_size(SPACE[0])
    part = gram_blocks(place, same, other, obs_value[None], obs_scale[None], copies)
    part = jnp.sum(exchanged(part, SPACE[0]), axis=0)
    part = jnp.sum(shared(part, SPACE[1]), axis=0)
    part, pieces = lax.optimization_barrier((part, pieces))
    parts = shared(part, MEMBER)
    cell_fields = (ksat, storage, recharge)
    down, up = borders(pieces, cell_fields)
    above = to_strips_beside(up, 1)
    below = to_strips_beside(down, -1)
    transform = transform_of(place, parts)
    fields, edge_fields, cells = analysed(place, cell_fields, transform, pieces, above, below)

    arrived = [None] * OWNERS
    for shifts in ((4,), (2, 6), (5, 3), (7, 1), (0,)):
        if shifts == (7, 1):
            cells, arrived[4] = lax.optimization_barrier((cells, arrived[4]))
        if shifts == (0,):
            cells, arrived[2], arrived[6] = lax.optimization_barrier((cells, arrived[2], arrived[6]))
        moved = forecasts(
            shifts, place, newton_counts, wide_counts, fields, edge_fields, [cells[i] for i in shifts]
        )
        moved, cells = lax.optimization_barrier((moved, cells))
        for i, field in zip(shifts, moved):
            arrived[i] = to_owner(field, i) if i else field
    early, late = (0, 4, 2, 6), (5, 3, 7, 1)
    result = unpacked(place, early, [arrived[i] for i in early])
    result = unpacked(place, late, [arrived[i] for i in late], result)
    return result.reshape(members, rows, columns)


def solution(mesh):
    x = 4
    finer = Mesh(
        mesh.devices.reshape(4, 2, -1, x), ("member_0", "member_1", "space_0", "space_1")
    )
    placed = (
        P(MEMBER, SPACE, None),
        P(SPACE),
        P(SPACE),
        P(SPACE),
        P(SPACE, None),
        P(SPACE, None),
        P(SPACE, None),
        P(),
    )
    return jax.shard_map(
        on_device, mesh=finer, in_specs=placed, out_specs=P(MEMBER, SPACE, None), check_vma=False
    )
```

```python
import functools

import jax
import jax.numpy as jnp
from jax import lax
from jax.experimental import pallas as pl
from jax.experimental.pallas import tpu as pltpu
from jax.sharding import Mesh
from jax.sharding import PartitionSpec as P

NS_ITERS = 12
DAMPING = 0.3
MEMBER = ("member_0", "member_1")
SPACE = ("space_0", "space_1")
HIGHEST = lax.Precision.HIGHEST
F32 = jnp.float32

OWNERS = 8
HELD = 32
ROWS = 16
LANES = 128
MEMBERS = OWNERS * HELD
EDGE = ROWS
SENT_ROWS = ROWS + 1
OUTER = 36
OWN = 72


def shape(*dims, dtype=F32):
    return jax.ShapeDtypeStruct(dims, dtype)


def whole(count):
    return [pl.BlockSpec(memory_space=pltpu.VMEM)] * count


def params(mib):
    return pltpu.CompilerParams(vmem_limit_bytes=mib * 2**20)


SCALARS = pl.BlockSpec(memory_space=pltpu.SMEM)


def relative(own, place, sign=1):
    chip, core = lax.div(own, 2), lax.rem(own, 2)
    chips = OWNERS // 2
    other = lax.rem(chip + sign * (place // 2) + chips, chips)
    return 2 * other + (1 - core if place % 2 else core)


def lane_ids(rows=8):
    return lax.broadcasted_iota(jnp.int32, (rows, LANES), 1)


def turned(array, amount):
    return pltpu.roll(array, amount % LANES, 1)


def dot(a, b, dims=((1,), (0,))):
    return lax.dot_general(a, b, (dims, ((), ())), precision=HIGHEST, preferred_element_type=F32)


def observe_kernel(index_ref, state_ref, seen_ref):
    values = state_ref[...]
    high = values.astype(jnp.bfloat16)
    rest = values - high.astype(F32)
    middle = rest.astype(jnp.bfloat16)
    low = (rest - middle.astype(F32)).astype(jnp.bfloat16)
    width = values.shape[1]
    step = 256
    for first in range(0, index_ref.shape[1], step):
        cell = index_ref[:, first : first + step]
        row = cell // width
        column = cell - row * width
        places = lax.broadcasted_iota(jnp.int32, (width, step), 0)
        chosen = (places == column).astype(F32).astype(jnp.bfloat16)
        picked = jnp.dot(low, chosen, preferred_element_type=F32)
        picked += jnp.dot(middle, chosen, preferred_element_type=F32)
        picked += jnp.dot(high, chosen, preferred_element_type=F32)
        picked = picked.reshape(HELD, ROWS, step)
        rows = lax.broadcasted_iota(jnp.int32, (ROWS, step), 0)
        seen = jnp.sum(jnp.where((rows == row)[None], picked, 0.0), axis=1)
        for copy in range(seen_ref.shape[0]):
            seen_ref[copy, :, first : first + step] = seen


def observed(state, obs_index, copies):
    return pl.pallas_call(
        observe_kernel,
        out_shape=shape(copies, HELD, obs_index.shape[1]),
        in_specs=whole(2),
        out_specs=whole(1)[0],
        compiler_params=params(20),
        name="observe",
    )(obs_index, state)


ORDER = (0, 1, EDGE, ROWS - 2, ROWS - 1) + tuple(range(2, ROWS - 2))
PLACE = {unit: at for at, unit in enumerate(ORDER)}


def pack_kernel(place_ref, state_ref, after_ref, *refs):
    own = place_ref[0]
    chips = OWNERS // 2
    joint_refs, given_ref, column_ref = refs[:chips], refs[chips], refs[chips + 1]

    def put(slot, row, members, value):
        if slot % 2:
            given_ref[slot // 2, row, members] = value
        else:
            joint_refs[slot // 2][0, row, members] = value

    lane = lane_ids()
    even = lane % 2 == 0
    near_left = (lane < OUTER) & even
    near_right = (lane < OUTER) & ~even
    far_left = (lane >= OUTER) & (lane < OUTER + 2 * ROWS) & even
    far_right = (lane >= OUTER + 3) & (lane < OUTER + 3 + 2 * ROWS) & ~even
    own_lanes = (lane >= OWN) & (lane < OWN + 2 * ROWS + 4)

    def one_group(group, carry):
        near, far = [], []
        members = pl.ds(pl.multiple_of(group * 8, 8), 8)
        lines = pl.ds(pl.multiple_of(group * 8 * ROWS, 8 * ROWS), 8 * ROWS)
        for slot in range(OWNERS):
            block = relative(own, slot, -1)
            packed_near = jnp.zeros((8, LANES), F32)
            packed_far = jnp.zeros((8, LANES), F32)
            start = pl.multiple_of(block * LANES, LANES)
            column_ref[slot] = state_ref[lines, pl.ds(start, LANES)]
            for r in range(ROWS):
                value = column_ref[slot, pl.ds(r, 8, stride=ROWS), :]
                put(slot, PLACE[r], members, value)
                at = 2 * (r + 1)
                packed_near = jnp.where(
                    (lane == at) | (lane == at + 1), turned(value, at + 1), packed_near
                )
                at = OUTER + 2 * r
                packed_far = jnp.where(
                    (lane == at) | (lane == at + 3), turned(value, at + 2), packed_far
                )
            near.append(packed_near)
            far.append(packed_far)
        for slot in range(OWNERS):
            block = relative(own, slot, -1)
            odd = lax.rem(block, 2) == 1
            beside, further = slot ^ 1, ((slot ^ 1) + 2) % OWNERS
            nearer = ((slot ^ 1) - 2) % OWNERS
            has_left = (block > 0).astype(F32)
            has_right = (block < OWNERS - 1).astype(F32)

            def left(packed):
                return jnp.where(odd, packed[beside], packed[further]) * has_left

            def right(packed):
                return jnp.where(odd, packed[nearer], packed[beside]) * has_right

            edge = jnp.where(own_lanes, turned(near[slot], OWN), 0.0)
            edge = jnp.where(near_left, left(near), edge)
            edge = jnp.where(far_left, left(far), edge)
            edge = jnp.where(near_right, right(near), edge)
            edge = jnp.where(far_right, right(far), edge)
            put(slot, PLACE[EDGE], members, edge)
        return carry

    lax.fori_loop(0, HELD // 8, one_group, 0)


def packed_blocks(place, state, after):
    chips = OWNERS // 2
    packed = pl.pallas_call(
        pack_kernel,
        out_shape=[shape(2, SENT_ROWS, HELD, LANES)] * chips
        + [shape(chips, SENT_ROWS, HELD, LANES)],
        in_specs=[SCALARS] + whole(1) + [pl.BlockSpec(memory_space=pl.ANY)],
        out_specs=whole(chips + 1),
        scratch_shapes=[pltpu.VMEM((OWNERS, 8 * ROWS, LANES), F32)],
        compiler_params=params(8),
        name="pack",
    )(place, state, after)
    return packed[:chips], packed[chips]


def fill_kernel(taken_ref, *refs):
    chips = OWNERS // 2
    joint_refs, sems = refs[chips : 2 * chips], refs[2 * chips]
    copies = [
        pltpu.make_async_copy(taken_ref.at[n], joint_refs[n].at[1], sems.at[n])
        for n in range(chips)
    ]
    for copy in copies:
        copy.start()
    for copy in copies:
        copy.wait()


def filled(taken, joint):
    chips = OWNERS // 2
    anywhere = [pl.BlockSpec(memory_space=pl.ANY)]
    return pl.pallas_call(
        fill_kernel,
        out_shape=[shape(2, SENT_ROWS, HELD, LANES)] * chips,
        in_specs=whole(1) + anywhere * chips,
        out_specs=anywhere * chips,
        input_output_aliases={1 + n: n for n in range(chips)},
        scratch_shapes=[pltpu.SemaphoreType.DMA((chips,))],
        compiler_params=params(4),
        name="fill",
    )(taken, *joint)


BORDER = OWNERS * 3 * HELD
FIELD_LINES = 3 * 2 * OWNERS


def border_kernel(*refs):
    chips = OWNERS // 2
    pieces, fields = refs[:chips], refs[chips : chips + 3]
    down_ref, up_ref = refs[chips + 3 :]
    size = 3 * HELD
    for i in range(OWNERS):
        piece = pieces[i // 2]
        down_ref[i * size : (i + 1) * size] = piece[i % 2, 0:3].reshape(size, LANES)
        up_ref[i * size : (i + 1) * size] = piece[i % 2, 2:5].reshape(size, LANES)
    for which, ref in enumerate(fields):
        for block in range(OWNERS):
            at = BORDER + (which * OWNERS + block) * 2
            lanes = slice(block * LANES, (block + 1) * LANES)
            down_ref[at : at + 2] = ref[0:2, lanes]
            up_ref[at : at + 2] = ref[ROWS - 2 : ROWS, lanes]


def borders(pieces, fields):
    size = BORDER + FIELD_LINES
    return pl.pallas_call(
        border_kernel,
        grid=(1,),
        out_shape=[shape(size, LANES)] * 2,
        in_specs=[pl.BlockSpec((2, 5, HELD, LANES), lambda g: (0, 0, 0, 0))] * (OWNERS // 2)
        + [pl.BlockSpec((ROWS, OWNERS * LANES), lambda g: (0, 0))] * 3,
        out_specs=[pl.BlockSpec((size, LANES), lambda g: (0, 0))] * 2,
        compiler_params=params(6),
        name="borders",
    )(*pieces, *fields)


def gram_kernel(place_ref, same_ref, other_ref, value_ref, scale_ref, out_ref):
    own = place_ref[0]
    total = jnp.sum(same_ref[...], axis=(0, 1)) + jnp.sum(other_ref[...], axis=(0, 1))
    mean = (total / MEMBERS)[None]
    scale = scale_ref[...]
    weight = scale / jnp.sqrt(F32(MEMBERS - 1))
    blocks = []
    for k in range(5):
        at = lax.rem(own + k, OWNERS) // 2
        block = same_ref[at] if k % 2 == 0 else other_ref[at]
        blocks.append((block - mean) * weight)
    innovation = scale * (value_ref[...] - mean)
    left = jnp.concatenate([blocks[0], jnp.broadcast_to(innovation, (8, mean.shape[1]))], axis=0)
    main = dot(left, jnp.concatenate(blocks[:4], axis=0), ((1,), (1,)))
    last = jnp.concatenate([blocks[4], jnp.zeros((96, mean.shape[1]), F32)], axis=0)
    opposite = dot(blocks[0], last, ((1,), (1,)))
    packed = opposite[0:8]
    for g in range(1, 4):
        packed += turned(opposite[8 * g : 8 * g + 8], HELD * g)
    for copy in range(out_ref.shape[0]):
        out_ref[copy, 0:40] = main
        out_ref[copy, 40:48] = packed


def gram_blocks(place, same, other, value, scale, copies):
    return pl.pallas_call(
        gram_kernel,
        out_shape=shape(copies, 48, LANES),
        in_specs=[SCALARS] + whole(4),
        out_specs=whole(1)[0],
        compiler_params=params(8),
        cost_estimate=pl.CostEstimate(flops=10**10, bytes_accessed=10**6, transcendentals=0),
        name="gram",
    )(place, same, other, value, scale)


def thirds(array):
    high = array.astype(jnp.bfloat16)
    rest = array - high.astype(F32)
    middle = rest.astype(jnp.bfloat16)
    return high, middle, (rest - middle.astype(F32)).astype(jnp.bfloat16)


def six_products(a, b):
    def product(i, j):
        return jnp.dot(a[i], b[j], preferred_element_type=F32)

    small = product(0, 2) + product(2, 0) + product(1, 1)
    return (small + (product(0, 1) + product(1, 0))) + product(0, 0)


def three_products(a, b):
    def product(i, j):
        return jnp.dot(a[i], b[j], preferred_element_type=F32)

    return (product(0, 1) + product(1, 0)) + product(0, 0)


def root_kernel(place_ref, parts_ref, out_ref, half_ref):
    own = place_ref[0]
    lane = lane_ids()
    drive_row = jnp.zeros((8, MEMBERS), F32)
    nothing = jnp.zeros((8, LANES), F32)
    for i in range(OWNERS):
        for g in range(4):
            rows = parts_ref[i, 8 * g : 8 * g + 8]
            rows = jnp.where(lane < HELD, 0.5 * rows, rows)
            fifth = turned(parts_ref[i, 40:48], -HELD * g)
            fifth = jnp.where(lane < HELD, 0.5 * fifth, 0.0)
            line = jnp.concatenate([rows, fifth], axis=1)
            half_ref[i * HELD + 8 * g : i * HELD + 8 * g + 8] = pltpu.roll(line, HELD * i, 1)
        drive = jnp.where(lane < HELD, parts_ref[relative(own, i), 32:40], 0.0)
        line = jnp.concatenate([drive, nothing], axis=1)
        drive_row += pltpu.roll(line, HELD * i, 1)
    half = half_ref[...]
    rows = lax.broadcasted_iota(jnp.int32, (MEMBERS, MEMBERS), 0)
    columns = lax.broadcasted_iota(jnp.int32, (MEMBERS, MEMBERS), 1)
    identity = (rows == columns).astype(F32)
    big = identity + (half + half.T)
    norm = jnp.sqrt(jnp.sum(big * big))
    upper = big / norm
    middle = 1.5 * identity - 0.5 * upper
    middle_parts = thirds(middle)
    upper = six_products(thirds(upper), middle_parts)
    lower = middle
    lower_parts = middle_parts
    for _ in range(NS_ITERS - 2):
        upper_parts = thirds(upper)
        middle_parts = thirds(1.5 * identity - 0.5 * three_products(lower_parts, upper_parts))
        upper = six_products(upper_parts, middle_parts)
        lower = six_products(middle_parts, lower_parts)
        lower_parts = thirds(lower)
    middle = 1.5 * identity - 0.5 * three_products(lower_parts, thirds(upper))
    root = six_products(thirds(middle), lower_parts) / jnp.sqrt(norm)

    def rows_in_order(matrix):
        half_ref[...] = matrix
        starts = [pl.multiple_of(relative(own, i) * HELD, HELD) for i in range(OWNERS)]
        return jnp.concatenate([half_ref[pl.ds(start, HELD)] for start in starts], axis=0)

    root = rows_in_order(rows_in_order(root).T)
    weights = dot(dot(drive_row, root, ((1,), (1,))), root, ((1,), (1,)))
    out_ref[...] = root + weights[0:1] / jnp.sqrt(F32(MEMBERS - 1))


def transform_of(place, parts):
    return pl.pallas_call(
        root_kernel,
        out_shape=shape(MEMBERS, MEMBERS),
        in_specs=[SCALARS] + whole(1),
        out_specs=whole(1)[0],
        scratch_shapes=[pltpu.VMEM((MEMBERS, MEMBERS), F32)],
        compiler_params=params(12),
        cost_estimate=pl.CostEstimate(flops=10**10, bytes_accessed=10**6, transcendentals=0),
        name="root",
    )(place, parts)


FIELD_ROWS = 20
NEAR_K, INNER_K, OUTER_K, NEAR_S, NEAR_R, NEAR_MASK = range(6)


def spread_fields(place_ref, ksat_ref, storage_ref, recharge_ref, above_ref, below_ref, out_ref, edge_ref):
    own = place_ref[0]
    lane = lane_ids(1)
    even = lane % 2 == 0
    left_block = jnp.maximum(own - 1, 0)
    right_block = jnp.minimum(own + 1, OWNERS - 1)
    has_left = own > 0
    has_right = own < OWNERS - 1
    packed = [jnp.zeros((1, LANES), F32) for _ in range(5)]
    for which, ref in enumerate((ksat_ref, storage_ref, recharge_ref)):
        for place in range(FIELD_ROWS):
            r = place - 2

            def row_of(block):
                line = BORDER + (which * OWNERS + block) * 2
                if r < 0:
                    return above_ref[pl.ds(line + r + 2, 1)]
                if r >= ROWS:
                    return below_ref[pl.ds(line + r - ROWS, 1)]
                return ref[r : r + 1, pl.ds(pl.multiple_of(block * LANES, LANES), LANES)]

            mine = row_of(own)
            out_ref[which, place] = jnp.broadcast_to(mine, (8, LANES))
            if r < -1 or r > ROWS:
                if which == 0:
                    out_ref[3, place] = jnp.zeros((8, LANES), F32)
                    out_ref[4, place] = jnp.zeros((8, LANES), F32)
                continue
            at = 2 * (r + 1)
            here = (lane == at) | (lane == at + 1)
            left = jnp.where(has_left, row_of(left_block), 0.0)
            right = jnp.where(has_right, row_of(right_block), 0.0)
            near = jnp.where(lane < LANES // 2, right, left)
            near = turned(near, at + 1)
            if which == 0:
                out_ref[3, place] = jnp.broadcast_to(turned(mine, 1), (8, LANES))
                beyond = jnp.where(lane == 0, turned(left, 1), turned(right, -1))
                out_ref[4, place] = jnp.broadcast_to(beyond, (8, LANES))
                inner = jnp.where(even, turned(mine, at), turned(mine, at + 2))
                outer = jnp.where(even, turned(left, at + 2), turned(right, at))
                packed[NEAR_K] = jnp.where(here, near, packed[NEAR_K])
                packed[INNER_K] = jnp.where(here, inner, packed[INNER_K])
                packed[OUTER_K] = jnp.where(here, outer, packed[OUTER_K])
            elif which == 1:
                packed[NEAR_S] = jnp.where(here, near, packed[NEAR_S])
            else:
                packed[NEAR_R] = jnp.where(here, near, packed[NEAR_R])
    for n in range(5):
        edge_ref[n] = jnp.broadcast_to(packed[n], (8, LANES))
    lane = lane_ids()
    keep = jnp.where(lane % 2 == 0, has_left.astype(F32), has_right.astype(F32))
    edge_ref[NEAR_MASK] = jnp.where((lane >= 2) & (lane < 2 * ROWS + 2), keep, 0.0)


UNITS = ROWS + 5


def halves(array):
    high = array.astype(jnp.bfloat16)
    return high, (array - high.astype(F32)).astype(jnp.bfloat16)


def analyse_kernel(*refs):
    place_ref, ksat_ref, storage_ref, recharge_ref, transform_ref = refs[:5]
    chips = OWNERS // 2
    piece_refs = refs[5 : 5 + chips]
    above_ref, below_ref, field_ref, edge_field_ref = refs[5 + chips : 9 + chips]
    out_refs = refs[9 + chips :]
    spread_fields(
        place_ref, ksat_ref, storage_ref, recharge_ref, above_ref, below_ref, field_ref, edge_field_ref
    )
    high, low = halves(transform_ref[...])
    lane = lax.broadcasted_iota(jnp.int32, (MEMBERS, LANES), 1)

    def joined(find):
        return jnp.concatenate([find(i) for i in range(OWNERS)], axis=0)

    def border(ref, n):
        return joined(lambda i: ref[(i * 3 + n) * HELD : (i * 3 + n + 1) * HELD])

    def cells(unit):
        if unit > SENT_ROWS + 1:
            return border(below_ref, unit - SENT_ROWS - 2)
        if unit >= SENT_ROWS:
            return border(above_ref, unit - SENT_ROWS + 1)
        found = joined(lambda i: piece_refs[i // 2][i % 2, PLACE[unit]])
        if unit == EDGE:
            top = border(above_ref, 0)
            bottom = border(below_ref, 2)
            first = (lane < 2) | ((lane >= OWN) & (lane < OWN + 2))
            last = 2 * ROWS + 2
            final = ((lane >= last) & (lane < last + 2)) | (
                (lane >= OWN + last) & (lane < OWN + last + 2)
            )
            found = jnp.where(first, turned(top, -2 * ROWS), found)
            found = jnp.where(final, turned(bottom, 2 * ROWS), found)
        return found

    def product(a, b):
        return jnp.dot(a, b, preferred_element_type=F32)

    for first in range(0, UNITS, 2):
        units = range(first, min(first + 2, UNITS))
        found = [cells(u) for u in units]
        state = found[0] if len(found) == 1 else jnp.concatenate(found, axis=1)
        mean = jnp.sum(state, axis=0, keepdims=True) / MEMBERS
        large, small = halves(state - mean)
        result = product(low, large) + product(high, small) + product(high, large) + mean
        for at, unit in enumerate(units):
            for i in range(OWNERS):
                out_refs[i][unit] = result[
                    i * HELD : (i + 1) * HELD, at * LANES : (at + 1) * LANES
                ]


def analysed(place, cell_fields, transform, pieces, above, below):
    found = pl.pallas_call(
        analyse_kernel,
        out_shape=[shape(5, FIELD_ROWS, 8, LANES), shape(6, 8, LANES)]
        + [shape(UNITS, HELD, LANES)] * OWNERS,
        in_specs=[SCALARS] + whole(6 + OWNERS // 2),
        out_specs=whole(2 + OWNERS),
        compiler_params=params(14),
        name="analyse",
    )(place, *cell_fields, transform, *pieces, above, below)
    return found[0], found[1], found[2:]


def logistic(x):
    return 0.5 * jnp.tanh(0.5 * x) + 0.5


BATCH = 16


def forecast_kernel(shifts, place_ref, counts_ref, wide_ref, field_ref, edge_field_ref, *refs):
    cells_refs, out_refs = refs[: len(shifts)], refs[len(shifts) : 2 * len(shifts)]
    iterate, goal, edge_row = refs[2 * len(shifts) :]
    own = place_ref[0]
    has_above = place_ref[1].astype(F32)
    has_below = place_ref[2].astype(F32)
    lane = lane_ids()
    even = lane % 2 == 0
    first_lane = lane == 0
    ends = first_lane | (lane == LANES - 1)
    sat, store, rain, left, ghosts = range(5)
    tiles = BATCH // 8

    def rolled(array, amount):
        return pltpu.roll(array, amount % LANES, 2)

    def face(level, other, cond, other_cond):
        return 0.5 * (cond + other_cond) * (other - level)

    def swapped(packed):
        return jnp.where(even, rolled(packed, -1), rolled(packed, 1))

    def one_batch(which, batch, carry):
        cells_ref, out_ref = cells_refs[which], out_refs[which]
        owner = relative(own, shifts[which])
        first_member = owner * HELD + batch * BATCH
        most = counts_ref[first_member]
        for n in range(1, BATCH):
            most = jnp.maximum(most, counts_ref[first_member + n])
        counts = wide_ref[pl.ds(pl.multiple_of(first_member, BATCH), BATCH)]
        counts = counts.reshape(tiles, 8, LANES)
        members = pl.ds(pl.multiple_of(batch * BATCH, BATCH), BATCH)

        def begun(level, flux, storage):
            bend = jnp.tanh(level)
            held = storage * bend
            derivative = (1.0 + storage) - held * bend
            return level + DAMPING * flux / derivative, level + held + flux

        def swept(value, target, storage, sweep):
            bend = jnp.tanh(value)
            held = storage * bend
            derivative = (1.0 + storage) - held * bend
            moved = value - DAMPING * (value + held - target) / derivative
            return jnp.where(counts > sweep, moved, value)

        def unit_at(unit):
            return cells_ref[unit, members].reshape(tiles, 8, LANES)

        def cell_at(r):
            if r < 0:
                return unit_at(SENT_ROWS + r + 2)
            if r >= ROWS:
                return unit_at(SENT_ROWS + 2 + r - ROWS)
            return unit_at(r)

        packed = unit_at(EDGE)
        near = jnp.where(lane < OUTER, packed, 0.0)
        inner = jnp.where(even, rolled(packed, -OWN - 1), rolled(packed, -OWN + 1))
        outer = jnp.where(even, rolled(packed, 2 - OUTER), rolled(packed, -OUTER))
        near_k = edge_field_ref[NEAR_K] * logistic(near)
        inner_k = edge_field_ref[INNER_K] * logistic(inner)
        outer_k = edge_field_ref[OUTER_K] * logistic(outer)
        inward = face(near, inner, near_k, inner_k)
        side = swapped(inward)
        flux = inward + face(near, outer, near_k, outer_k)
        flux += face(near, rolled(near, 2), near_k, rolled(near_k, 2))
        flux += face(near, rolled(near, -2), near_k, rolled(near_k, -2))
        flux += edge_field_ref[NEAR_R]
        value, target = begun(near, flux, edge_field_ref[NEAR_S])
        edge_row[0] = value
        edge_row[1] = target

        def conduct(level, r):
            return field_ref[sat, r + 2] * logistic(level)

        level, cond = cell_at(-1), conduct(cell_at(-1), -1)
        above = face(cell_at(-2), level, conduct(cell_at(-2), -2), cond)
        for r in range(-1, ROWS + 1):
            lower_level = cell_at(r + 1)
            lower_cond = conduct(lower_level, r + 1)
            under = face(level, lower_level, cond, lower_cond)
            beside = rolled(level, 1)
            across = face(beside, level, field_ref[left, r + 2] * logistic(beside), cond)
            across = jnp.where(first_lane, 0.0, across)
            flux = under - above + (rolled(across, -1) - across)
            flux -= jnp.where(ends, rolled(side, -2 * (r + 1) - 1), 0.0)
            flux += field_ref[rain, r + 2]
            iterate[r + 1], goal[r + 1] = begun(level, flux, field_ref[store, r + 2])
            level, cond, above = lower_level, lower_cond, under

        def first_sweep(sweep, carry):
            for n in range(ROWS + 2):
                iterate[n] = swept(iterate[n], goal[n], field_ref[store, n + 1], sweep)
            edge_row[0] = swept(edge_row[0], edge_row[1], edge_field_ref[NEAR_S], sweep)
            return carry

        lax.fori_loop(1, most, first_sweep, 0)

        near = edge_row[0] * edge_field_ref[NEAR_MASK]
        side = swapped(near)
        level = iterate[1]
        cond = conduct(level, 0)
        before = iterate[0] * has_above
        above = face(before, level, conduct(before, -1), cond)
        for r in range(ROWS):
            lower_level = iterate[r + 2]
            if r == ROWS - 1:
                lower_level = lower_level * has_below
            lower_cond = conduct(lower_level, r + 1)
            under = face(level, lower_level, cond, lower_cond)
            beside = rolled(level, 1)
            across = face(beside, level, field_ref[left, r + 2] * logistic(beside), cond)
            across = jnp.where(first_lane, 0.0, across)
            flux = under - above + (rolled(across, -1) - across)
            ghost = rolled(side, -2 * (r + 1) - 1)
            entering = face(level, ghost, cond, field_ref[ghosts, r + 2] * logistic(ghost))
            flux += jnp.where(ends, entering, 0.0)
            flux += field_ref[rain, r + 2]
            iterate[r + 1], goal[r + 1] = begun(level, flux, field_ref[store, r + 2])
            level, cond, above = lower_level, lower_cond, under

        def second_sweep(sweep, carry):
            for n in range(1, ROWS + 1):
                iterate[n] = swept(iterate[n], goal[n], field_ref[store, n + 1], sweep)
            return carry

        lax.fori_loop(1, most, second_sweep, 0)
        for r in range(ROWS):
            for tile in range(tiles):
                start = (batch * BATCH + tile * 8) * ROWS + r
                out_ref[pl.ds(start, 8, stride=ROWS), :] = iterate[r + 1, tile]
        return carry

    for which in range(len(shifts)):
        lax.fori_loop(0, HELD // BATCH, functools.partial(one_batch, which), 0)


def forecasts(shifts, place, counts, wide_counts, fields, edge_fields, cells):
    many = len(shifts)
    return pl.pallas_call(
        functools.partial(forecast_kernel, shifts),
        out_shape=[shape(HELD * ROWS, LANES)] * many,
        in_specs=[SCALARS, SCALARS] + whole(3 + many),
        out_specs=whole(many),
        scratch_shapes=[
            pltpu.VMEM((ROWS + 2, BATCH // 8, 8, LANES), F32),
            pltpu.VMEM((ROWS + 2, BATCH // 8, 8, LANES), F32),
            pltpu.VMEM((2, BATCH // 8, 8, LANES), F32),
        ],
        compiler_params=params(6),
        cost_estimate=pl.CostEstimate(flops=1, bytes_accessed=1, transcendentals=0),
        name="forecast",
    )(place, counts, wide_counts, fields, edge_fields, *cells)


def unpack_kernel(shifts, place_ref, *refs):
    out_ref, sems = refs[-2], refs[-1]
    copies = []
    for n, shift in enumerate(shifts):
        block = relative(place_ref[0], shift, -1)
        lanes = pl.ds(pl.multiple_of(block * LANES, LANES), LANES)
        copies.append(pltpu.make_async_copy(refs[n], out_ref.at[:, lanes], sems.at[n]))
    for copy in copies:
        copy.start()
    for copy in copies:
        copy.wait()


def unpacked(place, shifts, pieces, begun=None):
    many = len(shifts)
    anywhere = pl.BlockSpec(memory_space=pl.ANY)
    extra = [] if begun is None else [begun]
    return pl.pallas_call(
        functools.partial(unpack_kernel, shifts),
        out_shape=shape(HELD * ROWS, OWNERS * LANES),
        in_specs=[SCALARS] + whole(many) + [anywhere] * len(extra),
        out_specs=anywhere,
        input_output_aliases={1 + many: 0} if extra else {},
        scratch_shapes=[pltpu.SemaphoreType.DMA((many,))],
        compiler_params=params(4),
        name="unpack",
    )(place, *pieces, *extra)


def exchanged(copies, axis):
    return lax.all_to_all(copies, axis, split_axis=0, concat_axis=0, tiled=True)


def shared(array, axis):
    return exchanged(jnp.broadcast_to(array, (lax.axis_size(axis), *array.shape)), axis)


def along(array, axis, step):
    peers = lax.axis_size(axis)
    return lax.ppermute(array, axis, [(i, (i + step) % peers) for i in range(peers)])


def to_owner(array, place):
    chips = OWNERS // 2
    pairs = [(i, 2 * ((i // 2 + place // 2) % chips) + (i % 2 ^ place % 2)) for i in range(OWNERS)]
    return lax.ppermute(array, MEMBER, pairs)


def to_strips_beside(array, step):
    peers = lax.axis_size(SPACE)
    pairs = [(i, i + step) for i in range(peers) if 0 <= i + step < peers]
    return lax.ppermute(array, SPACE, pairs)


def on_device(state, obs_index, obs_value, obs_scale, ksat, storage, recharge, newton_counts):
    members, rows, columns = state.shape
    flat = state.reshape(members * rows, columns)
    own = lax.axis_index(MEMBER)
    strip = lax.axis_index(SPACE)
    place = jnp.stack(
        [own, (strip > 0).astype(jnp.int32), (strip < lax.axis_size(SPACE) - 1).astype(jnp.int32)]
    ).astype(jnp.int32)

    seen = observed(flat, obs_index[None], lax.axis_size(MEMBER[0]))
    same = exchanged(seen, MEMBER[0])

    joint, given = packed_blocks(place, flat, seen)
    wide_counts = jnp.broadcast_to(newton_counts[:, None], (MEMBERS, LANES))
    same, joint, given, wide_counts = lax.optimization_barrier((same, joint, given, wide_counts))
    other = along(same, MEMBER[1], 1)
    taken = along(given, MEMBER[1], 1)
    joint = filled(taken, joint)

    pieces = [joint[0]] + [along(joint[n], MEMBER[0], -n) for n in range(1, OWNERS // 2)]
    copies = lax.axis_size(SPACE[0])
    part = gram_blocks(place, same, other, obs_value[None], obs_scale[None], copies)
    part = jnp.sum(exchanged(part, SPACE[0]), axis=0)
    part = jnp.sum(shared(part, SPACE[1]), axis=0)
    part, pieces = lax.optimization_barrier((part, pieces))
    parts = shared(part, MEMBER)
    cell_fields = (ksat, storage, recharge)
    down, up = borders(pieces, cell_fields)
    above = to_strips_beside(up, 1)
    below = to_strips_beside(down, -1)
    transform = transform_of(place, parts)
    fields, edge_fields, cells = analysed(place, cell_fields, transform, pieces, above, below)

    arrived = [None] * OWNERS
    for shifts in ((4,), (2, 6), (5, 3), (7, 1), (0,)):
        if shifts == (7, 1):
            cells, arrived[4] = lax.optimization_barrier((cells, arrived[4]))
        if shifts == (0,):
            cells, arrived[2], arrived[6] = lax.optimization_barrier((cells, arrived[2], arrived[6]))
        moved = forecasts(
            shifts, place, newton_counts, wide_counts, fields, edge_fields, [cells[i] for i in shifts]
        )
        moved, cells = lax.optimization_barrier((moved, cells))
        for i, field in zip(shifts, moved):
            arrived[i] = to_owner(field, i) if i else field
    early, late = (0, 4, 2, 6), (5, 3, 7, 1)
    result = unpacked(place, early, [arrived[i] for i in early])
    result = unpacked(place, late, [arrived[i] for i in late], result)
    return result.reshape(members, rows, columns)


def solution(mesh):
    x = 4
    finer = Mesh(
        mesh.devices.reshape(4, 2, -1, x), ("member_0", "member_1", "space_0", "space_1")
    )
    placed = (
        P(MEMBER, SPACE, None),
        P(SPACE),
        P(SPACE),
        P(SPACE),
        P(SPACE, None),
        P(SPACE, None),
        P(SPACE, None),
        P(),
    )
    return jax.shard_map(
        on_device, mesh=finer, in_specs=placed, out_specs=P(MEMBER, SPACE, None), check_vma=False
    )
```

```python
import functools

import jax
import jax.numpy as jnp
from jax import lax
from jax.experimental import pallas as pl
from jax.experimental.pallas import tpu as pltpu
from jax.sharding import Mesh
from jax.sharding import PartitionSpec as P

NS_ITERS = 12
DAMPING = 0.3
MEMBER = ("member_0", "member_1")
SPACE = ("space_0", "space_1")
HIGHEST = lax.Precision.HIGHEST
F32 = jnp.float32

OWNERS = 8
HELD = 32
ROWS = 16
LANES = 128
MEMBERS = OWNERS * HELD
EDGE = ROWS
SENT_ROWS = ROWS + 1
OUTER = 36
OWN = 72


def shape(*dims, dtype=F32):
    return jax.ShapeDtypeStruct(dims, dtype)


def whole(count):
    return [pl.BlockSpec(memory_space=pltpu.VMEM)] * count


def params(mib):
    return pltpu.CompilerParams(vmem_limit_bytes=mib * 2**20)


SCALARS = pl.BlockSpec(memory_space=pltpu.SMEM)


def relative(own, place, sign=1):
    chip, core = lax.div(own, 2), lax.rem(own, 2)
    chips = OWNERS // 2
    other = lax.rem(chip + sign * (place // 2) + chips, chips)
    return 2 * other + (1 - core if place % 2 else core)


def lane_ids(rows=8):
    return lax.broadcasted_iota(jnp.int32, (rows, LANES), 1)


def turned(array, amount):
    return pltpu.roll(array, amount % LANES, 1)


def dot(a, b, dims=((1,), (0,))):
    return lax.dot_general(a, b, (dims, ((), ())), precision=HIGHEST, preferred_element_type=F32)


def observe_kernel(index_ref, state_ref, seen_ref):
    values = state_ref[...]
    high = values.astype(jnp.bfloat16)
    rest = values - high.astype(F32)
    middle = rest.astype(jnp.bfloat16)
    low = (rest - middle.astype(F32)).astype(jnp.bfloat16)
    parts = jnp.concatenate([low, middle, high], axis=0)
    width = values.shape[1]
    step = 256
    for first in range(0, index_ref.shape[1], step):
        cell = index_ref[:, first : first + step]
        row = cell // width
        column = cell - row * width
        places = lax.broadcasted_iota(jnp.int32, (width, step), 0)
        chosen = (places == column).astype(F32).astype(jnp.bfloat16)
        terms = jnp.dot(parts, chosen, preferred_element_type=F32).reshape(3, HELD, ROWS, step)
        picked = (terms[0] + terms[1]) + terms[2]
        rows = lax.broadcasted_iota(jnp.int32, (ROWS, step), 0)
        seen = jnp.sum(jnp.where((rows == row)[None], picked, 0.0), axis=1)
        for copy in range(seen_ref.shape[0]):
            seen_ref[copy, :, first : first + step] = seen


def observed(state, obs_index, copies):
    return pl.pallas_call(
        observe_kernel,
        out_shape=shape(copies, HELD, obs_index.shape[1]),
        in_specs=whole(2),
        out_specs=whole(1)[0],
        compiler_params=params(20),
        name="observe",
    )(obs_index, state)


ORDER = (0, 1, EDGE, ROWS - 2, ROWS - 1) + tuple(range(2, ROWS - 2))
PLACE = {unit: at for at, unit in enumerate(ORDER)}


def pack_kernel(place_ref, state_ref, after_ref, *refs):
    own = place_ref[0]
    chips = OWNERS // 2
    joint_refs, given_ref, column_ref = refs[:chips], refs[chips], refs[chips + 1]

    def put(slot, row, members, value):
        if slot % 2:
            given_ref[slot // 2, row, members] = value
        else:
            joint_refs[slot // 2][0, row, members] = value

    lane = lane_ids()
    even = lane % 2 == 0
    near_left = (lane < OUTER) & even
    near_right = (lane < OUTER) & ~even
    far_left = (lane >= OUTER) & (lane < OUTER + 2 * ROWS) & even
    far_right = (lane >= OUTER + 3) & (lane < OUTER + 3 + 2 * ROWS) & ~even
    own_lanes = (lane >= OWN) & (lane < OWN + 2 * ROWS + 4)

    def one_group(group, carry):
        near, far = [], []
        members = pl.ds(pl.multiple_of(group * 8, 8), 8)
        lines = pl.ds(pl.multiple_of(group * 8 * ROWS, 8 * ROWS), 8 * ROWS)
        for slot in range(OWNERS):
            block = relative(own, slot, -1)
            packed_near = jnp.zeros((8, LANES), F32)
            packed_far = jnp.zeros((8, LANES), F32)
            start = pl.multiple_of(block * LANES, LANES)
            column_ref[slot] = state_ref[lines, pl.ds(start, LANES)]
            for r in range(ROWS):
                value = column_ref[slot, pl.ds(r, 8, stride=ROWS), :]
                put(slot, PLACE[r], members, value)
                at = 2 * (r + 1)
                packed_near = jnp.where(
                    (lane == at) | (lane == at + 1), turned(value, at + 1), packed_near
                )
                at = OUTER + 2 * r
                packed_far = jnp.where(
                    (lane == at) | (lane == at + 3), turned(value, at + 2), packed_far
                )
            near.append(packed_near)
            far.append(packed_far)
        for slot in range(OWNERS):
            block = relative(own, slot, -1)
            odd = lax.rem(block, 2) == 1
            beside, further = slot ^ 1, ((slot ^ 1) + 2) % OWNERS
            nearer = ((slot ^ 1) - 2) % OWNERS
            has_left = (block > 0).astype(F32)
            has_right = (block < OWNERS - 1).astype(F32)

            def left(packed):
                return jnp.where(odd, packed[beside], packed[further]) * has_left

            def right(packed):
                return jnp.where(odd, packed[nearer], packed[beside]) * has_right

            edge = jnp.where(own_lanes, turned(near[slot], OWN), 0.0)
            edge = jnp.where(near_left, left(near), edge)
            edge = jnp.where(far_left, left(far), edge)
            edge = jnp.where(near_right, right(near), edge)
            edge = jnp.where(far_right, right(far), edge)
            put(slot, PLACE[EDGE], members, edge)
        return carry

    lax.fori_loop(0, HELD // 8, one_group, 0)


def packed_blocks(place, state, after):
    chips = OWNERS // 2
    packed = pl.pallas_call(
        pack_kernel,
        out_shape=[shape(2, SENT_ROWS, HELD, LANES)] * chips
        + [shape(chips, SENT_ROWS, HELD, LANES)],
        in_specs=[SCALARS] + whole(1) + [pl.BlockSpec(memory_space=pl.ANY)],
        out_specs=whole(chips + 1),
        scratch_shapes=[pltpu.VMEM((OWNERS, 8 * ROWS, LANES), F32)],
        compiler_params=params(8),
        name="pack",
    )(place, state, after)
    return packed[:chips], packed[chips]


def fill_kernel(taken_ref, *refs):
    chips = OWNERS // 2
    joint_refs, sems = refs[chips : 2 * chips], refs[2 * chips]
    copies = [
        pltpu.make_async_copy(taken_ref.at[n], joint_refs[n].at[1], sems.at[n])
        for n in range(chips)
    ]
    for copy in copies:
        copy.start()
    for copy in copies:
        copy.wait()


def filled(taken, joint):
    chips = OWNERS // 2
    anywhere = [pl.BlockSpec(memory_space=pl.ANY)]
    return pl.pallas_call(
        fill_kernel,
        out_shape=[shape(2, SENT_ROWS, HELD, LANES)] * chips,
        in_specs=whole(1) + anywhere * chips,
        out_specs=anywhere * chips,
        input_output_aliases={1 + n: n for n in range(chips)},
        scratch_shapes=[pltpu.SemaphoreType.DMA((chips,))],
        compiler_params=params(4),
        name="fill",
    )(taken, *joint)


BORDER = OWNERS * 3 * HELD
FIELD_LINES = 3 * 2 * OWNERS


def border_kernel(*refs):
    chips = OWNERS // 2
    pieces, fields = refs[:chips], refs[chips : chips + 3]
    down_ref, up_ref = refs[chips + 3 :]
    size = 3 * HELD
    for i in range(OWNERS):
        piece = pieces[i // 2]
        down_ref[i * size : (i + 1) * size] = piece[i % 2, 0:3].reshape(size, LANES)
        up_ref[i * size : (i + 1) * size] = piece[i % 2, 2:5].reshape(size, LANES)
    for which, ref in enumerate(fields):
        for block in range(OWNERS):
            at = BORDER + (which * OWNERS + block) * 2
            lanes = slice(block * LANES, (block + 1) * LANES)
            down_ref[at : at + 2] = ref[0:2, lanes]
            up_ref[at : at + 2] = ref[ROWS - 2 : ROWS, lanes]


def borders(pieces, fields):
    size = BORDER + FIELD_LINES
    return pl.pallas_call(
        border_kernel,
        grid=(1,),
        out_shape=[shape(size, LANES)] * 2,
        in_specs=[pl.BlockSpec((2, 5, HELD, LANES), lambda g: (0, 0, 0, 0))] * (OWNERS // 2)
        + [pl.BlockSpec((ROWS, OWNERS * LANES), lambda g: (0, 0))] * 3,
        out_specs=[pl.BlockSpec((size, LANES), lambda g: (0, 0))] * 2,
        compiler_params=params(6),
        name="borders",
    )(*pieces, *fields)


def gram_kernel(place_ref, same_ref, other_ref, value_ref, scale_ref, out_ref):
    own = place_ref[0]
    total = jnp.sum(same_ref[...], axis=(0, 1)) + jnp.sum(other_ref[...], axis=(0, 1))
    mean = (total / MEMBERS)[None]
    scale = scale_ref[...]
    weight = scale / jnp.sqrt(F32(MEMBERS - 1))
    blocks = []
    for k in range(5):
        at = lax.rem(own + k, OWNERS) // 2
        block = same_ref[at] if k % 2 == 0 else other_ref[at]
        blocks.append((block - mean) * weight)
    innovation = scale * (value_ref[...] - mean)
    left = jnp.concatenate([blocks[0], jnp.broadcast_to(innovation, (8, mean.shape[1]))], axis=0)
    main = dot(left, jnp.concatenate(blocks[:4], axis=0), ((1,), (1,)))
    last = jnp.concatenate([blocks[4], jnp.zeros((96, mean.shape[1]), F32)], axis=0)
    opposite = dot(blocks[0], last, ((1,), (1,)))
    packed = opposite[0:8]
    for g in range(1, 4):
        packed += turned(opposite[8 * g : 8 * g + 8], HELD * g)
    for copy in range(out_ref.shape[0]):
        out_ref[copy, 0:40] = main
        out_ref[copy, 40:48] = packed


def gram_blocks(place, same, other, value, scale, copies):
    return pl.pallas_call(
        gram_kernel,
        out_shape=shape(copies, 48, LANES),
        in_specs=[SCALARS] + whole(4),
        out_specs=whole(1)[0],
        compiler_params=params(8),
        cost_estimate=pl.CostEstimate(flops=10**10, bytes_accessed=10**6, transcendentals=0),
        name="gram",
    )(place, same, other, value, scale)


def thirds(array):
    high = array.astype(jnp.bfloat16)
    rest = array - high.astype(F32)
    middle = rest.astype(jnp.bfloat16)
    return high, middle, (rest - middle.astype(F32)).astype(jnp.bfloat16)


def six_products(a, b):
    def product(i, j):
        return jnp.dot(a[i], b[j], preferred_element_type=F32)

    small = product(0, 2) + product(2, 0) + product(1, 1)
    return (small + (product(0, 1) + product(1, 0))) + product(0, 0)


def three_products(a, b):
    def product(i, j):
        return jnp.dot(a[i], b[j], preferred_element_type=F32)

    return (product(0, 1) + product(1, 0)) + product(0, 0)


def root_kernel(place_ref, parts_ref, out_ref, half_ref):
    own = place_ref[0]
    lane = lane_ids()
    drive_row = jnp.zeros((8, MEMBERS), F32)
    nothing = jnp.zeros((8, LANES), F32)
    for i in range(OWNERS):
        for g in range(4):
            rows = parts_ref[i, 8 * g : 8 * g + 8]
            rows = jnp.where(lane < HELD, 0.5 * rows, rows)
            fifth = turned(parts_ref[i, 40:48], -HELD * g)
            fifth = jnp.where(lane < HELD, 0.5 * fifth, 0.0)
            line = jnp.concatenate([rows, fifth], axis=1)
            half_ref[i * HELD + 8 * g : i * HELD + 8 * g + 8] = pltpu.roll(line, HELD * i, 1)
        drive = jnp.where(lane < HELD, parts_ref[relative(own, i), 32:40], 0.0)
        line = jnp.concatenate([drive, nothing], axis=1)
        drive_row += pltpu.roll(line, HELD * i, 1)
    half = half_ref[...]
    rows = lax.broadcasted_iota(jnp.int32, (MEMBERS, MEMBERS), 0)
    columns = lax.broadcasted_iota(jnp.int32, (MEMBERS, MEMBERS), 1)
    identity = (rows == columns).astype(F32)
    big = identity + (half + half.T)
    norm = jnp.sqrt(jnp.sum(big * big))
    upper = big / norm
    middle = 1.5 * identity - 0.5 * upper
    middle_parts = thirds(middle)
    upper = six_products(thirds(upper), middle_parts)
    lower = middle
    lower_parts = middle_parts
    for _ in range(NS_ITERS - 2):
        upper_parts = thirds(upper)
        middle_parts = thirds(1.5 * identity - 0.5 * three_products(lower_parts, upper_parts))
        upper = six_products(upper_parts, middle_parts)
        lower = six_products(middle_parts, lower_parts)
        lower_parts = thirds(lower)
    middle = 1.5 * identity - 0.5 * three_products(lower_parts, thirds(upper))
    root = six_products(thirds(middle), lower_parts) / jnp.sqrt(norm)

    def rows_in_order(matrix):
        half_ref[...] = matrix
        starts = [pl.multiple_of(relative(own, i) * HELD, HELD) for i in range(OWNERS)]
        return jnp.concatenate([half_ref[pl.ds(start, HELD)] for start in starts], axis=0)

    root = rows_in_order(rows_in_order(root).T)
    weights = dot(dot(drive_row, root, ((1,), (1,))), root, ((1,), (1,)))
    out_ref[...] = root + weights[0:1] / jnp.sqrt(F32(MEMBERS - 1))


def transform_of(place, parts):
    return pl.pallas_call(
        root_kernel,
        out_shape=shape(MEMBERS, MEMBERS),
        in_specs=[SCALARS] + whole(1),
        out_specs=whole(1)[0],
        scratch_shapes=[pltpu.VMEM((MEMBERS, MEMBERS), F32)],
        compiler_params=params(12),
        cost_estimate=pl.CostEstimate(flops=10**10, bytes_accessed=10**6, transcendentals=0),
        name="root",
    )(place, parts)


FIELD_ROWS = 20
NEAR_K, INNER_K, OUTER_K, NEAR_S, NEAR_R, NEAR_MASK = range(6)


def spread_fields(place_ref, ksat_ref, storage_ref, recharge_ref, above_ref, below_ref, out_ref, edge_ref):
    own = place_ref[0]
    lane = lane_ids(1)
    even = lane % 2 == 0
    left_block = jnp.maximum(own - 1, 0)
    right_block = jnp.minimum(own + 1, OWNERS - 1)
    has_left = own > 0
    has_right = own < OWNERS - 1
    packed = [jnp.zeros((1, LANES), F32) for _ in range(5)]
    for which, ref in enumerate((ksat_ref, storage_ref, recharge_ref)):
        for place in range(FIELD_ROWS):
            r = place - 2

            def row_of(block):
                line = BORDER + (which * OWNERS + block) * 2
                if r < 0:
                    return above_ref[pl.ds(line + r + 2, 1)]
                if r >= ROWS:
                    return below_ref[pl.ds(line + r - ROWS, 1)]
                return ref[r : r + 1, pl.ds(pl.multiple_of(block * LANES, LANES), LANES)]

            mine = row_of(own)
            out_ref[which, place] = jnp.broadcast_to(mine, (8, LANES))
            if r < -1 or r > ROWS:
                if which == 0:
                    out_ref[3, place] = jnp.zeros((8, LANES), F32)
                    out_ref[4, place] = jnp.zeros((8, LANES), F32)
                continue
            at = 2 * (r + 1)
            here = (lane == at) | (lane == at + 1)
            left = jnp.where(has_left, row_of(left_block), 0.0)
            right = jnp.where(has_right, row_of(right_block), 0.0)
            near = jnp.where(lane < LANES // 2, right, left)
            near = turned(near, at + 1)
            if which == 0:
                out_ref[3, place] = jnp.broadcast_to(turned(mine, 1), (8, LANES))
                beyond = jnp.where(lane == 0, turned(left, 1), turned(right, -1))
                out_ref[4, place] = jnp.broadcast_to(beyond, (8, LANES))
                inner = jnp.where(even, turned(mine, at), turned(mine, at + 2))
                outer = jnp.where(even, turned(left, at + 2), turned(right, at))
                packed[NEAR_K] = jnp.where(here, near, packed[NEAR_K])
                packed[INNER_K] = jnp.where(here, inner, packed[INNER_K])
                packed[OUTER_K] = jnp.where(here, outer, packed[OUTER_K])
            elif which == 1:
                packed[NEAR_S] = jnp.where(here, near, packed[NEAR_S])
            else:
                packed[NEAR_R] = jnp.where(here, near, packed[NEAR_R])
    for n in range(5):
        edge_ref[n] = jnp.broadcast_to(packed[n], (8, LANES))
    lane = lane_ids()
    keep = jnp.where(lane % 2 == 0, has_left.astype(F32), has_right.astype(F32))
    edge_ref[NEAR_MASK] = jnp.where((lane >= 2) & (lane < 2 * ROWS + 2), keep, 0.0)


UNITS = ROWS + 5


def halves(array):
    high = array.astype(jnp.bfloat16)
    return high, (array - high.astype(F32)).astype(jnp.bfloat16)


def analyse_kernel(*refs):
    place_ref, ksat_ref, storage_ref, recharge_ref, transform_ref = refs[:5]
    chips = OWNERS // 2
    piece_refs = refs[5 : 5 + chips]
    above_ref, below_ref, field_ref, edge_field_ref = refs[5 + chips : 9 + chips]
    out_refs = refs[9 + chips :]
    spread_fields(
        place_ref, ksat_ref, storage_ref, recharge_ref, above_ref, below_ref, field_ref, edge_field_ref
    )
    high, low = halves(transform_ref[...])
    lane = lax.broadcasted_iota(jnp.int32, (MEMBERS, LANES), 1)

    def joined(find):
        return jnp.concatenate([find(i) for i in range(OWNERS)], axis=0)

    def border(ref, n):
        return joined(lambda i: ref[(i * 3 + n) * HELD : (i * 3 + n + 1) * HELD])

    def cells(unit):
        if unit > SENT_ROWS + 1:
            return border(below_ref, unit - SENT_ROWS - 2)
        if unit >= SENT_ROWS:
            return border(above_ref, unit - SENT_ROWS + 1)
        found = joined(lambda i: piece_refs[i // 2][i % 2, PLACE[unit]])
        if unit == EDGE:
            top = border(above_ref, 0)
            bottom = border(below_ref, 2)
            first = (lane < 2) | ((lane >= OWN) & (lane < OWN + 2))
            last = 2 * ROWS + 2
            final = ((lane >= last) & (lane < last + 2)) | (
                (lane >= OWN + last) & (lane < OWN + last + 2)
            )
            found = jnp.where(first, turned(top, -2 * ROWS), found)
            found = jnp.where(final, turned(bottom, 2 * ROWS), found)
        return found

    def product(a, b):
        return jnp.dot(a, b, preferred_element_type=F32)

    for first in range(0, UNITS, 2):
        units = range(first, min(first + 2, UNITS))
        found = [cells(u) for u in units]
        state = found[0] if len(found) == 1 else jnp.concatenate(found, axis=1)
        mean = jnp.sum(state, axis=0, keepdims=True) / MEMBERS
        large, small = halves(state - mean)
        result = product(low, large) + product(high, small) + product(high, large) + mean
        for at, unit in enumerate(units):
            for i in range(OWNERS):
                out_refs[i][unit] = result[
                    i * HELD : (i + 1) * HELD, at * LANES : (at + 1) * LANES
                ]


def analysed(place, cell_fields, transform, pieces, above, below):
    found = pl.pallas_call(
        analyse_kernel,
        out_shape=[shape(5, FIELD_ROWS, 8, LANES), shape(6, 8, LANES)]
        + [shape(UNITS, HELD, LANES)] * OWNERS,
        in_specs=[SCALARS] + whole(6 + OWNERS // 2),
        out_specs=whole(2 + OWNERS),
        compiler_params=params(14),
        name="analyse",
    )(place, *cell_fields, transform, *pieces, above, below)
    return found[0], found[1], found[2:]


def logistic(x):
    return 0.5 * jnp.tanh(0.5 * x) + 0.5


BATCH = 16


def forecast_kernel(shifts, place_ref, counts_ref, wide_ref, field_ref, edge_field_ref, *refs):
    cells_refs, out_refs = refs[: len(shifts)], refs[len(shifts) : 2 * len(shifts)]
    iterate, goal, edge_row = refs[2 * len(shifts) :]
    own = place_ref[0]
    has_above = place_ref[1].astype(F32)
    has_below = place_ref[2].astype(F32)
    lane = lane_ids()
    even = lane % 2 == 0
    first_lane = lane == 0
    ends = first_lane | (lane == LANES - 1)
    sat, store, rain, left, ghosts = range(5)
    tiles = BATCH // 8

    def rolled(array, amount):
        return pltpu.roll(array, amount % LANES, 2)

    def face(level, other, cond, other_cond):
        return 0.5 * (cond + other_cond) * (other - level)

    def swapped(packed):
        return jnp.where(even, rolled(packed, -1), rolled(packed, 1))

    def one_batch(which, batch, carry):
        cells_ref, out_ref = cells_refs[which], out_refs[which]
        owner = relative(own, shifts[which])
        first_member = owner * HELD + batch * BATCH
        most = counts_ref[first_member]
        for n in range(1, BATCH):
            most = jnp.maximum(most, counts_ref[first_member + n])
        counts = wide_ref[pl.ds(pl.multiple_of(first_member, BATCH), BATCH)]
        counts = counts.reshape(tiles, 8, LANES)
        members = pl.ds(pl.multiple_of(batch * BATCH, BATCH), BATCH)

        def begun(level, flux, storage):
            bend = jnp.tanh(level)
            held = storage * bend
            derivative = (1.0 + storage) - held * bend
            return level + DAMPING * flux / derivative, level + held + flux

        def swept(value, target, storage, sweep):
            bend = jnp.tanh(value)
            held = storage * bend
            derivative = (1.0 + storage) - held * bend
            moved = value - DAMPING * (value + held - target) / derivative
            return jnp.where(counts > sweep, moved, value)

        def unit_at(unit):
            return cells_ref[unit, members].reshape(tiles, 8, LANES)

        def cell_at(r):
            if r < 0:
                return unit_at(SENT_ROWS + r + 2)
            if r >= ROWS:
                return unit_at(SENT_ROWS + 2 + r - ROWS)
            return unit_at(r)

        packed = unit_at(EDGE)
        near = jnp.where(lane < OUTER, packed, 0.0)
        inner = jnp.where(even, rolled(packed, -OWN - 1), rolled(packed, -OWN + 1))
        outer = jnp.where(even, rolled(packed, 2 - OUTER), rolled(packed, -OUTER))
        near_k = edge_field_ref[NEAR_K] * logistic(near)
        inner_k = edge_field_ref[INNER_K] * logistic(inner)
        outer_k = edge_field_ref[OUTER_K] * logistic(outer)
        inward = face(near, inner, near_k, inner_k)
        side = swapped(inward)
        flux = inward + face(near, outer, near_k, outer_k)
        flux += face(near, rolled(near, 2), near_k, rolled(near_k, 2))
        flux += face(near, rolled(near, -2), near_k, rolled(near_k, -2))
        flux += edge_field_ref[NEAR_R]
        value, target = begun(near, flux, edge_field_ref[NEAR_S])
        edge_row[0] = value
        edge_row[1] = target

        def conduct(level, r):
            return field_ref[sat, r + 2] * logistic(level)

        level, cond = cell_at(-1), conduct(cell_at(-1), -1)
        above = face(cell_at(-2), level, conduct(cell_at(-2), -2), cond)
        for r in range(-1, ROWS + 1):
            lower_level = cell_at(r + 1)
            lower_cond = conduct(lower_level, r + 1)
            under = face(level, lower_level, cond, lower_cond)
            beside = rolled(level, 1)
            across = face(beside, level, field_ref[left, r + 2] * logistic(beside), cond)
            across = jnp.where(first_lane, 0.0, across)
            flux = under - above + (rolled(across, -1) - across)
            flux -= jnp.where(ends, rolled(side, -2 * (r + 1) - 1), 0.0)
            flux += field_ref[rain, r + 2]
            iterate[r + 1], goal[r + 1] = begun(level, flux, field_ref[store, r + 2])
            level, cond, above = lower_level, lower_cond, under

        def first_sweep(sweep, carry):
            for n in range(ROWS + 2):
                iterate[n] = swept(iterate[n], goal[n], field_ref[store, n + 1], sweep)
            edge_row[0] = swept(edge_row[0], edge_row[1], edge_field_ref[NEAR_S], sweep)
            return carry

        lax.fori_loop(1, most, first_sweep, 0)

        near = edge_row[0] * edge_field_ref[NEAR_MASK]
        side = swapped(near)
        level = iterate[1]
        cond = conduct(level, 0)
        before = iterate[0] * has_above
        above = face(before, level, conduct(before, -1), cond)
        for r in range(ROWS):
            lower_level = iterate[r + 2]
            if r == ROWS - 1:
                lower_level = lower_level * has_below
            lower_cond = conduct(lower_level, r + 1)
            under = face(level, lower_level, cond, lower_cond)
            beside = rolled(level, 1)
            across = face(beside, level, field_ref[left, r + 2] * logistic(beside), cond)
            across = jnp.where(first_lane, 0.0, across)
            flux = under - above + (rolled(across, -1) - across)
            ghost = rolled(side, -2 * (r + 1) - 1)
            entering = face(level, ghost, cond, field_ref[ghosts, r + 2] * logistic(ghost))
            flux += jnp.where(ends, entering, 0.0)
            flux += field_ref[rain, r + 2]
            iterate[r + 1], goal[r + 1] = begun(level, flux, field_ref[store, r + 2])
            level, cond, above = lower_level, lower_cond, under

        def second_sweep(sweep, carry):
            for n in range(1, ROWS + 1):
                iterate[n] = swept(iterate[n], goal[n], field_ref[store, n + 1], sweep)
            return carry

        lax.fori_loop(1, most, second_sweep, 0)
        for r in range(ROWS):
            for tile in range(tiles):
                start = (batch * BATCH + tile * 8) * ROWS + r
                out_ref[pl.ds(start, 8, stride=ROWS), :] = iterate[r + 1, tile]
        return carry

    for which in range(len(shifts)):
        lax.fori_loop(0, HELD // BATCH, functools.partial(one_batch, which), 0)


def forecasts(shifts, place, counts, wide_counts, fields, edge_fields, cells):
    many = len(shifts)
    return pl.pallas_call(
        functools.partial(forecast_kernel, shifts),
        out_shape=[shape(HELD * ROWS, LANES)] * many,
        in_specs=[SCALARS, SCALARS] + whole(3 + many),
        out_specs=whole(many),
        scratch_shapes=[
            pltpu.VMEM((ROWS + 2, BATCH // 8, 8, LANES), F32),
            pltpu.VMEM((ROWS + 2, BATCH // 8, 8, LANES), F32),
            pltpu.VMEM((2, BATCH // 8, 8, LANES), F32),
        ],
        compiler_params=params(6),
        cost_estimate=pl.CostEstimate(flops=1, bytes_accessed=1, transcendentals=0),
        name="forecast",
    )(place, counts, wide_counts, fields, edge_fields, *cells)


def unpack_kernel(shifts, place_ref, *refs):
    out_ref, sems = refs[-2], refs[-1]
    copies = []
    for n, shift in enumerate(shifts):
        block = relative(place_ref[0], shift, -1)
        lanes = pl.ds(pl.multiple_of(block * LANES, LANES), LANES)
        copies.append(pltpu.make_async_copy(refs[n], out_ref.at[:, lanes], sems.at[n]))
    for copy in copies:
        copy.start()
    for copy in copies:
        copy.wait()


def unpacked(place, shifts, pieces, begun=None):
    many = len(shifts)
    anywhere = pl.BlockSpec(memory_space=pl.ANY)
    extra = [] if begun is None else [begun]
    return pl.pallas_call(
        functools.partial(unpack_kernel, shifts),
        out_shape=shape(HELD * ROWS, OWNERS * LANES),
        in_specs=[SCALARS] + whole(many) + [anywhere] * len(extra),
        out_specs=anywhere,
        input_output_aliases={1 + many: 0} if extra else {},
        scratch_shapes=[pltpu.SemaphoreType.DMA((many,))],
        compiler_params=params(4),
        name="unpack",
    )(place, *pieces, *extra)


def exchanged(copies, axis):
    return lax.all_to_all(copies, axis, split_axis=0, concat_axis=0, tiled=True)


def total_kernel(parts_ref, out_ref):
    total = jnp.sum(parts_ref[...], axis=0)
    for copy in range(out_ref.shape[0]):
        out_ref[copy] = total


def totals(parts, copies):
    return pl.pallas_call(
        total_kernel,
        out_shape=shape(copies, *parts.shape[1:]),
        in_specs=whole(1),
        out_specs=whole(1)[0],
        compiler_params=params(4),
        name="total",
    )(parts)


def along(array, axis, step):
    peers = lax.axis_size(axis)
    return lax.ppermute(array, axis, [(i, (i + step) % peers) for i in range(peers)])


def to_owner(array, place):
    chips = OWNERS // 2
    pairs = [(i, 2 * ((i // 2 + place // 2) % chips) + (i % 2 ^ place % 2)) for i in range(OWNERS)]
    return lax.ppermute(array, MEMBER, pairs)


def to_strips_beside(array, step):
    peers = lax.axis_size(SPACE)
    pairs = [(i, i + step) for i in range(peers) if 0 <= i + step < peers]
    return lax.ppermute(array, SPACE, pairs)


def on_device(state, obs_index, obs_value, obs_scale, ksat, storage, recharge, newton_counts):
    members, rows, columns = state.shape
    flat = state.reshape(members * rows, columns)
    own = lax.axis_index(MEMBER)
    strip = lax.axis_index(SPACE)
    place = jnp.stack(
        [own, (strip > 0).astype(jnp.int32), (strip < lax.axis_size(SPACE) - 1).astype(jnp.int32)]
    ).astype(jnp.int32)

    seen = observed(flat, obs_index[None], lax.axis_size(MEMBER[0]))
    same = exchanged(seen, MEMBER[0])

    joint, given = packed_blocks(place, flat, seen)
    wide_counts = jnp.broadcast_to(newton_counts[:, None], (MEMBERS, LANES))
    same, joint, given, wide_counts = lax.optimization_barrier((same, joint, given, wide_counts))
    other = along(same, MEMBER[1], 1)
    taken = along(given, MEMBER[1], 1)
    joint = filled(taken, joint)

    pieces = [joint[0]] + [along(joint[n], MEMBER[0], -n) for n in range(1, OWNERS // 2)]
    copies = lax.axis_size(SPACE[0])
    part = gram_blocks(place, same, other, obs_value[None], obs_scale[None], copies)
    part = exchanged(totals(exchanged(part, SPACE[0]), lax.axis_size(SPACE[1])), SPACE[1])
    part = totals(part, OWNERS)
    part, pieces = lax.optimization_barrier((part, pieces))
    parts = exchanged(part, MEMBER)
    cell_fields = (ksat, storage, recharge)
    down, up = borders(pieces, cell_fields)
    above = to_strips_beside(up, 1)
    below = to_strips_beside(down, -1)
    transform = transform_of(place, parts)
    fields, edge_fields, cells = analysed(place, cell_fields, transform, pieces, above, below)

    arrived = [None] * OWNERS
    for shifts in ((4,), (2, 6), (5, 3), (7, 1), (0,)):
        if shifts == (7, 1):
            cells, arrived[4] = lax.optimization_barrier((cells, arrived[4]))
        if shifts == (0,):
            cells, arrived[2], arrived[6] = lax.optimization_barrier((cells, arrived[2], arrived[6]))
        moved = forecasts(
            shifts, place, newton_counts, wide_counts, fields, edge_fields, [cells[i] for i in shifts]
        )
        moved, cells = lax.optimization_barrier((moved, cells))
        for i, field in zip(shifts, moved):
            arrived[i] = to_owner(field, i) if i else field
    early, late = (0, 4, 2, 6), (5, 3, 7, 1)
    result = unpacked(place, early, [arrived[i] for i in early])
    result = unpacked(place, late, [arrived[i] for i in late], result)
    return result.reshape(members, rows, columns)


def solution(mesh):
    x = 4
    finer = Mesh(
        mesh.devices.reshape(4, 2, -1, x), ("member_0", "member_1", "space_0", "space_1")
    )
    placed = (
        P(MEMBER, SPACE, None),
        P(SPACE),
        P(SPACE),
        P(SPACE),
        P(SPACE, None),
        P(SPACE, None),
        P(SPACE, None),
        P(),
    )
    return jax.shard_map(
        on_device, mesh=finer, in_specs=placed, out_specs=P(MEMBER, SPACE, None), check_vma=False
    )
```
